32 devices in a mesh: groups: 2 (over x), gx: 16 (over z, y, core).
Axes of the slice: x: 2, y: 2, z: 4, core: 2. Of those that a mesh axis runs over, the one named last changes fastest.
Arguments:
- coupling: bfloat16 [8, 60, 60, 32, 128], P('groups', None, None, 'gx'), parts along dimension 0, may hold values from -0.1875 to 0.1875
- inverse: bfloat16 [120, 60, 32, 128], P('groups', None, 'gx'), parts along dimension 0, may hold values from -1 to 2, as said below
- source: float32 [120, 32, 128], P('groups', 'gx'), parts along dimension 0, may hold values from -6 to 6
- color_order: int32 [8], P('groups'), parts along dimension 0, may hold values from 0 to 3, each once
Outputs:
- adjoint: float32 [120, 32, 128], P('groups', 'gx'), parts along dimension 0
- off_term: float32 [120, 32, 128], P('groups', 'gx'), parts along dimension 0
The draws below stay inside these ranges and needn't reach their ends.
There are 2 independent parts, one for each index of `groups`. The reference program is written for one: setup_inputs(seed, part) draws one part's arguments, and reference() takes and returns one part's arrays. A program takes and returns all parts, laid end to end along the dimension named above; each array names one. Nothing has to cross between parts.
Inputs may be any that keep to these rules, and one draw needn't show every extreme that they name: `color_order`: each color 0 to 3 appears once. `inverse`: a diagonal part between 0.5 and 1.5 plus small noise on every entry.
All inputs are finite; a program needn't handle non-finite values.
Results may differ from the reference program's by a relative error of at most 0.012.
Values sent between devices are 32-bit elements; how exact they have to be, the bound alone decides.
No kernel may reach another device: no remote copies, remote signals or barrier semaphores. Data moves between devices by JAX's collectives and lax.ppermute only.
A program may use at most 192 MiB of HBM per device.

```python
import jax
import jax.numpy as jnp
from jax import lax

BLK = 60
TX = 2
TY = 8
SWEEPS = 2
NY = 128
NX = 32


def draw_inverse(key, part):
    key = jax.random.fold_in(key, 11)
    first, second = jax.random.split(key)
    diag = jnp.exp(jax.random.uniform(first, (BLK, 1, NX, NY), jnp.float32, jnp.log(0.5), jnp.log(1.5)))
    eye = jnp.eye(BLK, dtype=jnp.float32)[:, :, None, None]
    noise = jax.random.normal(second, (BLK, BLK, NX, NY), jnp.float32) * (0.3 / BLK ** 0.5)
    noise = jnp.clip(noise, -0.45, 0.45)
    return (eye * diag + noise).astype(jnp.bfloat16)


def block_levels(rng, extent, cuts, smallest, high):
    gain = 1.0
    for dim, blocks in cuts:
        steps = jax.random.uniform(jax.random.fold_in(jax.random.fold_in(rng, 6), dim), (blocks,), jnp.float32, smallest / len(cuts), high / len(cuts))
        gain = gain * jnp.repeat(jnp.exp(steps), extent[dim] // blocks).reshape((-1,) + (1,) * (len(extent) - 1 - dim))
    return gain


def bell_draw(stream_key, shape, deviation, bound, cuts=(), held_as=jnp.bfloat16):
    drawn = jax.random.normal(stream_key, shape, jnp.float32) * deviation
    if len(cuts) > 0:
        drawn = block_levels(stream_key, shape, cuts, -0.22, 0.18) * drawn
    return jnp.clip(drawn, min=-bound, max=bound).astype(held_as)


def setup_inputs(seed: int = 0, part: int = 0) -> dict:
    splits = jax.random.split(jax.random.key(seed), 5)
    part_splits = jax.random.split(jax.random.fold_in(splits[4], part), 5)
    return {
        "coupling": bell_draw(part_splits[0], (4, BLK, BLK, NX, NY), (16 * BLK) ** -0.5, 0.1875, ((3, 16),)),
        "inverse": draw_inverse(jax.random.fold_in(jax.random.fold_in(splits[4], part), 71), part),
        "source": bell_draw(part_splits[2], (BLK, NX, NY), 1.0, 6.0, ((1, 16),), jnp.float32),
        "color_order": jax.random.permutation(part_splits[3], 4).astype(jnp.int32),
    }


def face_parts(coupling, adjoint):
    rounded = adjoint.astype(jnp.bfloat16).astype(jnp.float32)
    result = []
    for face in range(4):
        block = coupling[face].astype(jnp.float32)
        result.append(jnp.einsum('ijxy,ixy->jxy', block, rounded, precision=lax.Precision.HIGHEST))
    return result


def gather_incoming(parts):
    total = jnp.pad(parts[0][:, 1:, :], ((0, 0), (0, 1), (0, 0)))
    total = total + jnp.pad(parts[1][:, :-1, :], ((0, 0), (1, 0), (0, 0)))
    total = total + jnp.pad(parts[2][:, :, 1:], ((0, 0), (0, 0), (0, 1)))
    total = total + jnp.pad(parts[3][:, :, :-1], ((0, 0), (0, 0), (1, 0)))
    return total


def reference(coupling, inverse, source, color_order):
    xpar = (jnp.arange(NX) // TX) % 2
    ypar = (jnp.arange(NY) // TY) % 2
    colors = (2 * xpar[:, None] + ypar[None, :]).astype(jnp.int32)
    inverse_wide = inverse.astype(jnp.float32)
    adjoint = jnp.zeros((BLK, NX, NY), jnp.float32)
    for sweep_index in range(SWEEPS):
        for position in range(4):
            slot = position if sweep_index % 2 == 0 else 3 - position
            target = color_order[slot]
            incoming = gather_incoming(face_parts(coupling, adjoint))
            rhs = (source - incoming).astype(jnp.bfloat16).astype(jnp.float32)
            update = jnp.einsum('ijxy,jxy->ixy', inverse_wide, rhs, precision=lax.Precision.HIGHEST)
            adjoint = jnp.where((colors == target)[None, :, :], update, adjoint)
    off_term = gather_incoming(face_parts(coupling, adjoint))
    return adjoint, off_term
```

```python
import functools

import jax
import jax.numpy as jnp
from jax import lax
from jax.experimental import pallas as pl
from jax.experimental.pallas import tpu as pltpu
from jax.sharding import PartitionSpec as P

BLK = 60
HALF = BLK // 2
ROWS = 2 * BLK
PAIR = 2 * ROWS
PAIRS = HALF // 2
TILE = 8
LANES = 128
MROWS = 64
SUMS = 768
F32, BF16 = jnp.float32, jnp.bfloat16
VMEM, SMEM = pltpu.VMEM, pltpu.SMEM


def lane(shape):
    return lax.broadcasted_iota(jnp.int32, shape, len(shape) - 1)


def row_parity(shape):
    return lax.broadcasted_iota(jnp.int32, shape, len(shape) - 2) & 1


def own_lanes(shape, q):
    return ((lane(shape) >> 3) & 1) == q


def shift(x, by):
    return pltpu.roll(x, by % LANES, len(x.shape) - 1)


def compact(ref, m0, m1):
    def step(k, _):
        rows = pl.ds(pl.multiple_of(k * PAIR, PAIR), PAIR)
        even = ((lane((PAIR, LANES)) >> 3) & 1) == 0
        first, second = ref[m0, rows, :], ref[m1, rows, :]
        moved = shift(jnp.where(even, second, first), TILE)
        ref[m0, rows, :] = jnp.where(even, first, moved)
        ref[m1, rows, :] = jnp.where(even, moved, second)
        return 0

    lax.fori_loop(0, PAIRS, step, 0)


def write_selector(sel):
    shape = (MROWS, SUMS)
    col = lax.broadcasted_iota(jnp.int32, shape, 1)
    row = lax.broadcasted_iota(jnp.int32, shape, 0)
    pair = (col * 1366) >> 16
    inner = col - pair * 48
    odd = jnp.where(inner < 16, 0, jnp.where(inner < 32, (inner >> 3) & 1, 1))
    target = 4 * pair + 2 * odd + (inner & 1)
    sel[...] = jnp.where((row == target) & (col < 48 * PAIRS), 1.0, 0.0).astype(BF16)


def local_incoming(p):
    shape = (ROWS // 8, 8, LANES)
    even = row_parity(shape) == 0
    from_right = pltpu.roll(p[0].reshape(shape), 7, 1)
    from_left = pltpu.roll(p[1].reshape(shape), 1, 1)
    inner = jnp.where(even, from_right, from_left).reshape(ROWS, LANES)
    y = lane((ROWS, LANES))
    above = jnp.where(y == LANES - 1, 0.0, shift(p[2], -1))
    below = jnp.where(y == 0, 0.0, shift(p[3], 1))
    return inner + above + below


def face_terms(q, faces, w, p, e):
    def face(f, _):
        def group(g, acc):
            total = None
            for r in range(3):
                k = 3 * g + r
                rows = pl.ds(pl.multiple_of(k * PAIR, PAIR), PAIR)
                block = w[2 * f + q, rows, :].reshape(15, 16, LANES)
                tiles = e[k]
                low = block[:7] * tiles[0][None]
                mid = block[7:8] * tiles[1][None]
                high = block[8:] * tiles[2][None]
                prod = jnp.concatenate([low, mid, high], axis=0)
                total = prod if total is None else total + prod
            return acc + total.reshape(PAIR, LANES).astype(F32)

        acc = lax.fori_loop(0, PAIRS // 3, group, jnp.zeros((PAIR, LANES), F32))
        half = acc[:ROWS] + acc[ROWS:]
        part = half + shift(half, -TILE)
        p[f] = jnp.where(own_lanes((ROWS, LANES), q), part, p[f])
        return 0

    lax.fori_loop(faces[0], faces[1], face, 0)


def write_tiles(q, u, e):
    even = row_parity((8, LANES)) == 0
    for k in range(PAIRS):
        first, second = [
            jnp.where(
                even,
                jnp.broadcast_to(u[q, pl.ds(r, 1), :], (8, LANES)),
                jnp.broadcast_to(u[q, pl.ds(r + 1, 1), :], (8, LANES)),
            )
            for r in (4 * k, 4 * k + 2)
        ]
        e[k, 0] = jnp.concatenate([first, first], axis=0).astype(BF16)
        e[k, 1] = jnp.concatenate([first, second], axis=0).astype(BF16)
        e[k, 2] = jnp.concatenate([second, second], axis=0).astype(BF16)


def update(q, incoming, source, winv, sel, u, e, rhs, sums):
    value = (source[...] - incoming).astype(BF16).astype(F32)
    value = jnp.where(own_lanes((ROWS, LANES), q), value, shift(value, TILE))
    rhs[...] = jnp.concatenate([value, value], axis=0).astype(BF16)

    def step(k, _):
        rows = pl.ds(pl.multiple_of(k * PAIR, PAIR), PAIR)
        prod = (winv[q, rows, :] * rhs[...]).reshape(15, 16, LANES)
        low = (prod[0] + prod[1]) + (prod[2] + prod[3]) + ((prod[4] + prod[5]) + prod[6])
        high = (prod[8] + prod[9]) + (prod[10] + prod[11]) + ((prod[12] + prod[13]) + prod[14])
        base = pl.multiple_of(k * 48, 16)
        sums[pl.ds(base, 48), :] = jnp.concatenate([low, prod[7], high], axis=0)
        return 0

    lax.fori_loop(0, PAIRS, step, 0)
    u[q] = jnp.dot(sel[...], sums[...], preferred_element_type=F32)
    write_tiles(q, u, e)


def write_messages(p, to_a, to_b):
    odd = (lax.axis_index("gx") & 1) == 1
    to_left = p[0, pl.ds(0, BLK, stride=2), :]
    to_right = p[1, pl.ds(1, BLK, stride=2), :]
    to_a[0:BLK, :] = jnp.where(odd, to_left, to_right)
    to_b[0:BLK, :] = jnp.where(odd, to_right, to_left)
    to_a[BLK:, :] = jnp.zeros((MROWS - BLK, LANES), F32)
    to_b[BLK:, :] = jnp.zeros((MROWS - BLK, LANES), F32)


def write_outer(n, from_a, from_b, outer):
    me = lax.axis_index("gx")
    odd = (me & 1) == 1
    end = (me == 0) | (me == n - 1)
    a, b = from_a[0:BLK, :], jnp.where(end, 0.0, from_b[0:BLK, :])
    outer[pl.ds(0, BLK, stride=2), :] = jnp.where(odd, a, b)
    outer[pl.ds(1, BLK, stride=2), :] = jnp.where(odd, b, a)


def write_schedule(order, sched):
    parity = lax.axis_index("gx") & 1
    place = []
    for side in (parity, 1 - parity):
        for q in (0, 1):
            c = 2 * side + q
            at = jnp.int32(0)
            for i in range(1, 4):
                at = jnp.where(order[i] == c, i, at)
            place.append(at)
    mine, theirs = place[:2], place[2:]
    first = jnp.where(mine[0] < mine[1], 0, 1)
    longer = ((order[0] ^ 2) == order[1]) & ((order[0] ^ 3) == order[2])
    s1, s2 = [], []
    for q in (0, 1):
        leads = mine[q] < theirs[q]
        long1 = jnp.where(mine[q] == 0, 0, jnp.where(mine[q] == 3, 2, 1))
        long2 = jnp.where(mine[q] == 0, 4, jnp.where(mine[q] == 3, 2, 3))
        s1.append(jnp.where(longer, long1, jnp.where(leads, 0, 1)))
        s2.append(jnp.where(longer, long2, jnp.where(leads, 4, 1)))
    zero = first == 0
    sched[0] = first
    sched[1] = 1 - first
    sched[2] = jnp.where(zero, s1[0], s1[1])
    sched[3] = jnp.where(zero, s1[1], s1[0])
    sched[4] = jnp.where(zero, s2[1], s2[0])
    sched[5] = jnp.where(zero, s2[0], s2[1])
    sched[6] = jnp.where(longer, 1, 0)


def slot(sched, t):
    q = sched[0] if t in (0, 3) else sched[1]
    return q, sched[2 + t]


def last_color(sched, phase):
    last = jnp.int32(-1)
    for t in range(4):
        q, at = slot(sched, t)
        last = jnp.where(at == phase, q, last)
    return last


def steps(phase, slots, dirty, sched, outer, source, w, winv, sel, u, p, e, rhs, sums):
    def step(t, _):
        q = jnp.where((t == 0) | (t == 3), sched[0], sched[1])

        @pl.when(sched[2 + t] == phase)
        def _():
            @pl.when(dirty[0] >= 0)
            def _():
                face_terms(dirty[0], (0, 4), w, p, e)

            incoming = local_incoming(p)
            if outer is not None:
                incoming = incoming + outer[...]
            update(q, incoming, source, winv, sel, u, e, rhs, sums)
            dirty[0] = q

        return 0

    lax.fori_loop(slots[0], slots[1], step, 0)


def first_kernel(order, coupling, inverse, source, w, winv, sel, sched, u, p, e, to_a, to_b, flag, rhs, sums, dirty, sems):
    copies = [pltpu.make_async_copy(inverse, winv, sems.at[0])]
    for f in range(4):
        pieces = pl.ds(2 * f, 2)
        copies.append(pltpu.make_async_copy(coupling.at[pieces], w.at[pieces], sems.at[1 + f]))
    for copy in copies:
        copy.start()
    write_schedule(order, sched)
    write_selector(sel)
    p[...] = jnp.zeros(p.shape, F32)
    u[...] = jnp.zeros(u.shape, F32)
    e[...] = jnp.zeros(e.shape, BF16)
    sums[48 * PAIRS :, :] = jnp.zeros((SUMS - 48 * PAIRS, LANES), BF16)
    flag[...] = jnp.zeros(flag.shape, F32) + sched[6].astype(F32)
    dirty[0] = -1
    copies[0].wait()
    compact(winv, 0, 1)
    steps(0, (0, 1), dirty, sched, None, source, w, winv, sel, u, p, e, rhs, sums)
    for f in range(4):
        copies[1 + f].wait()
        compact(w, 2 * f, 2 * f + 1)
    steps(0, (1, 2), dirty, sched, None, source, w, winv, sel, u, p, e, rhs, sums)

    @pl.when(dirty[0] >= 0)
    def _():
        face_terms(dirty[0], (0, 2), w, p, e)

    write_messages(p, to_a, to_b)


def phase_kernel(phase, n, sched, from_a, from_b, source, w, winv, sel, u_in, p_in, e_in, u, p, e, to_a, to_b, rhs, sums, outer, dirty):
    del u_in, p_in, e_in
    dirty[0] = -1
    last = last_color(sched, phase)

    @pl.when(last >= 0)
    def _():
        write_outer(n, from_a, from_b, outer)
        sums[48 * PAIRS :, :] = jnp.zeros((SUMS - 48 * PAIRS, LANES), BF16)
        steps(phase, (0, 4), dirty, sched, outer, source, w, winv, sel, u, p, e, rhs, sums)
        face_terms(dirty[0], (0, 2), w, p, e)

    write_messages(p, to_a, to_b)


def beside_kernel(phases, sched, w, e, p_in, p):
    del p_in
    last = jnp.int32(-1)
    for phase in reversed(phases):
        at = last_color(sched, phase)
        last = jnp.where(at >= 0, at, last)

    @pl.when(last >= 0)
    def _():
        face_terms(last, (2, 4), w, p, e)


def last_beside_kernel(phases, sched, w, e, u, p_in, p, adjoint, local):
    beside_kernel(phases, sched, w, e, p_in, p)
    local[...] = local_incoming(p)
    own0 = own_lanes((2 * HALF, LANES), 0)
    u0, u1 = u[0, 0 : 2 * HALF, :], u[1, 0 : 2 * HALF, :]
    adjoint[0 : 2 * HALF, :] = jnp.where(own0, u0, shift(u1, -TILE))
    adjoint[2 * HALF :, :] = jnp.where(own0, shift(u0, -TILE), u1)


def final_kernel(n, from_a, from_b, local, off, outer):
    write_outer(n, from_a, from_b, outer)
    off[...] = local[...] + outer[...]


def cost(products):
    return pl.CostEstimate(flops=products, bytes_accessed=products // 2, transcendentals=0)


def spec(space):
    return pl.BlockSpec(memory_space=space)


def pinned(x):
    return pltpu.with_memory_space_constraint(x, VMEM)


def params(mib):
    return pltpu.CompilerParams(vmem_limit_bytes=mib * 2**20)


def body(n, groups, coupling, inverse, source, order):
    coupling = coupling.reshape(8, HALF * ROWS, LANES)
    inverse = inverse.reshape(2, HALF * ROWS, LANES)
    source = source.reshape(ROWS, LANES)
    message = VMEM((MROWS, LANES), F32)
    u_shape, p_shape, e_shape = VMEM((2, MROWS, LANES), F32), VMEM((4, ROWS, LANES), F32), VMEM((PAIRS, 3, 16, LANES), BF16)
    work = [VMEM((PAIR, LANES), BF16), VMEM((SUMS, LANES), BF16)]
    outer = VMEM((ROWS, LANES), F32)
    small = SMEM((8,), jnp.int32)

    w, winv, sel, sched, u, p, e, to_a, to_b, flag = pl.pallas_call(
        first_kernel,
        out_shape=(
            VMEM(coupling.shape, BF16), VMEM(inverse.shape, BF16), VMEM((MROWS, SUMS), BF16), small,
            u_shape, p_shape, e_shape, message, message, VMEM((8, LANES), F32),
        ),
        in_specs=[spec(SMEM), spec(pl.ANY), spec(pl.ANY), spec(VMEM)],
        out_specs=(spec(VMEM),) * 3 + (spec(SMEM),) + (spec(VMEM),) * 6,
        scratch_shapes=work + [SMEM((1,), jnp.int32), pltpu.SemaphoreType.DMA((5,))],
        compiler_params=params(32),
        cost_estimate=cost(40_000_000),
        name="first",
    )(order, pltpu.with_memory_space_constraint(coupling, pltpu.HBM), pltpu.with_memory_space_constraint(inverse, pltpu.HBM), source)
    w, winv, sel = pinned(w), pinned(winv), pinned(sel)
    sched = pltpu.with_memory_space_constraint(sched, SMEM)

    flat = [(g, i) for g in range(groups) for i in range(n)]
    index = {gi: k for k, gi in enumerate(flat)}
    axes = ("groups", "gx")

    def across(g):
        return g ^ 1 if (g ^ 1) < groups else g

    swap_a = [(index[g, i], index[g, i ^ 1]) for g, i in flat]
    swap_b = []
    for g, i in flat:
        j = i + 1 if i & 1 else i - 1
        to = (across(g), i) if j in (-1, n) else (g, j)
        if to != (g, i):
            swap_b.append((index[g, i], index[to]))

    def exchange(to_a, to_b):
        from_b = lax.ppermute(to_b, axes, swap_b)
        from_a = lax.ppermute(to_a, axes, swap_a)
        return from_a, from_b

    def beside(phases, p, e):
        return pl.pallas_call(
            functools.partial(beside_kernel, phases),
            out_shape=p_shape,
            in_specs=[spec(SMEM), spec(VMEM), spec(VMEM), spec(VMEM)],
            out_specs=spec(VMEM),
            input_output_aliases={3: 0},
            compiler_params=params(16),
            cost_estimate=cost(4_000_000),
            name="beside",
        )(sched, w, pinned(e), pinned(p))

    def run_phase(phase, from_a, from_b, u, p, e):
        return pl.pallas_call(
            functools.partial(phase_kernel, phase, n),
            out_shape=(u_shape, p_shape, e_shape, message, message),
            in_specs=[spec(SMEM)] + [spec(VMEM)] * 9,
            out_specs=(spec(VMEM),) * 5,
            scratch_shapes=work + [outer, SMEM((1,), jnp.int32)],
            input_output_aliases={7: 0, 8: 1, 9: 2},
            compiler_params=params(16),
            cost_estimate=cost(20_000_000),
            name="phase",
        )(sched, from_a, from_b, source, w, winv, sel, pinned(u), pinned(p), pinned(e))

    def turn(before, phase, u, p, e, to_a, to_b):
        from_a, from_b = exchange(to_a, to_b)
        p = beside(before, p, e)
        return run_phase(phase, from_a, from_b, u, p, e)

    any_long = flag
    for by in range(1, groups):
        any_long = jnp.maximum(any_long, lax.ppermute(flag, "groups", [(g, (g + by) % groups) for g in range(groups)]))
    state = turn((0,), 1, u, p, e, to_a, to_b)

    def five(state):
        return turn((2,), 3, *turn((1,), 2, *state))

    state = lax.cond(any_long[0, 0] > 0, five, lambda s: s, state)
    u, p, e, to_a, to_b = turn((3, 1), 4, *state)

    from_a, from_b = exchange(to_a, to_b)
    p, adjoint, local = pl.pallas_call(
        functools.partial(last_beside_kernel, (4,)),
        out_shape=(p_shape, jax.ShapeDtypeStruct((ROWS, LANES), F32), VMEM((ROWS, LANES), F32)),
        in_specs=[spec(SMEM)] + [spec(VMEM)] * 4,
        out_specs=(spec(VMEM),) * 3,
        input_output_aliases={4: 0},
        compiler_params=params(16),
        cost_estimate=cost(4_000_000),
        name="last_beside",
    )(sched, w, pinned(e), pinned(u), pinned(p))
    off = pl.pallas_call(
        functools.partial(final_kernel, n),
        out_shape=jax.ShapeDtypeStruct((ROWS, LANES), F32),
        in_specs=[spec(VMEM)] * 3,
        out_specs=spec(VMEM),
        scratch_shapes=[outer],
        compiler_params=params(16),
        cost_estimate=cost(100_000),
        name="final",
    )(from_a, from_b, pinned(local))
    return adjoint.reshape(BLK, 2, LANES), off.reshape(BLK, 2, LANES)


def solution(mesh):
    call = functools.partial(body, mesh.shape["gx"], mesh.shape["groups"])
    return jax.shard_map(
        call,
        mesh=mesh,
        in_specs=(
            P("groups", None, None, "gx", None),
            P("groups", None, "gx", None),
            P("groups", "gx", None),
            P("groups"),
        ),
        out_specs=(P("groups", "gx", None), P("groups", "gx", None)),
        check_vma=False,
    )
```

```python
import functools

import jax
import jax.numpy as jnp
from jax import lax
from jax.experimental import pallas as pl
from jax.experimental.pallas import tpu as pltpu
from jax.sharding import PartitionSpec as P

BLK = 60
HALF = BLK // 2
ROWS = 2 * BLK
PAIR = 2 * ROWS
PAIRS = HALF // 2
TILE = 8
LANES = 128
MROWS = 64
CHUNK = 1200
F32, BF16 = jnp.float32, jnp.bfloat16
VMEM, SMEM = pltpu.VMEM, pltpu.SMEM


def lane(shape):
    return lax.broadcasted_iota(jnp.int32, shape, len(shape) - 1)


def row_parity(shape):
    return lax.broadcasted_iota(jnp.int32, shape, len(shape) - 2) & 1


def own_lanes(shape, q):
    return ((lane(shape) >> 3) & 1) == q


def shift(x, by):
    return pltpu.roll(x, by % LANES, len(x.shape) - 1)


def compact(ref, m):
    def step(k, _):
        rows = pl.ds(pl.multiple_of(k * CHUNK, CHUNK), CHUNK)
        even = (lax.broadcasted_iota(jnp.int16, (CHUNK, LANES), 1) & TILE) == 0
        first, second = ref[2 * m, rows, :], ref[2 * m + 1, rows, :]
        moved = shift(jnp.where(even, second, first), TILE)
        ref[2 * m, rows, :] = jnp.where(even, first, moved)
        ref[2 * m + 1, rows, :] = jnp.where(even, moved, second)
        return 0

    lax.fori_loop(0, HALF * ROWS // CHUNK, step, 0)


def local_incoming(p):
    shape = (ROWS // 8, 8, LANES)
    even = row_parity(shape) == 0
    from_right = pltpu.roll(p[0].reshape(shape), 7, 1)
    from_left = pltpu.roll(p[1].reshape(shape), 1, 1)
    inner = jnp.where(even, from_right, from_left).reshape(ROWS, LANES)
    y = lane((ROWS, LANES))
    above = jnp.where(y == LANES - 1, 0.0, shift(p[2], -1))
    below = jnp.where(y == 0, 0.0, shift(p[3], 1))
    return inner + above + below


def face_terms(q, faces, w, p, e, acc):
    def face(f, _):
        for first, end, tile in ((0, 4, 0), (4, 7, 0), (7, 8, 1), (8, 12, 2), (12, 15, 2)):
            total = None
            for k in range(PAIRS):
                block = w[2 * f + q, pl.ds(k * PAIR + 16 * first, 16 * (end - first)), :].reshape(end - first, 16, LANES)
                prod = block.astype(F32) * e[k, tile][None].astype(F32)
                total = prod if total is None else total + prod
            acc[pl.ds(16 * first, 16 * (end - first)), :] = total.reshape(16 * (end - first), LANES)
        half = acc[0:ROWS, :] + acc[ROWS:, :]
        part = half + shift(half, -TILE)
        p[faces + f] = jnp.where(own_lanes((ROWS, LANES), q), part, p[faces + f])
        return 0

    lax.fori_loop(0, 2, face, 0)


def update(q, incoming, source, winv, u, e, rhs, sums):
    value = (source[...] - incoming).astype(BF16).astype(F32)
    value = jnp.where(own_lanes((ROWS, LANES), q), value, shift(value, TILE))
    rhs[...] = jnp.concatenate([value, value], axis=0).astype(BF16)

    def step(g, _):
        for r in range(3):
            k = 3 * g + r
            rows = pl.ds(pl.multiple_of(k * PAIR, PAIR), PAIR)
            prod = winv[q, rows, :].astype(F32) * rhs[...].astype(F32)
            sums[2 * k] = jnp.sum(prod[:ROWS].reshape(ROWS // 8, 8, LANES), axis=0)
            sums[2 * k + 1] = jnp.sum(prod[ROWS:].reshape(ROWS // 8, 8, LANES), axis=0)
        return 0

    lax.fori_loop(0, PAIRS // 3, step, 0)
    total = sums[...]
    total = total + pltpu.roll(total, 4, 1)
    total = total + pltpu.roll(total, 2, 1)
    for k in range(PAIRS):
        first, second = total[2 * k], total[2 * k + 1]
        u[q, 4 * k : 4 * k + 2, :] = first[0:2]
        u[q, 4 * k + 2 : 4 * k + 4, :] = second[0:2]
        e[k, 0] = jnp.concatenate([first, first], axis=0).astype(BF16)
        e[k, 1] = jnp.concatenate([first, second], axis=0).astype(BF16)
        e[k, 2] = jnp.concatenate([second, second], axis=0).astype(BF16)


def write_messages(p, to_a, to_b):
    odd = (lax.axis_index("gx") & 1) == 1
    to_left = p[0, pl.ds(0, BLK, stride=2), :]
    to_right = p[1, pl.ds(1, BLK, stride=2), :]
    to_a[0:BLK, :] = jnp.where(odd, to_left, to_right)
    to_b[0:BLK, :] = jnp.where(odd, to_right, to_left)
    to_a[BLK:, :] = jnp.zeros((MROWS - BLK, LANES), F32)
    to_b[BLK:, :] = jnp.zeros((MROWS - BLK, LANES), F32)


def write_outer(n, from_a, from_b, outer):
    me = lax.axis_index("gx")
    odd = (me & 1) == 1
    end = (me == 0) | (me == n - 1)
    a, b = from_a[0:BLK, :], jnp.where(end, 0.0, from_b[0:BLK, :])
    outer[pl.ds(0, BLK, stride=2), :] = jnp.where(odd, a, b)
    outer[pl.ds(1, BLK, stride=2), :] = jnp.where(odd, b, a)


def write_schedule(order, sched):
    parity = lax.axis_index("gx") & 1
    place = []
    for side in (parity, 1 - parity):
        for q in (0, 1):
            c = 2 * side + q
            at = jnp.int32(0)
            for i in range(1, 4):
                at = jnp.where(order[i] == c, i, at)
            place.append(at)
    mine, theirs = place[:2], place[2:]
    first = jnp.where(mine[0] < mine[1], 0, 1)
    longer = ((order[0] ^ 2) == order[1]) & ((order[0] ^ 3) == order[2])
    s1, s2 = [], []
    for q in (0, 1):
        leads = mine[q] < theirs[q]
        long1 = jnp.where(mine[q] == 0, 0, jnp.where(mine[q] == 3, 2, 1))
        long2 = jnp.where(mine[q] == 0, 4, jnp.where(mine[q] == 3, 2, 3))
        s1.append(jnp.where(longer, long1, jnp.where(leads, 0, 1)))
        s2.append(jnp.where(longer, long2, jnp.where(leads, 2, 1)))
    zero = first == 0
    sched[0] = first
    sched[1] = 1 - first
    sched[2] = jnp.where(zero, s1[0], s1[1])
    sched[3] = jnp.where(zero, s1[1], s1[0])
    sched[4] = jnp.where(zero, s2[1], s2[0])
    sched[5] = jnp.where(zero, s2[0], s2[1])
    sched[6] = jnp.where(longer, 1, 0)


def slot(sched, t):
    q = sched[0] if t in (0, 3) else sched[1]
    return q, sched[2 + t]


def last_color(sched, phase):
    last = jnp.int32(-1)
    for t in range(4):
        q, at = slot(sched, t)
        last = jnp.where(at == phase, q, last)
    return last


def steps(phase, slots, dirty, sched, outer, source, wx, wy, winv, u, p, e, rhs, sums, acc):
    def step(t, _):
        q = jnp.where((t == 0) | (t == 3), sched[0], sched[1])

        @pl.when(sched[2 + t] == phase)
        def _():
            @pl.when(dirty[0] >= 0)
            def _():
                face_terms(dirty[0], 0, wx, p, e, acc)
                face_terms(dirty[0], 2, wy, p, e, acc)

            incoming = local_incoming(p)
            if outer is not None:
                incoming = incoming + outer[...]
            update(q, incoming, source, winv, u, e, rhs, sums)
            dirty[0] = q

        return 0

    lax.fori_loop(slots[0], slots[1], step, 0)


def both_first(sched):
    return (sched[2] == 0) & (sched[3] == 0)


def first_kernel(
    order_hbm, coupling, inverse, source_hbm,
    wx, wy, winv, source, sched, u, p, e, to_a, to_b, flag,
    order, rhs, sums, acc, dirty, sems,
):
    get_order = pltpu.make_async_copy(order_hbm, order, sems.at[0])
    get_inverse = pltpu.make_async_copy(inverse, winv, sems.at[1])
    get_source = pltpu.make_async_copy(source_hbm, source, sems.at[2])
    get_x = [pltpu.make_async_copy(coupling.at[pl.ds(2 * f, 2)], wx.at[pl.ds(2 * f, 2)], sems.at[3 + f]) for f in (0, 1)]
    get_y = [pltpu.make_async_copy(coupling.at[pl.ds(4 + 2 * f, 2)], wy.at[pl.ds(2 * f, 2)], sems.at[5 + f]) for f in (0, 1)]
    for copy in [get_order, get_inverse, get_source] + get_x:
        copy.start()
    p[...] = jnp.zeros(p.shape, F32)
    u[...] = jnp.zeros(u.shape, F32)
    e[...] = jnp.zeros(e.shape, BF16)
    dirty[0] = -1
    get_order.wait()
    write_schedule(order, sched)
    flag[...] = jnp.zeros(flag.shape, F32) + sched[6].astype(F32)
    work = (wx, wy, winv, u, p, e, rhs, sums, acc)
    get_inverse.wait()
    compact(winv, 0)
    get_source.wait()
    steps(0, (0, 1), dirty, sched, None, source, *work)
    for f in (0, 1):
        get_x[f].wait()
        compact(wx, f)

    @pl.when(both_first(sched))
    def _():
        for copy in get_y:
            copy.start()
        for f in (0, 1):
            get_y[f].wait()
            compact(wy, f)
        steps(0, (1, 2), dirty, sched, None, source, *work)

    @pl.when(dirty[0] >= 0)
    def _():
        face_terms(dirty[0], 0, wx, p, e, acc)

    write_messages(p, to_a, to_b)


def phase_kernel(
    phase, n, sched, from_a, from_b, source, wx, wy, winv, u_in, p_in, e_in,
    u, p, e, to_a, to_b, outer, rhs, sums, acc, dirty,
):
    del u_in, p_in, e_in
    dirty[0] = -1

    @pl.when(last_color(sched, phase) >= 0)
    def _():
        write_outer(n, from_a, from_b, outer)
        steps(phase, (0, 4), dirty, sched, outer, source, wx, wy, winv, u, p, e, rhs, sums, acc)
        face_terms(dirty[0], 0, wx, p, e, acc)

    write_messages(p, to_a, to_b)


def y_terms(phase, sched, wy, p, e, acc):
    last = last_color(sched, phase)

    @pl.when(last >= 0)
    def _():
        face_terms(last, 2, wy, p, e, acc)


def first_beside_kernel(sched, coupling, e, wy_in, p_in, wy, p, acc, sems):
    del wy_in, p_in
    get_y = [pltpu.make_async_copy(coupling.at[pl.ds(4 + 2 * f, 2)], wy.at[pl.ds(2 * f, 2)], sems.at[f]) for f in (0, 1)]

    @pl.when(jnp.logical_not(both_first(sched)))
    def _():
        for copy in get_y:
            copy.start()
        for f in (0, 1):
            get_y[f].wait()
            compact(wy, f)

    y_terms(0, sched, wy, p, e, acc)


def beside_kernel(phase, sched, wy, e, p_in, p, acc):
    del p_in
    y_terms(phase, sched, wy, p, e, acc)


def last_beside_kernel(phase, sched, wy, e, u, flag, p_in, p, adjoint, local, longer, acc):
    del p_in
    y_terms(phase, sched, wy, p, e, acc)
    local[...] = local_incoming(p)
    own0 = own_lanes((2 * HALF, LANES), 0)
    u0, u1 = u[0, 0 : 2 * HALF, :], u[1, 0 : 2 * HALF, :]
    adjoint[0 : 2 * HALF, :] = jnp.where(own0, u0, shift(u1, -TILE))
    adjoint[2 * HALF :, :] = jnp.where(own0, shift(u0, -TILE), u1)
    longer[0] = (flag[0, 0] > 0).astype(jnp.int32)


def final_kernel(n, from_a, from_b, local, off, outer):
    write_outer(n, from_a, from_b, outer)
    off[...] = local[...] + outer[...]


def cost(products):
    return pl.CostEstimate(flops=products, bytes_accessed=products // 2, transcendentals=0)


def spec(space):
    return pl.BlockSpec(memory_space=space)


def specs(text):
    return [spec({"v": VMEM, "s": SMEM, "h": pl.ANY}[c]) for c in text]


def pinned(x, space=VMEM):
    return pltpu.with_memory_space_constraint(x, space)


def params(mib):
    return pltpu.CompilerParams(vmem_limit_bytes=mib * 2**20)


def body(n, groups, coupling, inverse, source, order):
    coupling = pinned(coupling.reshape(8, HALF * ROWS, LANES), pltpu.HBM)
    inverse = pinned(inverse.reshape(2, HALF * ROWS, LANES), pltpu.HBM)
    source = pinned(source.reshape(ROWS, LANES), pltpu.HBM)
    message = VMEM((MROWS, LANES), F32)
    faces = VMEM((4, HALF * ROWS, LANES), BF16)
    u_shape, p_shape, e_shape = VMEM((2, MROWS, LANES), F32), VMEM((4, ROWS, LANES), F32), VMEM((PAIRS, 3, 16, LANES), BF16)
    rhs, sums, acc = VMEM((PAIR, LANES), BF16), VMEM((HALF, 8, LANES), F32), VMEM((PAIR, LANES), F32)
    outer = VMEM((ROWS, LANES), F32)
    dirty = SMEM((1,), jnp.int32)

    wx, wy, winv, source, sched, u, p, e, to_a, to_b, flag = pl.pallas_call(
        first_kernel,
        out_shape=(
            faces, faces, VMEM(inverse.shape, BF16), outer, SMEM((8,), jnp.int32),
            u_shape, p_shape, e_shape, message, message, VMEM((8, LANES), F32),
        ),
        in_specs=specs("hhhh"),
        out_specs=specs("vvvvsvvvvvv"),
        scratch_shapes=[SMEM((4,), jnp.int32), rhs, sums, acc, dirty, pltpu.SemaphoreType.DMA((7,))],
        compiler_params=params(8),
        cost_estimate=cost(40_000_000),
        name="first",
    )(pinned(order, pltpu.HBM), coupling, inverse, source)
    wx, winv, source, sched = pinned(wx), pinned(winv), pinned(source), pinned(sched, SMEM)

    flat = [(g, i) for g in range(groups) for i in range(n)]
    index = {gi: k for k, gi in enumerate(flat)}
    axes = ("groups", "gx")

    def across(g):
        return g ^ 1 if (g ^ 1) < groups else g

    swap_a = [(index[g, i], index[g, i ^ 1]) for g, i in flat]
    swap_b = []
    for g, i in flat:
        j = i + 1 if i & 1 else i - 1
        to = (across(g), i) if j in (-1, n) else (g, j)
        if to != (g, i):
            swap_b.append((index[g, i], index[to]))

    def exchange(to_a, to_b):
        from_b = lax.ppermute(to_b, axes, swap_b)
        from_a = lax.ppermute(to_a, axes, swap_a)
        return pinned(from_a), pinned(from_b)

    def beside(phase, p, e):
        return pl.pallas_call(
            functools.partial(beside_kernel, phase),
            out_shape=p_shape,
            in_specs=specs("svvv"),
            out_specs=spec(VMEM),
            scratch_shapes=[acc],
            input_output_aliases={3: 0},
            compiler_params=params(4),
            cost_estimate=cost(4_000_000),
            name="beside",
        )(sched, wy, pinned(e), pinned(p))

    def run_phase(phase, from_a, from_b, u, p, e):
        return pl.pallas_call(
            functools.partial(phase_kernel, phase, n),
            out_shape=(u_shape, p_shape, e_shape, message, message),
            in_specs=specs("svvvvvvvvv"),
            out_specs=specs("vvvvv"),
            scratch_shapes=[outer, rhs, sums, acc, dirty],
            input_output_aliases={7: 0, 8: 1, 9: 2},
            compiler_params=params(4),
            cost_estimate=cost(20_000_000),
            name="phase",
        )(sched, from_a, from_b, source, wx, wy, winv, pinned(u), pinned(p), pinned(e))

    def last_beside(phase, u, p, e):
        return pl.pallas_call(
            functools.partial(last_beside_kernel, phase),
            out_shape=(p_shape, jax.ShapeDtypeStruct((ROWS, LANES), F32), outer, SMEM((1,), jnp.int32)),
            in_specs=specs("svvvvv"),
            out_specs=specs("vvvs"),
            scratch_shapes=[acc],
            input_output_aliases={5: 0},
            compiler_params=params(4),
            cost_estimate=cost(4_000_000),
            name="last_beside",
        )(sched, wy, pinned(e), pinned(u), flag, pinned(p))

    from_a, from_b = exchange(to_a, to_b)
    for by in range(1, groups):
        other = lax.ppermute(flag, "groups", [(g, (g + by) % groups) for g in range(groups)])
        flag = jnp.maximum(flag, other)
    flag = pinned(flag)
    wy, p = pl.pallas_call(
        first_beside_kernel,
        out_shape=(faces, p_shape),
        in_specs=specs("shvvv"),
        out_specs=specs("vv"),
        scratch_shapes=[acc, pltpu.SemaphoreType.DMA((2,))],
        input_output_aliases={3: 0, 4: 1},
        compiler_params=params(4),
        cost_estimate=cost(8_000_000),
        name="first_beside",
    )(sched, coupling, pinned(e), pinned(wy), pinned(p))
    wy = pinned(wy)
    u, p, e, to_a, to_b = run_phase(1, from_a, from_b, u, p, e)

    from_a, from_b = exchange(to_a, to_b)
    p = beside(1, p, e)
    u, p, e, to_a, to_b = run_phase(2, from_a, from_b, u, p, e)

    from_a, from_b = exchange(to_a, to_b)
    p, adjoint, local, longer = last_beside(2, u, p, e)

    def more(state):
        from_a, from_b, u, p, e = state[:5]
        u, p, e, to_a, to_b = run_phase(3, pinned(from_a), pinned(from_b), u, p, e)
        from_a, from_b = exchange(to_a, to_b)
        p = beside(3, p, e)
        u, p, e, to_a, to_b = run_phase(4, from_a, from_b, u, p, e)
        from_a, from_b = exchange(to_a, to_b)
        _, adjoint, local, _ = last_beside(4, u, p, e)
        return from_a, from_b, adjoint, local

    def no_more(state):
        return state[0], state[1], state[5], state[6]

    state = (from_a, from_b, u, p, e, adjoint, local)
    from_a, from_b, adjoint, local = lax.cond(longer[0] > 0, more, no_more, state)
    off = pl.pallas_call(
        functools.partial(final_kernel, n),
        out_shape=jax.ShapeDtypeStruct((ROWS, LANES), F32),
        in_specs=specs("vvv"),
        out_specs=spec(VMEM),
        scratch_shapes=[outer],
        compiler_params=params(4),
        cost_estimate=cost(100_000),
        name="final",
    )(pinned(from_a), pinned(from_b), pinned(local))
    return adjoint.reshape(BLK, 2, LANES), off.reshape(BLK, 2, LANES)


def solution(mesh):
    call = functools.partial(body, mesh.shape["gx"], mesh.shape["groups"])
    return jax.shard_map(
        call,
        mesh=mesh,
        in_specs=(
            P("groups", None, None, "gx", None),
            P("groups", None, "gx", None),
            P("groups", "gx", None),
            P("groups"),
        ),
        out_specs=(P("groups", "gx", None), P("groups", "gx", None)),
        check_vma=False,
    )
```

```python
import functools

import jax
import jax.numpy as jnp
from jax import lax
from jax.experimental import pallas as pl
from jax.experimental.pallas import tpu as pltpu
from jax.sharding import PartitionSpec as P

BLK = 60
HALF = BLK // 2
ROWS = 2 * BLK
PAIR = 2 * ROWS
PAIRS = HALF // 2
TILE = 8
LANES = 128
MROWS = 64
CHUNK = 1200
F32, BF16 = jnp.float32, jnp.bfloat16
VMEM, SMEM = pltpu.VMEM, pltpu.SMEM


def lane(shape):
    return lax.broadcasted_iota(jnp.int32, shape, len(shape) - 1)


def row_parity(shape):
    return lax.broadcasted_iota(jnp.int32, shape, len(shape) - 2) & 1


def own_lanes(shape, q):
    return ((lane(shape) >> 3) & 1) == q


def shift(x, by):
    return pltpu.roll(x, by % LANES, len(x.shape) - 1)


def compact(ref, m):
    def step(k, _):
        rows = pl.ds(pl.multiple_of(k * CHUNK, CHUNK), CHUNK)
        even = (lax.broadcasted_iota(jnp.int16, (CHUNK, LANES), 1) & TILE) == 0
        first, second = ref[2 * m, rows, :], ref[2 * m + 1, rows, :]
        moved = shift(jnp.where(even, second, first), TILE)
        ref[2 * m, rows, :] = jnp.where(even, first, moved)
        ref[2 * m + 1, rows, :] = jnp.where(even, moved, second)
        return 0

    lax.fori_loop(0, HALF * ROWS // CHUNK, step, 0)


def local_incoming(p):
    shape = (ROWS // 8, 8, LANES)
    even = row_parity(shape) == 0
    from_right = pltpu.roll(p[0].reshape(shape), 7, 1)
    from_left = pltpu.roll(p[1].reshape(shape), 1, 1)
    inner = jnp.where(even, from_right, from_left).reshape(ROWS, LANES)
    y = lane((ROWS, LANES))
    above = jnp.where(y == LANES - 1, 0.0, shift(p[2], -1))
    below = jnp.where(y == 0, 0.0, shift(p[3], 1))
    return inner + above + below


def half_sum(w, m, tiles, acc, add):
    for first, end, tile in ((0, 4, 0), (4, 7, 0), (7, 8, 1), (8, 12, 2), (12, 15, 2)):
        total = None
        for k in range(PAIRS):
            block = w[m, pl.ds(k * PAIR + 16 * first, 16 * (end - first)), :].reshape(end - first, 16, LANES)
            prod = block.astype(F32) * tiles[k, tile][None].astype(F32)
            total = prod if total is None else total + prod
        rows = pl.ds(16 * first, 16 * (end - first))
        total = total.reshape(16 * (end - first), LANES)
        acc[rows, :] = acc[rows, :] + total if add else total


def face_terms(q, faces, w, p, e, acc):
    def face(f, _):
        half_sum(w, 2 * f + q, e, acc, False)
        half = acc[0:ROWS, :] + acc[ROWS:, :]
        part = half + shift(half, -TILE)
        p[faces + f] = jnp.where(own_lanes((ROWS, LANES), q), part, p[faces + f])
        return 0

    lax.fori_loop(0, 2, face, 0)


def plain_face_terms(q, faces, w, p, plain, acc):
    def face(f, _):
        acc[...] = jnp.zeros(acc.shape, F32)

        def half(h, _):
            half_sum(w, 2 * f + h, plain.at[h], acc, True)
            return 0

        lax.fori_loop(0, 2, half, 0)
        part = acc[0:ROWS, :] + acc[ROWS:, :]
        p[faces + f] = jnp.where(own_lanes((ROWS, LANES), q), part, p[faces + f])
        return 0

    lax.fori_loop(0, 2, face, 0)


def row_sums(winv, m, rhs, sums, at):
    def step(g, _):
        for r in range(3):
            k = 3 * g + r
            rows = pl.ds(pl.multiple_of(k * PAIR, PAIR), PAIR)
            prod = winv[m, rows, :].astype(F32) * rhs[...].astype(F32)
            sums[at + 2 * k] = jnp.sum(prod[:ROWS].reshape(ROWS // 8, 8, LANES), axis=0)
            sums[at + 2 * k + 1] = jnp.sum(prod[ROWS:].reshape(ROWS // 8, 8, LANES), axis=0)
        return 0

    lax.fori_loop(0, PAIRS // 3, step, 0)


def totals(sums):
    total = sums + pltpu.roll(sums, 4, 1)
    return total + pltpu.roll(total, 2, 1)


def write_tiles(total, e):
    for k in range(PAIRS):
        first, second = total[2 * k], total[2 * k + 1]
        e[k, 0] = jnp.concatenate([first, first], axis=0).astype(BF16)
        e[k, 1] = jnp.concatenate([first, second], axis=0).astype(BF16)
        e[k, 2] = jnp.concatenate([second, second], axis=0).astype(BF16)


def write_u(q, total, u):
    for i in range(HALF):
        u[q, 2 * i : 2 * i + 2, :] = total[i, 0:2]


def write_rhs(value, rhs):
    rhs[...] = jnp.concatenate([value, value], axis=0).astype(BF16)


def update(q, incoming, source, winv, u, e, rhs, sums):
    value = (source[...] - incoming).astype(BF16).astype(F32)
    write_rhs(jnp.where(own_lanes((ROWS, LANES), q), value, shift(value, TILE)), rhs)
    row_sums(winv, q, rhs, sums, 0)
    total = totals(sums[0:HALF])
    write_tiles(total, e)
    write_u(q, total, u)


def plain_update(q, incoming, source, winv, u, e, plain, rhs, sums):
    write_rhs(source[...] - incoming, rhs)

    def half(h, _):
        row_sums(winv, h, rhs, sums, HALF * h)
        return 0

    lax.fori_loop(0, 2, half, 0)
    both = [totals(sums[0:HALF]), totals(sums[HALF:])]
    for h in (0, 1):
        write_tiles(both[h], plain.at[h])
    zero = q == 0
    total = jnp.where(
        own_lanes((HALF, 8, LANES), q),
        jnp.where(zero, both[0], both[1]),
        shift(jnp.where(zero, both[1], both[0]), TILE),
    )
    write_tiles(total, e)
    write_u(q, total, u)


def write_messages(p, to_a, to_b):
    odd = (lax.axis_index("gx") & 1) == 1
    to_left = p[0, pl.ds(0, BLK, stride=2), :]
    to_right = p[1, pl.ds(1, BLK, stride=2), :]
    to_a[0:BLK, :] = jnp.where(odd, to_left, to_right)
    to_b[0:BLK, :] = jnp.where(odd, to_right, to_left)
    to_a[BLK:, :] = jnp.zeros((MROWS - BLK, LANES), F32)
    to_b[BLK:, :] = jnp.zeros((MROWS - BLK, LANES), F32)


def write_outer(n, from_a, from_b, outer):
    me = lax.axis_index("gx")
    odd = (me & 1) == 1
    end = (me == 0) | (me == n - 1)
    a, b = from_a[0:BLK, :], jnp.where(end, 0.0, from_b[0:BLK, :])
    outer[pl.ds(0, BLK, stride=2), :] = jnp.where(odd, a, b)
    outer[pl.ds(1, BLK, stride=2), :] = jnp.where(odd, b, a)


def write_schedule(order, sched):
    parity = lax.axis_index("gx") & 1
    place = []
    for side in (parity, 1 - parity):
        for q in (0, 1):
            c = 2 * side + q
            at = jnp.int32(0)
            for i in range(1, 4):
                at = jnp.where(order[i] == c, i, at)
            place.append(at)
    mine, theirs = place[:2], place[2:]
    first = jnp.where(mine[0] < mine[1], 0, 1)
    longer = ((order[0] ^ 2) == order[1]) & ((order[0] ^ 3) == order[2])
    s1, s2 = [], []
    for q in (0, 1):
        leads = mine[q] < theirs[q]
        long1 = jnp.where(mine[q] == 0, 0, jnp.where(mine[q] == 3, 2, 1))
        long2 = jnp.where(mine[q] == 0, 4, jnp.where(mine[q] == 3, 2, 3))
        s1.append(jnp.where(longer, long1, jnp.where(leads, 0, 1)))
        s2.append(jnp.where(longer, long2, jnp.where(leads, 2, 1)))
    zero = first == 0
    sched[0] = first
    sched[1] = 1 - first
    sched[2] = jnp.where(zero, s1[0], s1[1])
    sched[3] = jnp.where(zero, s1[1], s1[0])
    sched[4] = jnp.where(zero, s2[1], s2[0])
    sched[5] = jnp.where(zero, s2[0], s2[1])
    sched[6] = jnp.where(longer, 1, 0)


def slot(sched, t):
    q = sched[0] if t in (0, 3) else sched[1]
    return q, sched[2 + t]


def last_color(sched, phase):
    last = jnp.int32(-1)
    for t in range(4):
        q, at = slot(sched, t)
        last = jnp.where(at == phase, q, last)
    return last


def steps(phase, dirty, sched, outer, source, wx, wy, winv, u, p, e, rhs, sums, acc):
    def step(t, _):
        q = jnp.where((t == 0) | (t == 3), sched[0], sched[1])

        @pl.when(sched[2 + t] == phase)
        def _():
            @pl.when(dirty[0] >= 0)
            def _():
                face_terms(dirty[0], 0, wx, p, e, acc)
                face_terms(dirty[0], 2, wy, p, e, acc)

            update(q, local_incoming(p) + outer[...], source, winv, u, e, rhs, sums)
            dirty[0] = q

        return 0

    lax.fori_loop(0, 4, step, 0)


def rearrange(winv, wx, wy):
    compact(winv, 0)
    for w in (wx, wy):

        def face(f, _):
            compact(w, f)
            return 0

        lax.fori_loop(0, 2, face, 0)


def first_kernel(
    order_hbm, coupling, inverse, source_hbm,
    wx, wy, winv, source, sched, u, p, e, to_a, to_b,
    order, plain, rhs, sums, acc, sems,
):
    get_order = pltpu.make_async_copy(order_hbm, order, sems.at[0])
    get_source = pltpu.make_async_copy(source_hbm, source, sems.at[1])
    get_inverse = pltpu.make_async_copy(inverse, winv, sems.at[2])
    get_x = pltpu.make_async_copy(coupling.at[pl.ds(0, 4)], wx, sems.at[3])
    get_y = pltpu.make_async_copy(coupling.at[pl.ds(4, 4)], wy, sems.at[4])
    for copy in (get_order, get_source, get_inverse, get_x, get_y):
        copy.start()
    p[...] = jnp.zeros(p.shape, F32)
    u[...] = jnp.zeros(u.shape, F32)
    e[...] = jnp.zeros(e.shape, BF16)
    get_order.wait()
    write_schedule(order, sched)
    last = last_color(sched, 0)
    get_source.wait()
    get_inverse.wait()

    @pl.when(last >= 0)
    def _():
        plain_update(sched[0], jnp.zeros((ROWS, LANES), F32), source, winv, u, e, plain, rhs, sums)

    get_x.wait()

    @pl.when((last >= 0) & (last != sched[0]))
    def _():
        get_y.wait()
        plain_face_terms(sched[0], 0, wx, p, plain, acc)
        plain_face_terms(sched[0], 2, wy, p, plain, acc)
        plain_update(last, local_incoming(p), source, winv, u, e, plain, rhs, sums)

    @pl.when(last >= 0)
    def _():
        plain_face_terms(last, 0, wx, p, plain, acc)

    write_messages(p, to_a, to_b)

    @pl.when((last < 0) | (last == sched[0]))
    def _():
        get_y.wait()

    @pl.when(last < 0)
    def _():
        rearrange(winv, wx, wy)


def phase_kernel(
    phase, n, sched, from_a, from_b, source, wx, wy, winv, *rest
):
    extra = list(rest)
    flags = []
    while phase == 2 and len(extra) > 13 + 1:
        flags.append(extra.pop(0))
    u_in, p_in, e_in, u, p, e, to_a, to_b = extra[:8]
    outer, rhs, sums, acc, dirty = extra[-5:]
    if phase == 1:
        extra[8][...] = jnp.zeros(extra[8].shape, F32) + sched[6].astype(F32)
    if phase == 2:
        longer = sched[6]
        for flag in flags:
            longer = jnp.where(flag[0, 0] > 0, 1, longer)
        extra[8][0] = longer
    dirty[0] = -1

    @pl.when(last_color(sched, phase) >= 0)
    def _():
        write_outer(n, from_a, from_b, outer)
        steps(phase, dirty, sched, outer, source, wx, wy, winv, u, p, e, rhs, sums, acc)
        face_terms(dirty[0], 0, wx, p, e, acc)

    write_messages(p, to_a, to_b)


def y_terms(phase, sched, wy, p, e, acc):
    last = last_color(sched, phase)

    @pl.when(last >= 0)
    def _():
        face_terms(last, 2, wy, p, e, acc)


def first_beside_kernel(sched, e, winv_in, wx_in, wy_in, p_in, winv, wx, wy, p, acc):
    @pl.when(last_color(sched, 0) >= 0)
    def _():
        rearrange(winv, wx, wy)

    y_terms(0, sched, wy, p, e, acc)


def beside_kernel(phase, sched, wy, e, p_in, p, acc):
    del p_in
    y_terms(phase, sched, wy, p, e, acc)


def last_beside_kernel(phase, sched, wy, e, u, p_in, p, adjoint, local, acc):
    del p_in
    y_terms(phase, sched, wy, p, e, acc)
    local[...] = local_incoming(p)
    own0 = own_lanes((2 * HALF, LANES), 0)
    u0, u1 = u[0, 0 : 2 * HALF, :], u[1, 0 : 2 * HALF, :]
    adjoint[0 : 2 * HALF, :] = jnp.where(own0, u0, shift(u1, -TILE))
    adjoint[2 * HALF :, :] = jnp.where(own0, shift(u0, -TILE), u1)


def final_kernel(n, from_a, from_b, local, off, outer):
    write_outer(n, from_a, from_b, outer)
    off[...] = local[...] + outer[...]


def cost(products):
    return pl.CostEstimate(flops=products, bytes_accessed=products // 2, transcendentals=0)


def spec(space):
    return pl.BlockSpec(memory_space=space)


def specs(text):
    return [spec({"v": VMEM, "s": SMEM, "h": pl.ANY}[c]) for c in text]


def pinned(x, space=VMEM):
    return pltpu.with_memory_space_constraint(x, space)


def params(mib):
    return pltpu.CompilerParams(vmem_limit_bytes=mib * 2**20)


def body(n, groups, coupling, inverse, source, order):
    coupling = pinned(coupling.reshape(8, HALF * ROWS, LANES), pltpu.HBM)
    inverse = pinned(inverse.reshape(2, HALF * ROWS, LANES), pltpu.HBM)
    source = pinned(source.reshape(ROWS, LANES), pltpu.HBM)
    message, flag_shape = VMEM((MROWS, LANES), F32), VMEM((8, LANES), F32)
    faces, square = VMEM((4, HALF * ROWS, LANES), BF16), VMEM(inverse.shape, BF16)
    u_shape, p_shape, e_shape = VMEM((2, MROWS, LANES), F32), VMEM((4, ROWS, LANES), F32), VMEM((PAIRS, 3, 16, LANES), BF16)
    rhs, sums, acc = VMEM((PAIR, LANES), BF16), VMEM((BLK, 8, LANES), F32), VMEM((PAIR, LANES), F32)
    outer = VMEM((ROWS, LANES), F32)
    dirty = SMEM((1,), jnp.int32)

    wx, wy, winv, source, sched, u, p, e, to_a, to_b = pl.pallas_call(
        first_kernel,
        out_shape=(
            faces, faces, square, outer, SMEM((8,), jnp.int32), u_shape, p_shape, e_shape, message, message,
        ),
        in_specs=specs("hhhh"),
        out_specs=specs("vvvvsvvvvv"),
        scratch_shapes=[
            SMEM((4,), jnp.int32), VMEM((2, *e_shape.shape), BF16), rhs, sums, acc, pltpu.SemaphoreType.DMA((5,)),
        ],
        compiler_params=params(8),
        cost_estimate=cost(40_000_000),
        name="first",
    )(pinned(order, pltpu.HBM), coupling, inverse, source)
    source, sched = pinned(source), pinned(sched, SMEM)

    flat = [(g, i) for g in range(groups) for i in range(n)]
    index = {gi: k for k, gi in enumerate(flat)}
    axes = ("groups", "gx")

    def across(g):
        return g ^ 1 if (g ^ 1) < groups else g

    swap_a = [(index[g, i], index[g, i ^ 1]) for g, i in flat]
    swap_b = []
    for g, i in flat:
        j = i + 1 if i & 1 else i - 1
        to = (across(g), i) if j in (-1, n) else (g, j)
        if to != (g, i):
            swap_b.append((index[g, i], index[to]))

    def exchange(to_a, to_b):
        from_b = lax.ppermute(to_b, axes, swap_b)
        from_a = lax.ppermute(to_a, axes, swap_a)
        return from_a, from_b

    def beside(phase, p, e):
        return pl.pallas_call(
            functools.partial(beside_kernel, phase),
            out_shape=p_shape,
            in_specs=specs("svvv"),
            out_specs=spec(VMEM),
            scratch_shapes=[acc],
            input_output_aliases={3: 0},
            compiler_params=params(4),
            cost_estimate=cost(4_000_000),
            name="beside",
        )(sched, wy, pinned(e), pinned(p))

    def run_phase(phase, from_a, from_b, u, p, e, flags=()):
        more_out = {1: [flag_shape], 2: [SMEM((1,), jnp.int32)]}.get(phase, [])
        inputs = [sched, pinned(from_a), pinned(from_b), source, wx, wy, winv]
        inputs += [pinned(x) for x in (*flags, u, p, e)]
        at = len(inputs) - 3
        return pl.pallas_call(
            functools.partial(phase_kernel, phase, n),
            out_shape=[u_shape, p_shape, e_shape, message, message] + more_out,
            in_specs=specs("s" + "v" * (len(inputs) - 1)),
            out_specs=specs("vvvvv" + {1: "v", 2: "s"}.get(phase, "")),
            scratch_shapes=[outer, rhs, sums, acc, dirty],
            input_output_aliases={at: 0, at + 1: 1, at + 2: 2},
            compiler_params=params(4),
            cost_estimate=cost(20_000_000),
            name="phase",
        )(*inputs)

    def last_beside(phase, u, p, e):
        return pl.pallas_call(
            functools.partial(last_beside_kernel, phase),
            out_shape=(p_shape, jax.ShapeDtypeStruct((ROWS, LANES), F32), outer),
            in_specs=specs("svvvv"),
            out_specs=specs("vvv"),
            scratch_shapes=[acc],
            input_output_aliases={4: 0},
            compiler_params=params(4),
            cost_estimate=cost(4_000_000),
            name="last_beside",
        )(sched, wy, pinned(e), pinned(u), pinned(p))

    def final(from_a, from_b, local):
        return pl.pallas_call(
            functools.partial(final_kernel, n),
            out_shape=jax.ShapeDtypeStruct((ROWS, LANES), F32),
            in_specs=specs("vvv"),
            out_specs=spec(VMEM),
            scratch_shapes=[outer],
            compiler_params=params(4),
            cost_estimate=cost(100_000),
            name="final",
        )(pinned(from_a), pinned(from_b), pinned(local))

    from_a, from_b = exchange(to_a, to_b)
    winv, wx, wy, p = pl.pallas_call(
        first_beside_kernel,
        out_shape=(square, faces, faces, p_shape),
        in_specs=specs("svvvvv"),
        out_specs=specs("vvvv"),
        scratch_shapes=[acc],
        input_output_aliases={2: 0, 3: 1, 4: 2, 5: 3},
        compiler_params=params(4),
        cost_estimate=cost(8_000_000),
        name="first_beside",
    )(sched, pinned(e), pinned(winv), pinned(wx), pinned(wy), pinned(p))
    winv, wx, wy = pinned(winv), pinned(wx), pinned(wy)
    u, p, e, to_a, to_b, flag = run_phase(1, from_a, from_b, u, p, e)

    from_a, from_b = exchange(to_a, to_b)
    flags = [lax.ppermute(flag, "groups", [(g, (g + by) % groups) for g in range(groups)]) for by in range(1, groups)]
    p = beside(1, p, e)
    u, p, e, to_a, to_b, longer = run_phase(2, from_a, from_b, u, p, e, flags)

    from_a, from_b = exchange(to_a, to_b)
    p, adjoint, local = last_beside(2, u, p, e)

    def more(state):
        from_a, from_b, u, p, e = state[:5]
        u, p, e, to_a, to_b = run_phase(3, from_a, from_b, u, p, e)
        from_a, from_b = exchange(to_a, to_b)
        p = beside(3, p, e)
        u, p, e, to_a, to_b = run_phase(4, from_a, from_b, u, p, e)
        from_a, from_b = exchange(to_a, to_b)
        _, adjoint, local = last_beside(4, u, p, e)
        return adjoint, final(from_a, from_b, local)

    def no_more(state):
        from_a, from_b, _, _, _, adjoint, local = state
        return adjoint, final(from_a, from_b, local)

    state = (from_a, from_b, u, p, e, adjoint, local)
    adjoint, off = lax.cond(longer[0] > 0, more, no_more, state)
    return adjoint.reshape(BLK, 2, LANES), off.reshape(BLK, 2, LANES)


def solution(mesh):
    call = functools.partial(body, mesh.shape["gx"], mesh.shape["groups"])
    return jax.shard_map(
        call,
        mesh=mesh,
        in_specs=(
            P("groups", None, None, "gx", None),
            P("groups", None, "gx", None),
            P("groups", "gx", None),
            P("groups"),
        ),
        out_specs=(P("groups", "gx", None), P("groups", "gx", None)),
        check_vma=False,
    )
```

```python
import functools

import jax
import jax.numpy as jnp
from jax import lax
from jax.experimental import pallas as pl
from jax.experimental.pallas import tpu as pltpu
from jax.sharding import PartitionSpec as P

BLK = 60
HALF = BLK // 2
ROWS = 2 * BLK
PAIR = 2 * ROWS
PAIRS = HALF // 2
TILE = 8
LANES = 128
MROWS = 64
F32, BF16 = jnp.float32, jnp.bfloat16
VMEM, SMEM = pltpu.VMEM, pltpu.SMEM
LEAVES, STAYS, DOWN, UP = range(4)
STALE_Y, STALE_STAYS, STALE_LEAVES = 0, 2, 4


def lane(shape):
    return lax.broadcasted_iota(jnp.int32, shape, len(shape) - 1)


def even_row(shape):
    return (lax.broadcasted_iota(jnp.int32, shape, len(shape) - 2) & 1) == 0


def own_lanes(q):
    return ((lane((ROWS, LANES)) >> 3) & 1) == q


def shift(x, by):
    return pltpu.roll(x, by % LANES, len(x.shape) - 1)


def swapped_rows(x):
    x = x.reshape(ROWS // 8, 8, LANES)
    return jnp.where(even_row(x.shape), pltpu.roll(x, 7, 1), pltpu.roll(x, 1, 1)).reshape(ROWS, LANES)


def by_color(first, second):
    even = (lax.broadcasted_iota(jnp.int16, first.shape, 1) & TILE) == 0
    moved = shift(jnp.where(even, second, first), TILE)
    return jnp.where(even, first, moved), jnp.where(even, moved, second)


def rearrange(ref, m):
    chunk = 1200

    def step(k, _):
        rows = pl.ds(pl.multiple_of(k * chunk, chunk), chunk)
        ref[2 * m, rows, :], ref[2 * m + 1, rows, :] = by_color(ref[2 * m, rows, :], ref[2 * m + 1, rows, :])
        return 0

    lax.fori_loop(0, HALF * ROWS // chunk, step, 0)


def rearrange_x(w):
    chunk = 720

    def step(k, _):
        rows = pl.ds(pl.multiple_of(k * chunk, chunk), chunk)
        even = (lax.broadcasted_iota(jnp.int16, (chunk, LANES), 0) & 1) == 0
        left, right = [w[h, rows, :] for h in (0, 1)], [w[2 + h, rows, :] for h in (0, 1)]
        leaves = [jnp.where(even, left[h], right[h]) for h in (0, 1)]
        stays = [jnp.where(even, right[h], left[h]) for h in (0, 1)]
        w[2 * LEAVES, rows, :], w[2 * LEAVES + 1, rows, :] = by_color(*leaves)
        w[2 * STAYS, rows, :], w[2 * STAYS + 1, rows, :] = by_color(*stays)
        return 0

    lax.fori_loop(0, HALF * ROWS // chunk, step, 0)


def rearrange_y(w):
    def face(f, _):
        rearrange(w, f)
        return 0

    lax.fori_loop(DOWN, UP + 1, face, 0)


def half_sum(w, m, tiles, acc, at, add=False):
    for first, end, tile in ((0, 4, 0), (4, 7, 0), (7, 8, 1), (8, 12, 2), (12, 15, 2)):
        total = None
        for k in range(PAIRS):
            block = w[m, pl.ds(k * PAIR + 16 * first, 16 * (end - first)), :].reshape(end - first, 16, LANES)
            prod = block.astype(F32) * tiles[k, tile][None].astype(F32)
            total = prod if total is None else total + prod
        rows = pl.ds(16 * first, 16 * (end - first))
        total = total.reshape(16 * (end - first), LANES)
        acc[at, rows, :] = acc[at, rows, :] + total if add else total


def both_rows(acc, at):
    return acc[at, 0:ROWS, :] + acc[at, ROWS:, :]


def spread(half):
    return half + shift(half, -TILE)


def write_y(q, down, up, y):
    own, at = own_lanes(q), lane((ROWS, LANES))
    down = jnp.where(own & (at > 0), down, 0.0)
    up = jnp.where(own & (at < LANES - 1), up, 0.0)
    y[q] = shift(down, -1) + shift(up, 1)


def y_terms(q, w, e, y, acc):
    def face(f, _):
        half_sum(w, 2 * (DOWN + f) + q, e.at[q], acc, f)
        return 0

    lax.fori_loop(0, 2, face, 0)
    write_y(q, spread(both_rows(acc, 0)), spread(both_rows(acc, 1)), y)


def stay_terms(q, w, e, stays, acc):
    half_sum(w, 2 * STAYS + q, e.at[q], acc, 0)
    stays[q] = swapped_rows(jnp.where(own_lanes(q), spread(both_rows(acc, 0)), 0.0))


def leave_terms(q, w, e, leaves, acc):
    half_sum(w, 2 * LEAVES + q, e.at[q], acc, 0)
    leaves[...] = jnp.where(own_lanes(q), spread(both_rows(acc, 0)), leaves[...])


def plain_sums(face, w, plain, acc, copies):
    acc[...] = jnp.zeros(acc.shape, F32)

    def half(t, _):
        if copies is not None:
            copies(2 * face + t).wait()
        half_sum(w, 2 * face + t, plain.at[t & 1], acc, t >> 1, add=True)
        return 0

    lax.fori_loop(0, 4, half, 0)
    return both_rows(acc, 0), both_rows(acc, 1)


def plain_x_terms(q, w, plain, stays, leaves, acc, copies=None):
    left, right = plain_sums(0, w, plain, acc, copies)
    own, even = own_lanes(q), even_row((ROWS, LANES))
    leaves[...] = jnp.where(own, jnp.where(even, left, right), leaves[...])
    stays[q] = swapped_rows(jnp.where(own, jnp.where(even, right, left), 0.0))


def row_sums(winv, m, rhs, sums, at):
    for k in range(PAIRS):
        prod = winv[m, pl.ds(k * PAIR, PAIR), :].astype(F32) * rhs[...].astype(F32)
        sums[at + 2 * k] = jnp.sum(prod[:ROWS].reshape(ROWS // 8, 8, LANES), axis=0)
        sums[at + 2 * k + 1] = jnp.sum(prod[ROWS:].reshape(ROWS // 8, 8, LANES), axis=0)


def totals(sums):
    total = sums + pltpu.roll(sums, 4, 1)
    return total + pltpu.roll(total, 2, 1)


def write_tiles(total, e):
    for k in range(PAIRS):
        first, second = total[2 * k], total[2 * k + 1]
        e[k, 0] = jnp.concatenate([first, first], axis=0).astype(BF16)
        e[k, 1] = jnp.concatenate([first, second], axis=0).astype(BF16)
        e[k, 2] = jnp.concatenate([second, second], axis=0).astype(BF16)


def write_rhs(value, rhs):
    rhs[...] = jnp.concatenate([value, value], axis=0).astype(BF16)


def update(q, incoming, source, winv, u, e, rhs, sums):
    value = (source[...] - incoming).astype(BF16).astype(F32)
    write_rhs(jnp.where(own_lanes(q), value, shift(value, TILE)), rhs)
    row_sums(winv, q, rhs, sums, 0)
    total = totals(sums[0:HALF])
    write_tiles(total, e.at[q])
    u[q] = total


def plain_update(q, incoming, source, winv, u, e, plain, rhs, sums):
    write_rhs(source[...] - incoming, rhs)

    def half(h, _):
        row_sums(winv, h, rhs, sums, HALF * h)
        return 0

    lax.fori_loop(0, 2, half, 0)
    both = [totals(sums[0:HALF]), totals(sums[HALF:])]
    for h in (0, 1):
        write_tiles(both[h], plain.at[h])
    zero = q == 0
    own = ((lane((HALF, 8, LANES)) >> 3) & 1) == q
    mine, other = jnp.where(zero, both[0], both[1]), jnp.where(zero, both[1], both[0])
    total = jnp.where(own, mine, shift(other, TILE))
    write_tiles(total, e.at[q])
    u[q] = total


def local_incoming(y, stays):
    return (y[0] + y[1]) + (stays[0] + stays[1])


def write_messages(leaves, to_a, to_b):
    odd = (lax.axis_index("gx") & 1) == 1
    to_left = leaves[pl.ds(0, BLK, stride=2), :]
    to_right = leaves[pl.ds(1, BLK, stride=2), :]
    to_a[0:BLK, :] = jnp.where(odd, to_left, to_right)
    to_b[0:BLK, :] = jnp.where(odd, to_right, to_left)
    to_a[BLK:, :] = jnp.zeros((MROWS - BLK, LANES), F32)
    to_b[BLK:, :] = jnp.zeros((MROWS - BLK, LANES), F32)


def write_outer(n, from_a, from_b, outer):
    me = lax.axis_index("gx")
    odd = (me & 1) == 1
    end = (me == 0) | (me == n - 1)
    a, b = from_a[0:BLK, :], jnp.where(end, 0.0, from_b[0:BLK, :])
    outer[pl.ds(0, BLK, stride=2), :] = jnp.where(odd, a, b)
    outer[pl.ds(1, BLK, stride=2), :] = jnp.where(odd, b, a)


def write_schedule(order, sched):
    parity = lax.axis_index("gx") & 1
    place = []
    for side in (parity, 1 - parity):
        for q in (0, 1):
            c = 2 * side + q
            at = jnp.int32(0)
            for i in range(1, 4):
                at = jnp.where(order[i] == c, i, at)
            place.append(at)
    mine, theirs = place[:2], place[2:]
    first = jnp.where(mine[0] < mine[1], 0, 1)
    longer = ((order[0] ^ 2) == order[1]) & ((order[0] ^ 3) == order[2])
    s1, s2 = [], []
    for q in (0, 1):
        leads = mine[q] < theirs[q]
        long1 = jnp.where(mine[q] == 0, 0, jnp.where(mine[q] == 3, 2, 1))
        long2 = jnp.where(mine[q] == 0, 4, jnp.where(mine[q] == 3, 2, 3))
        s1.append(jnp.where(longer, long1, jnp.where(leads, 0, 1)))
        s2.append(jnp.where(longer, long2, jnp.where(leads, 2, 1)))
    zero = first == 0
    sched[0] = first
    sched[1] = 1 - first
    sched[2] = jnp.where(zero, s1[0], s1[1])
    sched[3] = jnp.where(zero, s1[1], s1[0])
    sched[4] = jnp.where(zero, s2[1], s2[0])
    sched[5] = jnp.where(zero, s2[0], s2[1])
    sched[6] = jnp.where(longer, 1, 0)


def slot(sched, t):
    q = sched[0] if t in (0, 3) else sched[1]
    return q, sched[2 + t]


def last_color(sched, phase):
    last = jnp.int32(-1)
    for t in range(4):
        q, at = slot(sched, t)
        last = jnp.where(at == phase, q, last)
    return last


def first_kernel(
    order_hbm, coupling, inverse, source_hbm,
    w, winv, source, sched, u, e, y, stays, leaves, to_a, to_b,
    order, plain, rhs, sums, acc, sems,
):
    get_order = pltpu.make_async_copy(order_hbm, order, sems.at[0])
    get_source = pltpu.make_async_copy(source_hbm, source, sems.at[1])
    get_inverse = pltpu.make_async_copy(inverse, winv, sems.at[2])

    def get(m):
        return pltpu.make_async_copy(coupling.at[m], w.at[m], sems.at[3 + m])

    def wait_for(first, end):
        def wait(m, _):
            get(m).wait()
            return 0

        lax.fori_loop(first, end, wait, 0)

    for copy in [get_order, get_source, get_inverse] + [get(m) for m in range(8)]:
        copy.start()
    for ref in (y, stays, leaves, u):
        ref[...] = jnp.zeros(ref.shape, F32)
    get_order.wait()
    write_schedule(order, sched)
    first, last = sched[0], last_color(sched, 0)
    get_source.wait()
    get_inverse.wait()

    @pl.when(last >= 0)
    def _():
        plain_update(first, jnp.zeros((ROWS, LANES), F32), source, winv, u, e, plain, rhs, sums)
        plain_x_terms(first, w, plain, stays, leaves, acc, get)

    @pl.when((last >= 0) & (last != first))
    def _():
        write_y(first, *plain_sums(2, w, plain, acc, get), y)
        plain_update(last, local_incoming(y, stays), source, winv, u, e, plain, rhs, sums)
        plain_x_terms(last, w, plain, stays, leaves, acc)

    write_messages(leaves, to_a, to_b)

    @pl.when(last == first)
    def _():
        wait_for(4, 8)

    @pl.when(last < 0)
    def _():
        rearrange(winv, 0)
        wait_for(0, 4)
        rearrange_x(w)
        wait_for(4, 8)
        rearrange_y(w)


def first_beside_kernel(sched, e, w_in, winv_in, y_in, stays, w, winv, y, local, acc):
    del w_in, winv_in, y_in
    last = last_color(sched, 0)

    @pl.when(last >= 0)
    def _():
        rearrange_y(w)
        y_terms(last, w, e, y, acc)
        local[...] = local_incoming(y, stays)
        rearrange(winv, 0)
        rearrange_x(w)

    @pl.when(last < 0)
    def _():
        local[...] = local_incoming(y, stays)


def phase_kernel(
    phase, n, sched, from_b, from_a, source, w, winv, local, u_in, e_in, y_in, stays_in, leaves_in,
    u, e, y, stays, leaves, to_a, to_b, stale, outer, now, rhs, sums, acc,
):
    del u_in, e_in, y_in, stays_in, leaves_in
    for i in range(6):
        stale[i] = 0

    @pl.when(last_color(sched, phase) >= 0)
    def _():
        write_outer(n, from_a, from_b, outer)
        outer[...] = source[...] - outer[...]
        now[...] = local[...]

        def step(t, fresh):
            q = jnp.where((t == 0) | (t == 3), sched[0], sched[1])
            active = sched[2 + t] == phase

            @pl.when(active & jnp.logical_not(fresh))
            def _():
                def color(c, _):
                    @pl.when(stale[STALE_Y + c] == 1)
                    def _():
                        y_terms(c, w, e, y, acc)
                        stale[STALE_Y + c] = 0

                    return 0

                lax.fori_loop(0, 2, color, 0)

                @pl.when(stale[STALE_STAYS + q] == 1)
                def _():
                    stay_terms(q, w, e, stays, acc)
                    stale[STALE_STAYS + q] = 0

                now[...] = local_incoming(y, stays)

            @pl.when(active)
            def _():
                update(q, now[...], outer, winv, u, e, rhs, sums)
                for kind in (STALE_Y, STALE_STAYS, STALE_LEAVES):
                    stale[kind + q] = 1

            return fresh & jnp.logical_not(active)

        lax.fori_loop(0, 4, step, True)

        def color(c, _):
            @pl.when(stale[STALE_LEAVES + c] == 1)
            def _():
                leave_terms(c, w, e, leaves, acc)

            return 0

        lax.fori_loop(0, 2, color, 0)

    write_messages(leaves, to_a, to_b)


def beside_kernel(stale, w, e, y_in, stays_in, y, stays, local, acc):
    del y_in, stays_in

    def color(c, _):
        @pl.when(stale[STALE_Y + c] == 1)
        def _():
            y_terms(c, w, e, y, acc)

        @pl.when(stale[STALE_STAYS + c] == 1)
        def _():
            stay_terms(c, w, e, stays, acc)

        return 0

    lax.fori_loop(0, 2, color, 0)
    local[...] = local_incoming(y, stays)


def last_beside_kernel(sched, stale, w, e, u, y_in, stays_in, y, stays, adjoint, local, longer, acc):
    beside_kernel(stale, w, e, y_in, stays_in, y, stays, local, acc)
    longer[0] = sched[6]
    even = ((lane((2, LANES)) >> 3) & 1) == 0
    for i in range(HALF):
        u0, u1 = u[0, i, 0:2, :], u[1, i, 0:2, :]
        adjoint[2 * i : 2 * i + 2, :] = jnp.where(even, u0, shift(u1, -TILE))
        adjoint[ROWS // 2 + 2 * i : ROWS // 2 + 2 * i + 2, :] = jnp.where(even, shift(u0, -TILE), u1)


def final_kernel(n, from_b, from_a, local, off, outer):
    write_outer(n, from_a, from_b, outer)
    off[...] = local[...] + outer[...]


def cost(products):
    return pl.CostEstimate(flops=products, bytes_accessed=products // 2, transcendentals=0)


def spec(space):
    return pl.BlockSpec(memory_space=space)


def specs(text):
    return [spec({"v": VMEM, "s": SMEM, "h": pl.ANY}[c]) for c in text]


def pinned(x, space=VMEM):
    return pltpu.with_memory_space_constraint(x, space)


def params(mib):
    return pltpu.CompilerParams(vmem_limit_bytes=mib * 2**20)


def body(n, groups, coupling, inverse, source, order):
    coupling = pinned(coupling.reshape(8, HALF * ROWS, LANES), pltpu.HBM)
    inverse = pinned(inverse.reshape(2, HALF * ROWS, LANES), pltpu.HBM)
    source = pinned(source.reshape(ROWS, LANES), pltpu.HBM)
    w_shape, winv_shape = VMEM(coupling.shape, BF16), VMEM(inverse.shape, BF16)
    message, field, two = VMEM((MROWS, LANES), F32), VMEM((ROWS, LANES), F32), VMEM((2, ROWS, LANES), F32)
    u_shape, e_shape = VMEM((2, HALF, 8, LANES), F32), VMEM((2, PAIRS, 3, 16, LANES), BF16)
    rhs, sums, acc = VMEM((PAIR, LANES), BF16), VMEM((BLK, 8, LANES), F32), VMEM((2, PAIR, LANES), F32)
    flags = SMEM((8,), jnp.int32)

    w, winv, source, sched, u, e, y, stays, leaves, to_a, to_b = pl.pallas_call(
        first_kernel,
        out_shape=(w_shape, winv_shape, field, flags, u_shape, e_shape, two, two, field, message, message),
        in_specs=specs("hhhh"),
        out_specs=specs("vvvsvvvvvvv"),
        scratch_shapes=[
            SMEM((4,), jnp.int32), VMEM((2, PAIRS, 3, 16, LANES), BF16), rhs, sums, acc, pltpu.SemaphoreType.DMA((11,)),
        ],
        compiler_params=params(8),
        cost_estimate=cost(40_000_000),
        name="first",
    )(pinned(order, pltpu.HBM), coupling, inverse, source)
    source, sched = pinned(source), pinned(sched, SMEM)

    flat = [(g, i) for g in range(groups) for i in range(n)]
    index = {gi: k for k, gi in enumerate(flat)}
    axes = ("groups", "gx")

    def across(g):
        return g ^ 1 if (g ^ 1) < groups else g

    swap_a = [(index[g, i], index[g, i ^ 1]) for g, i in flat]
    swap_b, inner_b = [], []
    for g, i in flat:
        j = i + 1 if i & 1 else i - 1
        if j in (-1, n):
            if across(g) != g:
                swap_b.append((index[g, i], index[across(g), i]))
        else:
            swap_b.append((index[g, i], index[g, j]))
            inner_b.append((index[g, i], index[g, j]))

    def exchange(to_a, to_b, pairs_b):
        from_b = lax.ppermute(to_b, axes, pairs_b)
        from_a = lax.ppermute(to_a, axes, swap_a)
        return from_a, from_b

    def run_phase(phase, from_a, from_b, local, u, e, y, stays, leaves):
        return pl.pallas_call(
            functools.partial(phase_kernel, phase, n),
            out_shape=(u_shape, e_shape, two, two, field, message, message, flags),
            in_specs=specs("svvvvvvvvvvv"),
            out_specs=specs("vvvvvvvs"),
            scratch_shapes=[field, field, rhs, sums, acc],
            input_output_aliases={7: 0, 8: 1, 9: 2, 10: 3, 11: 4},
            compiler_params=params(4),
            cost_estimate=cost(20_000_000),
            name="phase",
        )(
            sched, pinned(from_b), pinned(from_a), source, w, winv, pinned(local),
            pinned(u), pinned(e), pinned(y), pinned(stays), pinned(leaves),
        )

    def beside(stale, e, y, stays):
        return pl.pallas_call(
            beside_kernel,
            out_shape=(two, two, field),
            in_specs=specs("svvvv"),
            out_specs=specs("vvv"),
            scratch_shapes=[acc],
            input_output_aliases={3: 0, 4: 1},
            compiler_params=params(4),
            cost_estimate=cost(4_000_000),
            name="beside",
        )(pinned(stale, SMEM), w, pinned(e), pinned(y), pinned(stays))

    def last_beside(stale, u, e, y, stays):
        return pl.pallas_call(
            last_beside_kernel,
            out_shape=(two, two, jax.ShapeDtypeStruct((ROWS, LANES), F32), field, SMEM((1,), jnp.int32)),
            in_specs=specs("ssvvvvv"),
            out_specs=specs("vvvvs"),
            scratch_shapes=[acc],
            input_output_aliases={5: 0, 6: 1},
            compiler_params=params(4),
            cost_estimate=cost(4_000_000),
            name="last_beside",
        )(sched, pinned(stale, SMEM), w, pinned(e), pinned(u), pinned(y), pinned(stays))

    def final(from_a, from_b, local):
        return pl.pallas_call(
            functools.partial(final_kernel, n),
            out_shape=jax.ShapeDtypeStruct((ROWS, LANES), F32),
            in_specs=specs("vvv"),
            out_specs=spec(VMEM),
            scratch_shapes=[field],
            compiler_params=params(4),
            cost_estimate=cost(100_000),
            name="final",
        )(pinned(from_b), pinned(from_a), pinned(local))

    from_a, from_b = exchange(to_a, to_b, swap_b)
    w, winv, y, local = pl.pallas_call(
        first_beside_kernel,
        out_shape=(w_shape, winv_shape, two, field),
        in_specs=specs("svvvvv"),
        out_specs=specs("vvvv"),
        scratch_shapes=[acc],
        input_output_aliases={2: 0, 3: 1, 4: 2},
        compiler_params=params(4),
        cost_estimate=cost(8_000_000),
        name="first_beside",
    )(sched, pinned(e), pinned(w), pinned(winv), pinned(y), pinned(stays))
    w, winv = pinned(w), pinned(winv)
    u, e, y, stays, leaves, to_a, to_b, stale = run_phase(1, from_a, from_b, local, u, e, y, stays, leaves)

    from_a, from_b = exchange(to_a, to_b, swap_b)
    y, stays, local = beside(stale, e, y, stays)
    u, e, y, stays, leaves, to_a, to_b, stale = run_phase(2, from_a, from_b, local, u, e, y, stays, leaves)

    from_a, from_b = exchange(to_a, to_b, swap_b)
    y, stays, adjoint, local, longer = last_beside(stale, u, e, y, stays)

    def more(state):
        from_a, from_b, adjoint, local, u, e, y, stays, leaves = state
        u, e, y, stays, leaves, to_a, to_b, stale = run_phase(3, from_a, from_b, local, u, e, y, stays, leaves)
        from_a, from_b = exchange(to_a, to_b, inner_b)
        y, stays, local = beside(stale, e, y, stays)
        u, e, y, stays, leaves, to_a, to_b, stale = run_phase(4, from_a, from_b, local, u, e, y, stays, leaves)
        from_a, from_b = exchange(to_a, to_b, inner_b)
        y, stays, adjoint, local, _ = last_beside(stale, u, e, y, stays)
        return adjoint, final(from_a, from_b, local)

    def no_more(state):
        from_a, from_b, adjoint, local = state[:4]
        return adjoint, final(from_a, from_b, local)

    state = (from_a, from_b, adjoint, local, u, e, y, stays, leaves)
    adjoint, off = lax.cond(longer[0] > 0, more, no_more, state)
    return adjoint.reshape(BLK, 2, LANES), off.reshape(BLK, 2, LANES)


def solution(mesh):
    call = functools.partial(body, mesh.shape["gx"], mesh.shape["groups"])
    return jax.shard_map(
        call,
        mesh=mesh,
        in_specs=(
            P("groups", None, None, "gx", None),
            P("groups", None, "gx", None),
            P("groups", "gx", None),
            P("groups"),
        ),
        out_specs=(P("groups", "gx", None), P("groups", "gx", None)),
        check_vma=False,
    )
```

```python
import functools

import jax
import jax.numpy as jnp
from jax import lax
from jax.experimental import pallas as pl
from jax.experimental.pallas import tpu as pltpu
from jax.sharding import PartitionSpec as P

BLK = 60
HALF = BLK // 2
ROWS = 2 * BLK
PAIR = 2 * ROWS
PAIRS = HALF // 2
TILE = 8
LANES = 128
MROWS = 64
F32, BF16 = jnp.float32, jnp.bfloat16
VMEM, SMEM = pltpu.VMEM, pltpu.SMEM
LEAVES, STAYS, DOWN, UP = range(4)
STALE_Y, STALE_STAYS, STALE_LEAVES = 0, 2, 4


def lane(shape):
    return lax.broadcasted_iota(jnp.int32, shape, len(shape) - 1)


def even_row(shape):
    return (lax.broadcasted_iota(jnp.int32, shape, len(shape) - 2) & 1) == 0


def own_lanes(q):
    return ((lane((ROWS, LANES)) >> 3) & 1) == q


def shift(x, by):
    return pltpu.roll(x, by % LANES, len(x.shape) - 1)


def swapped_rows(x):
    x = x.reshape(ROWS // 8, 8, LANES)
    return jnp.where(even_row(x.shape), pltpu.roll(x, 7, 1), pltpu.roll(x, 1, 1)).reshape(ROWS, LANES)


def by_color(first, second):
    even = (lax.broadcasted_iota(jnp.int16, first.shape, 1) & TILE) == 0
    moved = shift(jnp.where(even, second, first), TILE)
    return jnp.where(even, first, moved), jnp.where(even, moved, second)


def rearrange(ref, m):
    chunk = 1200

    def step(k, _):
        rows = pl.ds(pl.multiple_of(k * chunk, chunk), chunk)
        ref[2 * m, rows, :], ref[2 * m + 1, rows, :] = by_color(ref[2 * m, rows, :], ref[2 * m + 1, rows, :])
        return 0

    lax.fori_loop(0, HALF * ROWS // chunk, step, 0)


def rearrange_x(w):
    chunk = 720

    def step(k, _):
        rows = pl.ds(pl.multiple_of(k * chunk, chunk), chunk)
        even = (lax.broadcasted_iota(jnp.int16, (chunk, LANES), 0) & 1) == 0
        left, right = [w[h, rows, :] for h in (0, 1)], [w[2 + h, rows, :] for h in (0, 1)]
        leaves = [jnp.where(even, left[h], right[h]) for h in (0, 1)]
        stays = [jnp.where(even, right[h], left[h]) for h in (0, 1)]
        w[2 * LEAVES, rows, :], w[2 * LEAVES + 1, rows, :] = by_color(*leaves)
        w[2 * STAYS, rows, :], w[2 * STAYS + 1, rows, :] = by_color(*stays)
        return 0

    lax.fori_loop(0, HALF * ROWS // chunk, step, 0)


def rearrange_y(w):
    def face(f, _):
        rearrange(w, f)
        return 0

    lax.fori_loop(DOWN, UP + 1, face, 0)


def half_sum(w, m, tiles, acc, at, add=False):
    for first, end, tile in ((0, 4, 0), (4, 7, 0), (7, 8, 1), (8, 12, 2), (12, 15, 2)):
        total = None
        for k in range(PAIRS):
            block = w[m, pl.ds(k * PAIR + 16 * first, 16 * (end - first)), :].reshape(end - first, 16, LANES)
            prod = block.astype(F32) * tiles[k, tile][None].astype(F32)
            total = prod if total is None else total + prod
        rows = pl.ds(16 * first, 16 * (end - first))
        total = total.reshape(16 * (end - first), LANES)
        acc[at, rows, :] = acc[at, rows, :] + total if add else total


def both_rows(acc, at):
    return acc[at, 0:ROWS, :] + acc[at, ROWS:, :]


def spread(half):
    return half + shift(half, -TILE)


def write_y(q, down, up, y):
    own, at = own_lanes(q), lane((ROWS, LANES))
    down = jnp.where(own & (at > 0), down, 0.0)
    up = jnp.where(own & (at < LANES - 1), up, 0.0)
    y[q] = shift(down, -1) + shift(up, 1)


def y_terms(q, w, e, y, acc):
    def face(f, _):
        half_sum(w, 2 * (DOWN + f) + q, e.at[q], acc, f)
        return 0

    lax.fori_loop(0, 2, face, 0)
    write_y(q, spread(both_rows(acc, 0)), spread(both_rows(acc, 1)), y)


def stay_terms(q, w, e, stays, acc):
    half_sum(w, 2 * STAYS + q, e.at[q], acc, 0)
    stays[q] = swapped_rows(jnp.where(own_lanes(q), spread(both_rows(acc, 0)), 0.0))


def leave_terms(q, w, e, leaves, acc):
    half_sum(w, 2 * LEAVES + q, e.at[q], acc, 0)
    leaves[...] = jnp.where(own_lanes(q), spread(both_rows(acc, 0)), leaves[...])


def plain_sums(face, w, plain, acc, copies):
    acc[...] = jnp.zeros(acc.shape, F32)

    def half(t, _):
        if copies is not None:
            copies(2 * face + t).wait()
        half_sum(w, 2 * face + t, plain.at[t & 1], acc, t >> 1, add=True)
        return 0

    lax.fori_loop(0, 4, half, 0)
    return both_rows(acc, 0), both_rows(acc, 1)


def plain_x_terms(q, w, plain, stays, leaves, acc, copies=None):
    left, right = plain_sums(0, w, plain, acc, copies)
    own, even = own_lanes(q), even_row((ROWS, LANES))
    leaves[...] = jnp.where(own, jnp.where(even, left, right), leaves[...])
    stays[q] = swapped_rows(jnp.where(own, jnp.where(even, right, left), 0.0))


def row_sums(winv, m, rhs, sums, at):
    for k in range(PAIRS):
        prod = winv[m, pl.ds(k * PAIR, PAIR), :].astype(F32) * rhs[...].astype(F32)
        sums[at + 2 * k] = jnp.sum(prod[:ROWS].reshape(ROWS // 8, 8, LANES), axis=0)
        sums[at + 2 * k + 1] = jnp.sum(prod[ROWS:].reshape(ROWS // 8, 8, LANES), axis=0)


def totals(sums):
    total = sums + pltpu.roll(sums, 4, 1)
    return total + pltpu.roll(total, 2, 1)


def write_tiles(total, e):
    for k in range(PAIRS):
        first, second = total[2 * k], total[2 * k + 1]
        e[k, 0] = jnp.concatenate([first, first], axis=0).astype(BF16)
        e[k, 1] = jnp.concatenate([first, second], axis=0).astype(BF16)
        e[k, 2] = jnp.concatenate([second, second], axis=0).astype(BF16)


def write_rhs(value, rhs):
    rhs[...] = jnp.concatenate([value, value], axis=0).astype(BF16)


def update(q, incoming, source, winv, u, e, rhs, sums):
    value = (source[...] - incoming).astype(BF16).astype(F32)
    write_rhs(jnp.where(own_lanes(q), value, shift(value, TILE)), rhs)
    row_sums(winv, q, rhs, sums, 0)
    total = totals(sums[0:HALF])
    write_tiles(total, e.at[q])
    u[q] = total


def plain_update(q, incoming, source, winv, u, e, plain, rhs, sums):
    write_rhs(source[...] - incoming, rhs)

    def half(h, _):
        row_sums(winv, h, rhs, sums, HALF * h)
        return 0

    lax.fori_loop(0, 2, half, 0)
    both = [totals(sums[0:HALF]), totals(sums[HALF:])]
    for h in (0, 1):
        write_tiles(both[h], plain.at[h])
    zero = q == 0
    own = ((lane((HALF, 8, LANES)) >> 3) & 1) == q
    mine, other = jnp.where(zero, both[0], both[1]), jnp.where(zero, both[1], both[0])
    total = jnp.where(own, mine, shift(other, TILE))
    write_tiles(total, e.at[q])
    u[q] = total


def local_incoming(y, stays):
    return (y[0] + y[1]) + (stays[0] + stays[1])


def write_messages(leaves, to_a, to_b):
    odd = (lax.axis_index("gx") & 1) == 1
    to_left = leaves[pl.ds(0, BLK, stride=2), :]
    to_right = leaves[pl.ds(1, BLK, stride=2), :]
    to_a[0:BLK, :] = jnp.where(odd, to_left, to_right)
    to_b[0:BLK, :] = jnp.where(odd, to_right, to_left)
    to_a[BLK:, :] = jnp.zeros((MROWS - BLK, LANES), F32)
    to_b[BLK:, :] = jnp.zeros((MROWS - BLK, LANES), F32)


def write_outer(n, from_a, from_b, outer):
    me = lax.axis_index("gx")
    odd = me & 1
    inside = (me > 0) & (me < n - 1)
    outer[pl.ds(1 - odd, BLK, stride=2), :] = from_a[0:BLK, :]
    for k, ref in from_b:

        @pl.when(inside & (odd == 1 - k))
        def _():
            outer[pl.ds(1 - k, BLK, stride=2), :] = ref[0:BLK, :]


def write_schedule(order, sched, mixed, lead):
    parity = lax.axis_index("gx") & 1
    place = []
    for side in (parity, 1 - parity):
        for q in (0, 1):
            c = 2 * side + q
            at = jnp.int32(0)
            for i in range(1, 4):
                at = jnp.where(order[i] == c, i, at)
            place.append(at)
    mine, theirs = place[:2], place[2:]
    first = jnp.where(mine[0] < mine[1], 0, 1)
    longer = ((order[0] ^ 2) == order[1]) & ((order[0] ^ 3) == order[2])
    s1, s2 = [], []
    for q in (0, 1):
        leads = mine[q] < theirs[q]
        long1 = jnp.where(mine[q] == 0, 0, jnp.where(mine[q] == 3, 2, 1))
        long2 = jnp.where(mine[q] == 0, 4, jnp.where(mine[q] == 3, 2, 3))
        s1.append(jnp.where(longer, long1, jnp.where(leads, 0, 1)))
        s2.append(jnp.where(longer, long2, jnp.where(leads, 2, 1)))
    zero = first == 0
    sched[0] = first
    sched[1] = 1 - first
    sched[2] = jnp.where(zero, s1[0], s1[1])
    sched[3] = jnp.where(zero, s1[1], s1[0])
    sched[4] = jnp.where(zero, s2[1], s2[0])
    sched[5] = jnp.where(zero, s2[0], s2[1])
    sched[6] = jnp.where(longer, 1, 0)
    mixed[0] = jnp.where((order[0] ^ 3) == order[1], 1, 0)
    lead[0] = order[0] >> 1


def slot(sched, t):
    q = sched[0] if t in (0, 3) else sched[1]
    return q, sched[2 + t]


def last_color(sched, phase):
    last = jnp.int32(-1)
    for t in range(4):
        q, at = slot(sched, t)
        last = jnp.where(at == phase, q, last)
    return last


def first_kernel(
    order_hbm, coupling, inverse, source_hbm,
    w, winv, source, sched, mixed, side, u, e, y, stays, leaves, outer, to_a, to_b,
    order, plain, rhs, sums, acc, sems,
):
    get_order = pltpu.make_async_copy(order_hbm, order, sems.at[0])
    get_source = pltpu.make_async_copy(source_hbm, source, sems.at[1])
    get_inverse = pltpu.make_async_copy(inverse, winv, sems.at[2])

    def get(m):
        return pltpu.make_async_copy(coupling.at[m], w.at[m], sems.at[3 + m])

    def wait_for(first, end):
        def wait(m, _):
            get(m).wait()
            return 0

        lax.fori_loop(first, end, wait, 0)

    for copy in (get_order, get_inverse, get_source):
        copy.start()
    for ref in (y, stays, leaves, u, outer):
        ref[...] = jnp.zeros(ref.shape, F32)
    get_order.wait()
    write_schedule(order, sched, mixed, side)
    first, last = sched[0], last_color(sched, 0)
    both = (last >= 0) & (last != first)

    def start(m, _):
        get(m ^ jnp.where(both, 4, 0)).start()
        return 0

    lax.fori_loop(0, 8, start, 0)
    get_source.wait()
    get_inverse.wait()

    @pl.when(last >= 0)
    def _():
        plain_update(first, jnp.zeros((ROWS, LANES), F32), source, winv, u, e, plain.at[0], rhs, sums)

    @pl.when(both)
    def _():
        write_y(first, *plain_sums(2, w, plain.at[0], acc, get), y)
        plain_update(last, local_incoming(y, stays), source, winv, u, e, plain.at[1], rhs, sums)

    @pl.when(last >= 0)
    def _():
        plain_x_terms(first, w, plain.at[0], stays, leaves, acc, get)

    @pl.when(both)
    def _():
        plain_x_terms(last, w, plain.at[1], stays, leaves, acc)

    write_messages(leaves, to_a, to_b)

    @pl.when(last < 0)
    def _():
        rearrange(winv, 0)
        wait_for(0, 4)
        rearrange_x(w)

    @pl.when(jnp.logical_not(both))
    def _():
        wait_for(4, 8)


def first_beside_kernel(sched, e, w_in, winv_in, y_in, stays, w, winv, y, local, acc):
    del w_in, winv_in, y_in
    last = last_color(sched, 0)
    rearrange_y(w)

    @pl.when(last >= 0)
    def _():
        y_terms(last, w, e, y, acc)
        rearrange(winv, 0)
        rearrange_x(w)

    local[...] = local_incoming(y, stays)


def phase_kernel(
    phase, n, sides, sched, *refs
):
    from_b, refs = [(k, ref) for k, ref in zip(sides, refs)], refs[len(sides) :]
    from_a, source, w, winv, local = refs[:5]
    u, e, y, stays, leaves, outer, to_a, to_b, stale, known, now, rhs, sums, acc = refs[11:]
    for i in range(6):
        stale[i] = 0
    write_outer(n, from_a, from_b, outer)

    @pl.when(last_color(sched, phase) >= 0)
    def _():
        known[...] = source[...] - outer[...]
        now[...] = local[...]

        def step(t, fresh):
            q = jnp.where((t == 0) | (t == 3), sched[0], sched[1])
            active = sched[2 + t] == phase

            @pl.when(active & jnp.logical_not(fresh))
            def _():
                def color(c, _):
                    @pl.when(stale[STALE_Y + c] == 1)
                    def _():
                        y_terms(c, w, e, y, acc)
                        stale[STALE_Y + c] = 0

                    return 0

                lax.fori_loop(0, 2, color, 0)

                @pl.when(stale[STALE_STAYS + q] == 1)
                def _():
                    stay_terms(q, w, e, stays, acc)
                    stale[STALE_STAYS + q] = 0

                now[...] = local_incoming(y, stays)

            @pl.when(active)
            def _():
                update(q, now[...], known, winv, u, e, rhs, sums)
                for kind in (STALE_Y, STALE_STAYS, STALE_LEAVES):
                    stale[kind + q] = 1

            return fresh & jnp.logical_not(active)

        lax.fori_loop(0, 4, step, True)

        def color(c, _):
            @pl.when(stale[STALE_LEAVES + c] == 1)
            def _():
                leave_terms(c, w, e, leaves, acc)

            return 0

        lax.fori_loop(0, 2, color, 0)

    write_messages(leaves, to_a, to_b)


def beside_kernel(stale, w, e, y_in, stays_in, y, stays, local, acc):
    del y_in, stays_in

    def color(c, _):
        @pl.when(stale[STALE_Y + c] == 1)
        def _():
            y_terms(c, w, e, y, acc)

        @pl.when(stale[STALE_STAYS + c] == 1)
        def _():
            stay_terms(c, w, e, stays, acc)

        return 0

    lax.fori_loop(0, 2, color, 0)
    local[...] = local_incoming(y, stays)


def last_beside_kernel(sched, stale, w, e, u, y_in, stays_in, y, stays, adjoint, local, longer, acc):
    beside_kernel(stale, w, e, y_in, stays_in, y, stays, local, acc)
    longer[0] = sched[6]
    even = ((lane((2, LANES)) >> 3) & 1) == 0
    for i in range(HALF):
        u0, u1 = u[0, i, 0:2, :], u[1, i, 0:2, :]
        adjoint[2 * i : 2 * i + 2, :] = jnp.where(even, u0, shift(u1, -TILE))
        adjoint[ROWS // 2 + 2 * i : ROWS // 2 + 2 * i + 2, :] = jnp.where(even, shift(u0, -TILE), u1)


def final_kernel(n, sides, *refs):
    from_b = [(k, ref) for k, ref in zip(sides, refs)]
    from_a, local, outer_in, off, outer = refs[len(sides) :]
    outer[...] = outer_in[...]
    write_outer(n, from_a, from_b, outer)
    off[...] = local[...] + outer[...]


def cost(products):
    return pl.CostEstimate(flops=products, bytes_accessed=products // 2, transcendentals=0)


def spec(space):
    return pl.BlockSpec(memory_space=space)


def specs(text):
    return [spec({"v": VMEM, "s": SMEM, "h": pl.ANY}[c]) for c in text]


def pinned(x, space=VMEM):
    return pltpu.with_memory_space_constraint(x, space)


def params(mib):
    return pltpu.CompilerParams(vmem_limit_bytes=mib * 2**20)


def body(n, groups, coupling, inverse, source, order):
    coupling = pinned(coupling.reshape(8, HALF * ROWS, LANES), pltpu.HBM)
    inverse = pinned(inverse.reshape(2, HALF * ROWS, LANES), pltpu.HBM)
    source = pinned(source.reshape(ROWS, LANES), pltpu.HBM)
    w_shape, winv_shape = VMEM(coupling.shape, BF16), VMEM(inverse.shape, BF16)
    message, field, two = VMEM((MROWS, LANES), F32), VMEM((ROWS, LANES), F32), VMEM((2, ROWS, LANES), F32)
    u_shape, e_shape = VMEM((2, HALF, 8, LANES), F32), VMEM((2, PAIRS, 3, 16, LANES), BF16)
    rhs, sums, acc = VMEM((PAIR, LANES), BF16), VMEM((BLK, 8, LANES), F32), VMEM((2, PAIR, LANES), F32)
    flags, flag = SMEM((8,), jnp.int32), SMEM((1,), jnp.int32)

    w, winv, source, sched, mixed, side, *state = pl.pallas_call(
        first_kernel,
        out_shape=(
            w_shape, winv_shape, field, flags, flag, flag, u_shape, e_shape, two, two, field, field, message, message,
        ),
        in_specs=specs("hhhh"),
        out_specs=specs("vvvsssvvvvvvvv"),
        scratch_shapes=[
            SMEM((4,), jnp.int32), VMEM((2, *e_shape.shape), BF16), rhs, sums, acc, pltpu.SemaphoreType.DMA((11,)),
        ],
        compiler_params=params(8),
        cost_estimate=cost(40_000_000),
        name="first",
    )(pinned(order, pltpu.HBM), coupling, inverse, source)

    axes = ("groups", "gx")

    def in_groups(to):
        return [(g * n + i, g * n + j) for g in range(groups) for i, j in to.items()]

    swap = in_groups({i: i ^ 1 for i in range(n)})

    def side_pairs(k):
        to = {i: i + 1 if i & 1 else i - 1 for i in range(3, n - 3)}
        to |= {0: 1, 1: 2, 2: 0} if k else {0: 2, 2: 1, 1: 0}
        to |= {n - 3: n - 2, n - 2: n - 1, n - 1: n - 3} if k else {n - 2: n - 3, n - 3: n - 1, n - 1: n - 2}
        return in_groups(to)

    def exchange(sides, to_a, to_b):
        from_b = [lax.ppermute(to_b, axes, side_pairs(k)) for k in sides]
        return [*from_b, lax.ppermute(to_a, axes, swap)]

    def rest(turns, w, winv, source, sched, u, e, y, stays, leaves, outer, to_a, to_b):
        source, sched = pinned(source), pinned(sched, SMEM)

        def run_phase(phase, sides, received, local, u, e, y, stays, leaves, outer):
            inputs = [*received, source, w, winv, local, u, e, y, stays, leaves, outer]
            at = len(inputs) - 5
            return pl.pallas_call(
                functools.partial(phase_kernel, phase, n, sides),
                out_shape=(u_shape, e_shape, two, two, field, field, message, message, flags),
                in_specs=specs("s" + "v" * len(inputs)),
                out_specs=specs("vvvvvvvvs"),
                scratch_shapes=[field, field, rhs, sums, acc],
                input_output_aliases={at + i: i for i in range(6)},
                compiler_params=params(4),
                cost_estimate=cost(20_000_000),
                name="phase",
            )(sched, *[pinned(x) for x in inputs])

        def beside(stale, e, y, stays):
            return pl.pallas_call(
                beside_kernel,
                out_shape=(two, two, field),
                in_specs=specs("svvvv"),
                out_specs=specs("vvv"),
                scratch_shapes=[acc],
                input_output_aliases={3: 0, 4: 1},
                compiler_params=params(4),
                cost_estimate=cost(4_000_000),
                name="beside",
            )(pinned(stale, SMEM), w, pinned(e), pinned(y), pinned(stays))

        def last_beside(stale, u, e, y, stays):
            return pl.pallas_call(
                last_beside_kernel,
                out_shape=(two, two, jax.ShapeDtypeStruct((ROWS, LANES), F32), field, flag),
                in_specs=specs("ssvvvvv"),
                out_specs=specs("vvvvs"),
                scratch_shapes=[acc],
                input_output_aliases={5: 0, 6: 1},
                compiler_params=params(4),
                cost_estimate=cost(4_000_000),
                name="last_beside",
            )(sched, pinned(stale, SMEM), w, pinned(e), pinned(u), pinned(y), pinned(stays))

        def final(sides, received, local, outer):
            inputs = [*received, local, outer]
            return pl.pallas_call(
                functools.partial(final_kernel, n, sides),
                out_shape=jax.ShapeDtypeStruct((ROWS, LANES), F32),
                in_specs=specs("v" * len(inputs)),
                out_specs=spec(VMEM),
                scratch_shapes=[field],
                compiler_params=params(4),
                cost_estimate=cost(100_000),
                name="final",
            )(*[pinned(x) for x in inputs])

        received = exchange(turns[0], to_a, to_b)
        w, winv, y, local = pl.pallas_call(
            first_beside_kernel,
            out_shape=(w_shape, winv_shape, two, field),
            in_specs=specs("svvvvv"),
            out_specs=specs("vvvv"),
            scratch_shapes=[acc],
            input_output_aliases={2: 0, 3: 1, 4: 2},
            compiler_params=params(4),
            cost_estimate=cost(8_000_000),
            name="first_beside",
        )(sched, pinned(e), pinned(w), pinned(winv), pinned(y), pinned(stays))
        w, winv = pinned(w), pinned(winv)

        def two_phases(phase, received, local, u, e, y, stays, leaves, outer):
            for i in (phase, phase + 1):
                u, e, y, stays, leaves, outer, to_a, to_b, stale = run_phase(
                    i, turns[i - 1], received, local, u, e, y, stays, leaves, outer
                )
                received = exchange(turns[i], to_a, to_b)
                if i == phase:
                    y, stays, local = beside(stale, e, y, stays)
            y, stays, adjoint, local, longer = last_beside(stale, u, e, y, stays)
            return longer, adjoint, received, (local, u, e, y, stays, leaves, outer)

        longer, adjoint, received, state = two_phases(1, received, local, u, e, y, stays, leaves, outer)

        def more(adjoint, received, *state):
            _, adjoint, received, (local, *_, outer) = two_phases(3, received, *state)
            return adjoint, final(turns[4], received, local, outer)

        def no_more(adjoint, received, local, *state):
            return adjoint, final(turns[2], received, local, state[-1])

        if len(turns) < 5:
            return no_more(adjoint, received, *state)
        return lax.cond(longer[0] > 0, more, no_more, adjoint, received, *state)

    def from_side(k):
        return functools.partial(rest, [(k,) if i % 2 == 0 else (1 - k,) for i in range(5)])

    def one_side(*state):
        return lax.cond(side[0] > 0, from_side(1), from_side(0), *state)

    both_sides = functools.partial(rest, [(0, 1)] * 3)
    adjoint, off = lax.cond(mixed[0] > 0, both_sides, one_side, w, winv, source, sched, *state)
    return adjoint.reshape(BLK, 2, LANES), off.reshape(BLK, 2, LANES)


def solution(mesh):
    call = functools.partial(body, mesh.shape["gx"], mesh.shape["groups"])
    return jax.shard_map(
        call,
        mesh=mesh,
        in_specs=(
            P("groups", None, None, "gx", None),
            P("groups", None, "gx", None),
            P("groups", "gx", None),
            P("groups"),
        ),
        out_specs=(P("groups", "gx", None), P("groups", "gx", None)),
        check_vma=False,
    )
```

```python
import functools

import jax
import jax.numpy as jnp
from jax import lax
from jax.experimental import pallas as pl
from jax.experimental.pallas import tpu as pltpu
from jax.sharding import PartitionSpec as P

BLK = 60
HALF = BLK // 2
ROWS = 2 * BLK
PAIR = 2 * ROWS
PAIRS = HALF // 2
TILE = 8
LANES = 128
MROWS = 64
F32, BF16 = jnp.float32, jnp.bfloat16
VMEM, SMEM = pltpu.VMEM, pltpu.SMEM
LEAVES, STAYS, DOWN, UP = range(4)


def lane(shape):
    return lax.broadcasted_iota(jnp.int32, shape, len(shape) - 1)


def even_row(shape):
    return (lax.broadcasted_iota(jnp.int32, shape, len(shape) - 2) & 1) == 0


def own_lanes(q):
    return ((lane((ROWS, LANES)) >> 3) & 1) == q


def shift(x, by):
    return pltpu.roll(x, by % LANES, len(x.shape) - 1)


def swapped_rows(x):
    x = x.reshape(ROWS // 8, 8, LANES)
    return jnp.where(even_row(x.shape), pltpu.roll(x, 7, 1), pltpu.roll(x, 1, 1)).reshape(ROWS, LANES)


def by_color(first, second):
    even = (lax.broadcasted_iota(jnp.int16, first.shape, 1) & TILE) == 0
    moved = shift(jnp.where(even, second, first), TILE)
    return jnp.where(even, first, moved), jnp.where(even, moved, second)


def rearrange(ref, m):
    chunk = 1200

    def step(k, _):
        rows = pl.ds(pl.multiple_of(k * chunk, chunk), chunk)
        ref[2 * m, rows, :], ref[2 * m + 1, rows, :] = by_color(ref[2 * m, rows, :], ref[2 * m + 1, rows, :])
        return 0

    lax.fori_loop(0, HALF * ROWS // chunk, step, 0)


def rearrange_x(w):
    chunk = 720

    def step(k, _):
        rows = pl.ds(pl.multiple_of(k * chunk, chunk), chunk)
        even = (lax.broadcasted_iota(jnp.int16, (chunk, LANES), 0) & 1) == 0
        left, right = [w[h, rows, :] for h in (0, 1)], [w[2 + h, rows, :] for h in (0, 1)]
        leaves = [jnp.where(even, left[h], right[h]) for h in (0, 1)]
        stays = [jnp.where(even, right[h], left[h]) for h in (0, 1)]
        w[2 * LEAVES, rows, :], w[2 * LEAVES + 1, rows, :] = by_color(*leaves)
        w[2 * STAYS, rows, :], w[2 * STAYS + 1, rows, :] = by_color(*stays)
        return 0

    lax.fori_loop(0, HALF * ROWS // chunk, step, 0)


def rearrange_y(w):
    def face(f, _):
        rearrange(w, f)
        return 0

    lax.fori_loop(DOWN, UP + 1, face, 0)


def half_sum(w, m, tiles, acc, at, add=False):
    for first, end, tile in ((0, 4, 0), (4, 7, 0), (7, 8, 1), (8, 12, 2), (12, 15, 2)):
        total = None
        for k in range(PAIRS):
            block = w[m, pl.ds(k * PAIR + 16 * first, 16 * (end - first)), :].reshape(end - first, 16, LANES)
            prod = block.astype(F32) * tiles[k, tile][None].astype(F32)
            total = prod if total is None else total + prod
        rows = pl.ds(16 * first, 16 * (end - first))
        total = total.reshape(16 * (end - first), LANES)
        acc[at, rows, :] = acc[at, rows, :] + total if add else total


def both_rows(acc, at):
    return acc[at, 0:ROWS, :] + acc[at, ROWS:, :]


def spread(half):
    return half + shift(half, -TILE)


def below_and_above(q, down, up, moves):
    at = lane((ROWS, LANES))
    down_to = (((at + 1) >> 3) & 1 == q) & (at < LANES - 1)
    up_to = (((at - 1) >> 3) & 1 == q) & (at > 0)
    down, up = sum(shift(down, -1 - by) for by in moves), sum(shift(up, 1 - by) for by in moves)
    return jnp.where(down_to, down, 0.0) + jnp.where(up_to, up, 0.0)


def local_terms(q, w, e, terms, acc):
    for kind in (DOWN, UP, STAYS):
        half_sum(w, 2 * kind + q, e.at[q], acc, kind)
    y = below_and_above(q, both_rows(acc, DOWN), both_rows(acc, UP), (0, TILE))
    stays = jnp.where(own_lanes(q), spread(both_rows(acc, STAYS)), 0.0)
    terms[q] = y + swapped_rows(stays)


def leave_terms(q, w, e, leaves, acc):
    half_sum(w, 2 * LEAVES + q, e.at[q], acc, LEAVES)
    leaves[...] = jnp.where(own_lanes(q), spread(both_rows(acc, LEAVES)), leaves[...])


def all_leave_terms(w, e, leaves, acc):
    for q in (0, 1):
        half_sum(w, 2 * LEAVES + q, e.at[q], acc, q)
    leaves[...] = jnp.where(own_lanes(0), spread(both_rows(acc, 0)), spread(both_rows(acc, 1)))


def plain_sums(face, w, plain, acc, copies):
    acc[...] = jnp.zeros(acc.shape, F32)

    def half(t, _):
        if copies is not None:
            copies(2 * face + t).wait()
        half_sum(w, 2 * face + t, plain.at[t & 1], acc, t >> 1, add=True)
        return 0

    lax.fori_loop(0, 4, half, 0)
    return both_rows(acc, 0), both_rows(acc, 1)


def plain_x_terms(q, w, plain, terms, leaves, acc, copies=None):
    left, right = plain_sums(0, w, plain, acc, copies)
    own, even = own_lanes(q), even_row((ROWS, LANES))
    leaves[...] = jnp.where(own, jnp.where(even, left, right), leaves[...])
    terms[q] = terms[q] + swapped_rows(jnp.where(own, jnp.where(even, right, left), 0.0))


def row_sums(winv, m, rhs, sums, at):
    for k in range(PAIRS):
        prod = winv[m, pl.ds(k * PAIR, PAIR), :].astype(F32) * rhs[...].astype(F32)
        sums[at + 2 * k] = jnp.sum(prod[:ROWS].reshape(ROWS // 8, 8, LANES), axis=0)
        sums[at + 2 * k + 1] = jnp.sum(prod[ROWS:].reshape(ROWS // 8, 8, LANES), axis=0)


def totals(sums):
    total = sums + pltpu.roll(sums, 4, 1)
    return total + pltpu.roll(total, 2, 1)


def write_tiles(total, e):
    for k in range(PAIRS):
        first, second = total[2 * k], total[2 * k + 1]
        e[k, 0] = jnp.concatenate([first, first], axis=0).astype(BF16)
        e[k, 1] = jnp.concatenate([first, second], axis=0).astype(BF16)
        e[k, 2] = jnp.concatenate([second, second], axis=0).astype(BF16)


def write_rhs(value, rhs):
    rhs[...] = jnp.concatenate([value, value], axis=0).astype(BF16)


def update(q, incoming, source, winv, u, e, rhs, sums):
    value = (source[...] - incoming).astype(BF16).astype(F32)
    write_rhs(jnp.where(own_lanes(q), value, shift(value, TILE)), rhs)
    row_sums(winv, q, rhs, sums, 0)
    total = totals(sums[0:HALF])
    write_tiles(total, e.at[q])
    u[q] = total


def plain_update(q, incoming, source, winv, u, e, plain, rhs, sums):
    write_rhs(source[...] - incoming, rhs)

    def half(h, _):
        row_sums(winv, h, rhs, sums, HALF * h)
        return 0

    lax.fori_loop(0, 2, half, 0)
    both = [totals(sums[0:HALF]), totals(sums[HALF:])]
    for h in (0, 1):
        write_tiles(both[h], plain.at[h])
    zero = q == 0
    own = ((lane((HALF, 8, LANES)) >> 3) & 1) == q
    mine, other = jnp.where(zero, both[0], both[1]), jnp.where(zero, both[1], both[0])
    total = jnp.where(own, mine, shift(other, TILE))
    write_tiles(total, e.at[q])
    u[q] = total


def write_messages(leaves, to_a, to_b):
    odd = (lax.axis_index("gx") & 1) == 1
    to_left = leaves[pl.ds(0, BLK, stride=2), :]
    to_right = leaves[pl.ds(1, BLK, stride=2), :]
    to_a[0:BLK, :] = jnp.where(odd, to_left, to_right)
    to_b[0:BLK, :] = jnp.where(odd, to_right, to_left)
    to_a[BLK:, :] = jnp.zeros((MROWS - BLK, LANES), F32)
    to_b[BLK:, :] = jnp.zeros((MROWS - BLK, LANES), F32)


def write_outer(n, from_a, from_b, outer):
    me = lax.axis_index("gx")
    odd = me & 1
    inside = (me > 0) & (me < n - 1)
    outer[pl.ds(1 - odd, BLK, stride=2), :] = from_a[0:BLK, :]
    for k, ref in from_b:

        @pl.when(inside & (odd == 1 - k))
        def _():
            outer[pl.ds(1 - k, BLK, stride=2), :] = ref[0:BLK, :]


def write_schedule(order, sched, mixed, lead):
    parity = lax.axis_index("gx") & 1
    place = []
    for side in (parity, 1 - parity):
        for q in (0, 1):
            c = 2 * side + q
            at = jnp.int32(0)
            for i in range(1, 4):
                at = jnp.where(order[i] == c, i, at)
            place.append(at)
    mine, theirs = place[:2], place[2:]
    first = jnp.where(mine[0] < mine[1], 0, 1)
    longer = ((order[0] ^ 2) == order[1]) & ((order[0] ^ 3) == order[2])
    s1, s2 = [], []
    for q in (0, 1):
        leads = mine[q] < theirs[q]
        long1 = jnp.where(mine[q] == 0, 0, jnp.where(mine[q] == 3, 2, 1))
        long2 = jnp.where(mine[q] == 0, 4, jnp.where(mine[q] == 3, 2, 3))
        s1.append(jnp.where(longer, long1, jnp.where(leads, 0, 1)))
        s2.append(jnp.where(longer, long2, jnp.where(leads, 2, 1)))
    zero = first == 0
    sched[0] = first
    sched[1] = 1 - first
    sched[2] = jnp.where(zero, s1[0], s1[1])
    sched[3] = jnp.where(zero, s1[1], s1[0])
    sched[4] = jnp.where(zero, s2[1], s2[0])
    sched[5] = jnp.where(zero, s2[0], s2[1])
    sched[6] = jnp.where(longer, 1, 0)
    mixed[0] = jnp.where((order[0] ^ 3) == order[1], 1, 0)
    lead[0] = order[0] >> 1


def slot(sched, t):
    q = sched[0] if t in (0, 3) else sched[1]
    return q, sched[2 + t]


def last_color(sched, phase):
    last = jnp.int32(-1)
    for t in range(4):
        q, at = slot(sched, t)
        last = jnp.where(at == phase, q, last)
    return last


def first_kernel(
    order_hbm, coupling, inverse, source_hbm,
    w, winv, source, sched, mixed, side, u, e, terms, leaves, outer, to_a, to_b,
    order, plain, rhs, sums, acc, sems,
):
    get_order = pltpu.make_async_copy(order_hbm, order, sems.at[0])
    get_source = pltpu.make_async_copy(source_hbm, source, sems.at[1])
    get_inverse = pltpu.make_async_copy(inverse, winv, sems.at[2])

    def get(m):
        return pltpu.make_async_copy(coupling.at[m], w.at[m], sems.at[3 + m])

    def wait_for(first, end):
        def wait(m, _):
            get(m).wait()
            return 0

        lax.fori_loop(first, end, wait, 0)

    for copy in (get_order, get_inverse, get_source):
        copy.start()
    for ref in (terms, leaves, u, outer):
        ref[...] = jnp.zeros(ref.shape, F32)
    e[...] = jnp.zeros(e.shape, BF16)
    get_order.wait()
    write_schedule(order, sched, mixed, side)
    first, last = sched[0], last_color(sched, 0)
    both = (last >= 0) & (last != first)

    def start(m, _):
        get(m ^ jnp.where(both, 4, 0)).start()
        return 0

    lax.fori_loop(0, 8, start, 0)
    get_source.wait()
    get_inverse.wait()

    @pl.when(last >= 0)
    def _():
        plain_update(first, jnp.zeros((ROWS, LANES), F32), source, winv, u, e, plain.at[0], rhs, sums)

    @pl.when(both)
    def _():
        down, up = plain_sums(2, w, plain.at[0], acc, get)
        terms[first] = below_and_above(first, down, up, (0,))
        plain_update(last, terms[first], source, winv, u, e, plain.at[1], rhs, sums)

    @pl.when(last >= 0)
    def _():
        plain_x_terms(first, w, plain.at[0], terms, leaves, acc, get)

    @pl.when(both)
    def _():
        plain_x_terms(last, w, plain.at[1], terms, leaves, acc)

    write_messages(leaves, to_a, to_b)

    @pl.when(last < 0)
    def _():
        rearrange(winv, 0)
        wait_for(0, 4)
        rearrange_x(w)

    @pl.when(jnp.logical_not(both))
    def _():
        wait_for(4, 8)


def first_beside_kernel(sched, e, w_in, winv_in, terms_in, w, winv, terms, acc):
    del w_in, winv_in, terms_in
    last = last_color(sched, 0)
    rearrange_y(w)

    @pl.when(last >= 0)
    def _():
        rearrange(winv, 0)
        rearrange_x(w)
        local_terms(last, w, e, terms, acc)


def phase_kernel(
    phase, n, sides, sched, *refs
):
    from_b, refs = [(k, ref) for k, ref in zip(sides, refs)], refs[len(sides) :]
    from_a, source, w, winv = refs[:4]
    u, e, terms, leaves, outer, to_a, to_b, known, dirty, rhs, sums, acc = refs[9:]
    write_outer(n, from_a, from_b, outer)
    last = last_color(sched, phase)

    @pl.when(last >= 0)
    def _():
        known[...] = source[...] - outer[...]
        dirty[0] = -1

        def step(t, several):
            q = jnp.where((t == 0) | (t == 3), sched[0], sched[1])
            before = dirty[0]
            active = sched[2 + t] == phase

            @pl.when(active & (before >= 0))
            def _():
                local_terms(before, w, e, terms, acc)

            @pl.when(active)
            def _():
                update(q, terms[0] + terms[1], known, winv, u, e, rhs, sums)
                dirty[0] = q

            return several | (active & (before >= 0) & (before != q))

        several = lax.fori_loop(0, 4, step, False)

        @pl.when(several)
        def _():
            all_leave_terms(w, e, leaves, acc)

        @pl.when(jnp.logical_not(several))
        def _():
            leave_terms(last, w, e, leaves, acc)

    write_messages(leaves, to_a, to_b)


def beside_kernel(phase, sched, w, e, terms_in, terms, acc):
    del terms_in
    last = last_color(sched, phase)

    @pl.when(last >= 0)
    def _():
        local_terms(last, w, e, terms, acc)


def last_beside_kernel(phase, sched, w, e, u, terms_in, terms, adjoint, local, longer, acc):
    beside_kernel(phase, sched, w, e, terms_in, terms, acc)
    local[...] = terms[0] + terms[1]
    longer[0] = sched[6]
    even = ((lane((2, LANES)) >> 3) & 1) == 0
    for i in range(HALF):
        u0, u1 = u[0, i, 0:2, :], u[1, i, 0:2, :]
        adjoint[2 * i : 2 * i + 2, :] = jnp.where(even, u0, shift(u1, -TILE))
        adjoint[ROWS // 2 + 2 * i : ROWS // 2 + 2 * i + 2, :] = jnp.where(even, shift(u0, -TILE), u1)


def final_kernel(n, sides, *refs):
    from_b = [(k, ref) for k, ref in zip(sides, refs)]
    from_a, local, outer_in, off, outer = refs[len(sides) :]
    outer[...] = outer_in[...]
    write_outer(n, from_a, from_b, outer)
    off[...] = local[...] + outer[...]


def cost(products):
    return pl.CostEstimate(flops=products, bytes_accessed=products // 2, transcendentals=0)


def spec(space):
    return pl.BlockSpec(memory_space=space)


def specs(text):
    return [spec({"v": VMEM, "s": SMEM, "h": pl.ANY}[c]) for c in text]


def pinned(x, space=VMEM):
    return pltpu.with_memory_space_constraint(x, space)


def params(mib):
    return pltpu.CompilerParams(vmem_limit_bytes=mib * 2**20)


def body(n, groups, coupling, inverse, source, order):
    coupling = pinned(coupling.reshape(8, HALF * ROWS, LANES), pltpu.HBM)
    inverse = pinned(inverse.reshape(2, HALF * ROWS, LANES), pltpu.HBM)
    source = pinned(source.reshape(ROWS, LANES), pltpu.HBM)
    w_shape, winv_shape = VMEM(coupling.shape, BF16), VMEM(inverse.shape, BF16)
    message, field, two = VMEM((MROWS, LANES), F32), VMEM((ROWS, LANES), F32), VMEM((2, ROWS, LANES), F32)
    u_shape, e_shape = VMEM((2, HALF, 8, LANES), F32), VMEM((2, PAIRS, 3, 16, LANES), BF16)
    rhs, sums, acc = VMEM((PAIR, LANES), BF16), VMEM((BLK, 8, LANES), F32), VMEM((4, PAIR, LANES), F32)
    flags, flag = SMEM((8,), jnp.int32), SMEM((1,), jnp.int32)

    w, winv, source, sched, mixed, side, *state = pl.pallas_call(
        first_kernel,
        out_shape=(
            w_shape, winv_shape, field, flags, flag, flag, u_shape, e_shape, two, field, field, message, message,
        ),
        in_specs=specs("hhhh"),
        out_specs=specs("vvvsssvvvvvvv"),
        scratch_shapes=[
            SMEM((4,), jnp.int32), VMEM((2, *e_shape.shape), BF16), rhs, sums, acc, pltpu.SemaphoreType.DMA((11,)),
        ],
        compiler_params=params(8),
        cost_estimate=cost(40_000_000),
        name="first",
    )(pinned(order, pltpu.HBM), coupling, inverse, source)

    axes = ("groups", "gx")

    def in_groups(to):
        return [(g * n + i, g * n + j) for g in range(groups) for i, j in to.items()]

    swap = in_groups({i: i ^ 1 for i in range(n)})

    def side_pairs(k):
        to = {i: i + 1 if i & 1 else i - 1 for i in range(3, n - 3)}
        to |= {0: 1, 1: 2, 2: 0} if k else {0: 2, 2: 1, 1: 0}
        to |= {n - 3: n - 2, n - 2: n - 1, n - 1: n - 3} if k else {n - 2: n - 3, n - 3: n - 1, n - 1: n - 2}
        return in_groups(to)

    def exchange(sides, to_a, to_b):
        from_b = [lax.ppermute(to_b, axes, side_pairs(k)) for k in sides]
        return [*from_b, lax.ppermute(to_a, axes, swap)]

    def rest(turns, w, winv, source, sched, u, e, terms, leaves, outer, to_a, to_b):
        source, sched = pinned(source), pinned(sched, SMEM)

        def run_phase(phase, sides, received, u, e, terms, leaves, outer):
            inputs = [*received, source, w, winv, u, e, terms, leaves, outer]
            at = 1 + len(inputs) - 5
            return pl.pallas_call(
                functools.partial(phase_kernel, phase, n, sides),
                out_shape=(u_shape, e_shape, two, field, field, message, message),
                in_specs=specs("s" + "v" * len(inputs)),
                out_specs=specs("vvvvvvv"),
                scratch_shapes=[field, flag, rhs, sums, acc],
                input_output_aliases={at + i: i for i in range(5)},
                compiler_params=params(4),
                cost_estimate=cost(20_000_000),
                name="phase",
            )(sched, *[pinned(x) for x in inputs])

        def beside(phase, e, terms):
            return pl.pallas_call(
                functools.partial(beside_kernel, phase),
                out_shape=two,
                in_specs=specs("svvv"),
                out_specs=spec(VMEM),
                scratch_shapes=[acc],
                input_output_aliases={3: 0},
                compiler_params=params(4),
                cost_estimate=cost(4_000_000),
                name="beside",
            )(sched, w, pinned(e), pinned(terms))

        def last_beside(phase, u, e, terms):
            return pl.pallas_call(
                functools.partial(last_beside_kernel, phase),
                out_shape=(two, jax.ShapeDtypeStruct((ROWS, LANES), F32), field, flag),
                in_specs=specs("svvvv"),
                out_specs=specs("vvvs"),
                scratch_shapes=[acc],
                input_output_aliases={4: 0},
                compiler_params=params(4),
                cost_estimate=cost(4_000_000),
                name="last_beside",
            )(sched, w, pinned(e), pinned(u), pinned(terms))

        def final(sides, received, local, outer):
            inputs = [*received, local, outer]
            return pl.pallas_call(
                functools.partial(final_kernel, n, sides),
                out_shape=jax.ShapeDtypeStruct((ROWS, LANES), F32),
                in_specs=specs("v" * len(inputs)),
                out_specs=spec(VMEM),
                scratch_shapes=[field],
                compiler_params=params(4),
                cost_estimate=cost(100_000),
                name="final",
            )(*[pinned(x) for x in inputs])

        received = exchange(turns[0], to_a, to_b)
        w, winv, terms = pl.pallas_call(
            first_beside_kernel,
            out_shape=(w_shape, winv_shape, two),
            in_specs=specs("svvvv"),
            out_specs=specs("vvv"),
            scratch_shapes=[acc],
            input_output_aliases={2: 0, 3: 1, 4: 2},
            compiler_params=params(4),
            cost_estimate=cost(8_000_000),
            name="first_beside",
        )(sched, pinned(e), pinned(w), pinned(winv), pinned(terms))
        w, winv = pinned(w), pinned(winv)

        def two_phases(phase, received, u, e, terms, leaves, outer):
            for i in (phase, phase + 1):
                u, e, terms, leaves, outer, to_a, to_b = run_phase(i, turns[i - 1], received, u, e, terms, leaves, outer)
                received = exchange(turns[i], to_a, to_b)
                if i == phase:
                    terms = beside(i, e, terms)
            terms, adjoint, local, longer = last_beside(i, u, e, terms)
            return longer, adjoint, received, local, (u, e, terms, leaves, outer)

        longer, adjoint, received, local, state = two_phases(1, received, u, e, terms, leaves, outer)

        def more(adjoint, received, local, *state):
            _, adjoint, received, local, state = two_phases(3, received, *state)
            return adjoint, final(turns[4], received, local, state[-1])

        def no_more(adjoint, received, local, *state):
            return adjoint, final(turns[2], received, local, state[-1])

        if len(turns) < 5:
            return no_more(adjoint, received, local, *state)
        return lax.cond(longer[0] > 0, more, no_more, adjoint, received, local, *state)

    def from_side(k):
        return functools.partial(rest, [(k,) if i % 2 == 0 else (1 - k,) for i in range(5)])

    def one_side(*state):
        return lax.cond(side[0] > 0, from_side(1), from_side(0), *state)

    both_sides = functools.partial(rest, [(0, 1)] * 3)
    adjoint, off = lax.cond(mixed[0] > 0, both_sides, one_side, w, winv, source, sched, *state)
    return adjoint.reshape(BLK, 2, LANES), off.reshape(BLK, 2, LANES)


def solution(mesh):
    call = functools.partial(body, mesh.shape["gx"], mesh.shape["groups"])
    return jax.shard_map(
        call,
        mesh=mesh,
        in_specs=(
            P("groups", None, None, "gx", None),
            P("groups", None, "gx", None),
            P("groups", "gx", None),
            P("groups"),
        ),
        out_specs=(P("groups", "gx", None), P("groups", "gx", None)),
        check_vma=False,
    )
```

```python
import functools

import jax
import jax.numpy as jnp
from jax import lax
from jax.experimental import pallas as pl
from jax.experimental.pallas import tpu as pltpu
from jax.sharding import PartitionSpec as P

BLK = 60
HALF = BLK // 2
ROWS = 2 * BLK
PAIR = 2 * ROWS
PAIRS = HALF // 2
TILE = 8
LANES = 128
MROWS = 64
F32, BF16 = jnp.float32, jnp.bfloat16
VMEM, SMEM = pltpu.VMEM, pltpu.SMEM
LEAVES, STAYS, DOWN, UP = range(4)


def lane(shape):
    return lax.broadcasted_iota(jnp.int32, shape, len(shape) - 1)


def even_row(shape):
    return (lax.broadcasted_iota(jnp.int32, shape, len(shape) - 2) & 1) == 0


def own_lanes(q):
    return ((lane((ROWS, LANES)) >> 3) & 1) == q


def shift(x, by):
    return pltpu.roll(x, by % LANES, len(x.shape) - 1)


def swapped_rows(x):
    x = x.reshape(ROWS // 8, 8, LANES)
    return jnp.where(even_row(x.shape), pltpu.roll(x, 7, 1), pltpu.roll(x, 1, 1)).reshape(ROWS, LANES)


def by_color(first, second):
    even = (lax.broadcasted_iota(jnp.int16, first.shape, 1) & TILE) == 0
    moved = shift(jnp.where(even, second, first), TILE)
    return jnp.where(even, first, moved), jnp.where(even, moved, second)


def rearrange(ref, m):
    chunk = 1200

    def step(k, _):
        rows = pl.ds(pl.multiple_of(k * chunk, chunk), chunk)
        ref[2 * m, rows, :], ref[2 * m + 1, rows, :] = by_color(ref[2 * m, rows, :], ref[2 * m + 1, rows, :])
        return 0

    lax.fori_loop(0, HALF * ROWS // chunk, step, 0)


def rearrange_x(w):
    chunk = 720

    def step(k, _):
        rows = pl.ds(pl.multiple_of(k * chunk, chunk), chunk)
        even = (lax.broadcasted_iota(jnp.int16, (chunk, LANES), 0) & 1) == 0
        left, right = [w[h, rows, :] for h in (0, 1)], [w[2 + h, rows, :] for h in (0, 1)]
        leaves = [jnp.where(even, left[h], right[h]) for h in (0, 1)]
        stays = [jnp.where(even, right[h], left[h]) for h in (0, 1)]
        w[2 * LEAVES, rows, :], w[2 * LEAVES + 1, rows, :] = by_color(*leaves)
        w[2 * STAYS, rows, :], w[2 * STAYS + 1, rows, :] = by_color(*stays)
        return 0

    lax.fori_loop(0, HALF * ROWS // chunk, step, 0)


def rearrange_y(w):
    def face(f, _):
        rearrange(w, f)
        return 0

    lax.fori_loop(DOWN, UP + 1, face, 0)


def half_sum(w, m, tiles, acc, at, add=False):
    for first, end, tile in ((0, 4, 0), (4, 7, 0), (7, 8, 1), (8, 12, 2), (12, 15, 2)):
        total = None
        for k in range(PAIRS):
            block = w[m, pl.ds(k * PAIR + 16 * first, 16 * (end - first)), :].reshape(end - first, 16, LANES)
            prod = block.astype(F32) * tiles[k, tile][None].astype(F32)
            total = prod if total is None else total + prod
        rows = pl.ds(16 * first, 16 * (end - first))
        total = total.reshape(16 * (end - first), LANES)
        acc[at, rows, :] = acc[at, rows, :] + total if add else total


def both_rows(acc, at):
    return acc[at, 0:ROWS, :] + acc[at, ROWS:, :]


def spread(half):
    return half + shift(half, -TILE)


def below_and_above(q, down, up, moves):
    at = lane((ROWS, LANES))
    down_to = (((at + 1) >> 3) & 1 == q) & (at < LANES - 1)
    up_to = (((at - 1) >> 3) & 1 == q) & (at > 0)
    down, up = sum(shift(down, -1 - by) for by in moves), sum(shift(up, 1 - by) for by in moves)
    return jnp.where(down_to, down, 0.0) + jnp.where(up_to, up, 0.0)


def local_terms(q, w, e, terms, acc):
    for kind in (DOWN, UP, STAYS):
        half_sum(w, 2 * kind + q, e.at[q], acc, kind)
    y = below_and_above(q, both_rows(acc, DOWN), both_rows(acc, UP), (0, TILE))
    stays = jnp.where(own_lanes(q), spread(both_rows(acc, STAYS)), 0.0)
    terms[q] = y + swapped_rows(stays)


def leave_terms(q, w, e, leaves, acc):
    half_sum(w, 2 * LEAVES + q, e.at[q], acc, LEAVES)
    leaves[...] = jnp.where(own_lanes(q), spread(both_rows(acc, LEAVES)), leaves[...])


def all_leave_terms(w, e, leaves, acc):
    for q in (0, 1):
        half_sum(w, 2 * LEAVES + q, e.at[q], acc, q)
    leaves[...] = jnp.where(own_lanes(0), spread(both_rows(acc, 0)), spread(both_rows(acc, 1)))


def plain_sums(faces, colors, w, plain, acc, get):
    acc[...] = jnp.zeros(acc.shape, F32)

    def half(t, _):
        get(2 * faces + t).wait()
        half_sum(w, 2 * faces + t, plain.at[0, t & 1], acc, t >> 1, add=True)

        @pl.when(colors == 2)
        def _():
            half_sum(w, 2 * faces + t, plain.at[1, t & 1], acc, 2 + (t >> 1), add=True)

        return 0

    lax.fori_loop(0, 4, half, 0)


def plain_x_terms(c, q, acc, terms, leaves):
    left, right = both_rows(acc, 2 * c), both_rows(acc, 2 * c + 1)
    own, even = own_lanes(q), even_row((ROWS, LANES))
    leaves[...] = jnp.where(own, jnp.where(even, left, right), leaves[...])
    terms[q] = terms[q] + swapped_rows(jnp.where(own, jnp.where(even, right, left), 0.0))


def row_sums(winv, m, rhs, sums, at):
    for k in range(PAIRS):
        prod = winv[m, pl.ds(k * PAIR, PAIR), :].astype(F32) * rhs[...].astype(F32)
        sums[at + 2 * k] = jnp.sum(prod[:ROWS].reshape(ROWS // 8, 8, LANES), axis=0)
        sums[at + 2 * k + 1] = jnp.sum(prod[ROWS:].reshape(ROWS // 8, 8, LANES), axis=0)


def totals(sums):
    total = sums + pltpu.roll(sums, 4, 1)
    return total + pltpu.roll(total, 2, 1)


def write_tiles(total, e):
    for k in range(PAIRS):
        first, second = total[2 * k], total[2 * k + 1]
        e[k, 0] = jnp.concatenate([first, first], axis=0).astype(BF16)
        e[k, 1] = jnp.concatenate([first, second], axis=0).astype(BF16)
        e[k, 2] = jnp.concatenate([second, second], axis=0).astype(BF16)


def write_rhs(value, rhs):
    rhs[...] = jnp.concatenate([value, value], axis=0).astype(BF16)


def update(q, incoming, source, winv, u, e, rhs, sums):
    value = (source[...] - incoming).astype(BF16).astype(F32)
    write_rhs(jnp.where(own_lanes(q), value, shift(value, TILE)), rhs)
    row_sums(winv, q, rhs, sums, 0)
    total = totals(sums[0:HALF])
    write_tiles(total, e.at[q])
    u[q] = total


def plain_update(q, incoming, source, winv, u, e, plain, rhs, sums):
    write_rhs(source[...] - incoming, rhs)

    def half(h, _):
        row_sums(winv, h, rhs, sums, HALF * h)
        return 0

    lax.fori_loop(0, 2, half, 0)
    both = [totals(sums[0:HALF]), totals(sums[HALF:])]
    for h in (0, 1):
        write_tiles(both[h], plain.at[h])
    zero = q == 0
    own = ((lane((HALF, 8, LANES)) >> 3) & 1) == q
    mine, other = jnp.where(zero, both[0], both[1]), jnp.where(zero, both[1], both[0])
    total = jnp.where(own, mine, shift(other, TILE))
    write_tiles(total, e.at[q])
    u[q] = total


def write_messages(leaves, to_a, to_b):
    odd = (lax.axis_index("gx") & 1) == 1
    to_left = leaves[pl.ds(0, BLK, stride=2), :]
    to_right = leaves[pl.ds(1, BLK, stride=2), :]
    to_a[0:BLK, :] = jnp.where(odd, to_left, to_right)
    to_b[0:BLK, :] = jnp.where(odd, to_right, to_left)
    to_a[BLK:, :] = jnp.zeros((MROWS - BLK, LANES), F32)
    to_b[BLK:, :] = jnp.zeros((MROWS - BLK, LANES), F32)


def write_outer(n, k, from_b, from_a, outer):
    me = lax.axis_index("gx")
    odd = me & 1
    outer[pl.ds(1 - odd, BLK, stride=2), :] = from_a[0:BLK, :]
    new = (me > 0) & (me < n - 1)

    @pl.when(new if k is None else new & (odd == 1 - k))
    def _():
        outer[pl.ds(odd, BLK, stride=2), :] = from_b[0:BLK, :]


def write_schedule(order, sched, lead):
    parity = lax.axis_index("gx") & 1
    place = []
    for side in (parity, 1 - parity):
        for q in (0, 1):
            c = 2 * side + q
            at = jnp.int32(0)
            for i in range(1, 4):
                at = jnp.where(order[i] == c, i, at)
            place.append(at)
    mine, theirs = place[:2], place[2:]
    first = jnp.where(mine[0] < mine[1], 0, 1)
    longer = ((order[0] ^ 2) == order[1]) & ((order[0] ^ 3) == order[2])
    s1, s2 = [], []
    for q in (0, 1):
        leads = mine[q] < theirs[q]
        long1 = jnp.where(mine[q] == 0, 0, jnp.where(mine[q] == 3, 2, 1))
        long2 = jnp.where(mine[q] == 0, 4, jnp.where(mine[q] == 3, 2, 3))
        s1.append(jnp.where(longer, long1, jnp.where(leads, 0, 1)))
        s2.append(jnp.where(longer, long2, jnp.where(leads, 2, 1)))
    zero = first == 0
    sched[0] = first
    sched[1] = 1 - first
    sched[2] = jnp.where(zero, s1[0], s1[1])
    sched[3] = jnp.where(zero, s1[1], s1[0])
    sched[4] = jnp.where(zero, s2[1], s2[0])
    sched[5] = jnp.where(zero, s2[0], s2[1])
    sched[6] = jnp.where(longer, 1, 0)
    sched[7] = jnp.where(longer | ((order[0] ^ 3) == order[1]), 0, 1)
    lead[0] = order[0] >> 1


def slot(sched, t):
    q = sched[0] if t in (0, 3) else sched[1]
    return q, sched[2 + t]


def last_color(sched, phase):
    last = jnp.int32(-1)
    for t in range(4):
        q, at = slot(sched, t)
        last = jnp.where(at == phase, q, last)
    return last


def first_kernel(
    order_hbm, coupling, inverse, source_hbm,
    w, winv, source, sched, side, u, e, terms, leaves, outer, to_a, to_b,
    order, plain, rhs, sums, acc, sems,
):
    get_order = pltpu.make_async_copy(order_hbm, order, sems.at[0])
    get_source = pltpu.make_async_copy(source_hbm, source, sems.at[1])
    get_inverse = pltpu.make_async_copy(inverse, winv, sems.at[2])

    def get(m):
        return pltpu.make_async_copy(coupling.at[m], w.at[m], sems.at[3 + m])

    def wait_for(first, end):
        def wait(m, _):
            get(m).wait()
            return 0

        lax.fori_loop(first, end, wait, 0)

    for copy in (get_order, get_inverse, get_source):
        copy.start()
    for ref in (terms, leaves, u, outer):
        ref[...] = jnp.zeros(ref.shape, F32)
    e[...] = jnp.zeros(e.shape, BF16)
    get_order.wait()
    write_schedule(order, sched, side)
    first, last = sched[0], last_color(sched, 0)
    any_step, one_sided = last >= 0, sched[7] == 1
    both = any_step & (last != first)

    def start(m, _):
        get(jnp.where(one_sided, m ^ 4, m)).start()
        return 0

    lax.fori_loop(0, jnp.where(one_sided, 8, 4), start, 0)
    get_source.wait()
    get_inverse.wait()

    @pl.when(any_step)
    def _():
        plain_update(first, jnp.zeros((ROWS, LANES), F32), source, winv, u, e, plain.at[0], rhs, sums)

    @pl.when(both)
    def _():
        plain_sums(2, 1, w, plain, acc, get)
        terms[first] = below_and_above(first, both_rows(acc, 0), both_rows(acc, 1), (0,))
        plain_update(last, terms[first], source, winv, u, e, plain.at[1], rhs, sums)

    @pl.when(any_step)
    def _():
        plain_sums(0, jnp.where(both, 2, 1), w, plain, acc, get)
        plain_x_terms(0, first, acc, terms, leaves)

    @pl.when(both)
    def _():
        plain_x_terms(1, last, acc, terms, leaves)

    write_messages(leaves, to_a, to_b)

    @pl.when(jnp.logical_not(any_step))
    def _():
        rearrange(winv, 0)

        @pl.when(one_sided)
        def _():
            wait_for(4, 8)
            rearrange_y(w)

        wait_for(0, 4)


def first_beside_kernel(sched, coupling, e, w_in, winv_in, terms_in, w, winv, terms, acc, sems):
    del w_in, winv_in, terms_in
    last, one_sided = last_color(sched, 0), sched[7] == 1

    def get(m):
        return pltpu.make_async_copy(coupling.at[m], w.at[m], sems.at[m - 4])

    @pl.when(jnp.logical_not(one_sided))
    def _():
        for m in range(4, 8):
            get(m).start()

    @pl.when(last >= 0)
    def _():
        rearrange(winv, 0)

    rearrange_x(w)

    @pl.when(jnp.logical_not(one_sided))
    def _():
        for m in range(4, 8):
            get(m).wait()

    @pl.when(jnp.logical_not(one_sided) | (last >= 0))
    def _():
        rearrange_y(w)

    @pl.when(last >= 0)
    def _():
        local_terms(last, w, e, terms, acc)


def phase_kernel(
    phase, n, k, sched, from_b, from_a, source, w, winv, u_in, e_in, terms_in, leaves_in, outer_in,
    u, e, terms, leaves, outer, to_a, to_b, known, dirty, rhs, sums, acc,
):
    del u_in, e_in, terms_in, leaves_in, outer_in
    write_outer(n, k, from_b, from_a, outer)
    last = last_color(sched, phase)

    @pl.when(last >= 0)
    def _():
        known[...] = source[...] - outer[...]
        dirty[0] = -1

        def step(t, several):
            q = jnp.where((t == 0) | (t == 3), sched[0], sched[1])
            before = dirty[0]
            active = sched[2 + t] == phase

            @pl.when(active & (before >= 0))
            def _():
                local_terms(before, w, e, terms, acc)

            @pl.when(active)
            def _():
                update(q, terms[0] + terms[1], known, winv, u, e, rhs, sums)
                dirty[0] = q

            return several | (active & (before >= 0) & (before != q))

        several = lax.fori_loop(0, 4, step, False)

        @pl.when(several)
        def _():
            all_leave_terms(w, e, leaves, acc)

        @pl.when(jnp.logical_not(several))
        def _():
            leave_terms(last, w, e, leaves, acc)

    write_messages(leaves, to_a, to_b)


def beside_kernel(phase, sched, w, e, terms_in, terms, acc):
    del terms_in
    last = last_color(sched, phase)

    @pl.when(last >= 0)
    def _():
        local_terms(last, w, e, terms, acc)


def last_beside_kernel(phase, sched, w, e, u, terms_in, terms, adjoint, local, longer, acc):
    beside_kernel(phase, sched, w, e, terms_in, terms, acc)
    local[...] = terms[0] + terms[1]
    longer[0] = sched[6]
    even = ((lane((2, LANES)) >> 3) & 1) == 0
    for i in range(HALF):
        u0, u1 = u[0, i, 0:2, :], u[1, i, 0:2, :]
        adjoint[2 * i : 2 * i + 2, :] = jnp.where(even, u0, shift(u1, -TILE))
        adjoint[ROWS // 2 + 2 * i : ROWS // 2 + 2 * i + 2, :] = jnp.where(even, shift(u0, -TILE), u1)


def final_kernel(n, k, from_b, from_a, local, outer_in, off, outer):
    outer[...] = outer_in[...]
    write_outer(n, k, from_b, from_a, outer)
    off[...] = local[...] + outer[...]


def cost(products):
    return pl.CostEstimate(flops=products, bytes_accessed=products // 2, transcendentals=0)


def spec(space):
    return pl.BlockSpec(memory_space=space)


def specs(text):
    return [spec({"v": VMEM, "s": SMEM, "h": pl.ANY}[c]) for c in text]


def pinned(x, space=VMEM):
    return pltpu.with_memory_space_constraint(x, space)


def params(mib):
    return pltpu.CompilerParams(vmem_limit_bytes=mib * 2**20)


def body(n, groups, coupling, inverse, source, order):
    coupling = pinned(coupling.reshape(8, HALF * ROWS, LANES), pltpu.HBM)
    inverse = pinned(inverse.reshape(2, HALF * ROWS, LANES), pltpu.HBM)
    source = pinned(source.reshape(ROWS, LANES), pltpu.HBM)
    w_shape, winv_shape = VMEM(coupling.shape, BF16), VMEM(inverse.shape, BF16)
    message, field, two = VMEM((MROWS, LANES), F32), VMEM((ROWS, LANES), F32), VMEM((2, ROWS, LANES), F32)
    u_shape, e_shape = VMEM((2, HALF, 8, LANES), F32), VMEM((2, PAIRS, 3, 16, LANES), BF16)
    rhs, sums, acc = VMEM((PAIR, LANES), BF16), VMEM((BLK, 8, LANES), F32), VMEM((4, PAIR, LANES), F32)
    flags, flag = SMEM((8,), jnp.int32), SMEM((1,), jnp.int32)

    w, winv, source, sched, side, u, e, terms, leaves, outer, to_a, to_b = pl.pallas_call(
        first_kernel,
        out_shape=(
            w_shape, winv_shape, field, flags, flag, u_shape, e_shape, two, field, field, message, message,
        ),
        in_specs=specs("hhhh"),
        out_specs=specs("vvvssvvvvvvv"),
        scratch_shapes=[
            SMEM((4,), jnp.int32), VMEM((2, *e_shape.shape), BF16), rhs, sums, acc, pltpu.SemaphoreType.DMA((11,)),
        ],
        compiler_params=params(8),
        cost_estimate=cost(40_000_000),
        name="first",
    )(pinned(order, pltpu.HBM), coupling, inverse, source)

    source, sched = pinned(source), pinned(sched, SMEM)

    axes = ("groups", "gx")

    def in_groups(to):
        return [(g * n + i, g * n + j) for g in range(groups) for i, j in to.items()]

    swap = in_groups({i: i ^ 1 for i in range(n)})
    inside = {i: i + 1 if i & 1 else i - 1 for i in range(1, n - 1)}
    far_swap = in_groups(inside)
    far_swap += [(g * n + i, (g ^ 1) * n + i) for g in range(groups) for i in (0, n - 1) if (g ^ 1) < groups]

    def side_pairs(k):
        to = inside | ({0: 1, 1: 2, 2: 0} if k else {0: 2, 2: 1, 1: 0})
        to |= {n - 3: n - 2, n - 2: n - 1, n - 1: n - 3} if k else {n - 2: n - 3, n - 3: n - 1, n - 1: n - 2}
        return in_groups(to)

    def exchange(k, to_a, to_b):
        from_b = lax.ppermute(to_b, axes, far_swap if k is None else side_pairs(k))
        return from_b, lax.ppermute(to_a, axes, swap)

    def run_phase(phase, k, received, u, e, terms, leaves, outer):
        inputs = [*received, source, w, winv, u, e, terms, leaves, outer]
        return pl.pallas_call(
            functools.partial(phase_kernel, phase, n, k),
            out_shape=(u_shape, e_shape, two, field, field, message, message),
            in_specs=specs("s" + "v" * len(inputs)),
            out_specs=specs("vvvvvvv"),
            scratch_shapes=[field, flag, rhs, sums, acc],
            input_output_aliases={6 + i: i for i in range(5)},
            compiler_params=params(4),
            cost_estimate=cost(20_000_000),
            name="phase",
        )(sched, *[pinned(x) for x in inputs])

    def beside(phase, e, terms):
        return pl.pallas_call(
            functools.partial(beside_kernel, phase),
            out_shape=two,
            in_specs=specs("svvv"),
            out_specs=spec(VMEM),
            scratch_shapes=[acc],
            input_output_aliases={3: 0},
            compiler_params=params(4),
            cost_estimate=cost(4_000_000),
            name="beside",
        )(sched, w, pinned(e), pinned(terms))

    def last_beside(phase, u, e, terms):
        return pl.pallas_call(
            functools.partial(last_beside_kernel, phase),
            out_shape=(two, jax.ShapeDtypeStruct((ROWS, LANES), F32), field, flag),
            in_specs=specs("svvvv"),
            out_specs=specs("vvvs"),
            scratch_shapes=[acc],
            input_output_aliases={4: 0},
            compiler_params=params(4),
            cost_estimate=cost(4_000_000),
            name="last_beside",
        )(sched, w, pinned(e), pinned(u), pinned(terms))

    def final(k, received, local, outer):
        return pl.pallas_call(
            functools.partial(final_kernel, n, k),
            out_shape=jax.ShapeDtypeStruct((ROWS, LANES), F32),
            in_specs=specs("vvvv"),
            out_specs=spec(VMEM),
            scratch_shapes=[field],
            compiler_params=params(4),
            cost_estimate=cost(100_000),
            name="final",
        )(*[pinned(x) for x in (*received, local, outer)])

    received = exchange(None, to_a, to_b)
    w, winv, terms = pl.pallas_call(
        first_beside_kernel,
        out_shape=(w_shape, winv_shape, two),
        in_specs=specs("shvvvv"),
        out_specs=specs("vvv"),
        scratch_shapes=[acc, pltpu.SemaphoreType.DMA((4,))],
        input_output_aliases={3: 0, 4: 1, 5: 2},
        compiler_params=params(4),
        cost_estimate=cost(8_000_000),
        name="first_beside",
    )(sched, coupling, pinned(e), pinned(w), pinned(winv), pinned(terms))
    w, winv = pinned(w), pinned(winv)

    def two_phases(phase, turns, received, u, e, terms, leaves, outer):
        for i in (0, 1):
            u, e, terms, leaves, outer, to_a, to_b = run_phase(
                phase + i, turns[i], received, u, e, terms, leaves, outer
            )
            received = exchange(turns[i + 1], to_a, to_b)
            if i == 0:
                terms = beside(phase, e, terms)
        terms, adjoint, local, longer = last_beside(phase + 1, u, e, terms)
        return longer, adjoint, received, local, (u, e, terms, leaves, outer)

    longer, adjoint, received, local, state = two_phases(1, (None,) * 3, received, u, e, terms, leaves, outer)

    def more(side, adjoint, received, local, *state):
        def from_side(k):
            def run(received, *state):
                _, adjoint, received, local, state = two_phases(3, (None, 1 - k, k), received, *state)
                return adjoint, final(k, received, local, state[-1])

            return run

        return lax.cond(side[0] > 0, from_side(1), from_side(0), received, *state)

    def no_more(side, adjoint, received, local, *state):
        return adjoint, final(None, received, local, state[-1])

    adjoint, off = lax.cond(longer[0] > 0, more, no_more, side, adjoint, received, local, *state)
    return adjoint.reshape(BLK, 2, LANES), off.reshape(BLK, 2, LANES)


def solution(mesh):
    call = functools.partial(body, mesh.shape["gx"], mesh.shape["groups"])
    return jax.shard_map(
        call,
        mesh=mesh,
        in_specs=(
            P("groups", None, None, "gx", None),
            P("groups", None, "gx", None),
            P("groups", "gx", None),
            P("groups"),
        ),
        out_specs=(P("groups", "gx", None), P("groups", "gx", None)),
        check_vma=False,
    )
```

```python
import functools

import jax
import jax.numpy as jnp
from jax import lax
from jax.experimental import pallas as pl
from jax.experimental.pallas import tpu as pltpu
from jax.sharding import PartitionSpec as P

BLK = 60
HALF = BLK // 2
ROWS = 2 * BLK
PAIR = 2 * ROWS
PAIRS = HALF // 2
TILE = 8
LANES = 128
MROWS = 64
CHUNK = 720
F32, BF16 = jnp.float32, jnp.bfloat16
VMEM, SMEM = pltpu.VMEM, pltpu.SMEM
LEAVES, STAYS, DOWN, UP = range(4)


def lane(shape):
    return lax.broadcasted_iota(jnp.int32, shape, len(shape) - 1)


def even_row(shape):
    return (lax.broadcasted_iota(jnp.int32, shape, len(shape) - 2) & 1) == 0


def own_lanes(q):
    return ((lane((ROWS, LANES)) >> 3) & 1) == q


def shift(x, by):
    return pltpu.roll(x, by % LANES, len(x.shape) - 1)


def swapped_rows(x):
    x = x.reshape(ROWS // 8, 8, LANES)
    return jnp.where(even_row(x.shape), pltpu.roll(x, 7, 1), pltpu.roll(x, 1, 1)).reshape(ROWS, LANES)


def by_color(first, second):
    even = (lax.broadcasted_iota(jnp.int16, first.shape, 1) & TILE) == 0
    moved = shift(jnp.where(even, second, first), TILE)
    return jnp.where(even, first, moved), jnp.where(even, moved, second)


def rearrange(ref, m):
    for start in range(0, HALF * ROWS, CHUNK):
        rows = pl.ds(start, CHUNK)
        ref[2 * m, rows, :], ref[2 * m + 1, rows, :] = by_color(ref[2 * m, rows, :], ref[2 * m + 1, rows, :])


def rearrange_x(w):
    for start in range(0, HALF * ROWS, CHUNK):
        rows = pl.ds(start, CHUNK)
        even = (lax.broadcasted_iota(jnp.int16, (CHUNK, LANES), 0) & 1) == 0
        left, right = [w[h, rows, :] for h in (0, 1)], [w[2 + h, rows, :] for h in (0, 1)]
        leaves = [jnp.where(even, left[h], right[h]) for h in (0, 1)]
        stays = [jnp.where(even, right[h], left[h]) for h in (0, 1)]
        w[2 * LEAVES, rows, :], w[2 * LEAVES + 1, rows, :] = by_color(*leaves)
        w[2 * STAYS, rows, :], w[2 * STAYS + 1, rows, :] = by_color(*stays)


def rearrange_y(w):
    def face(f, _):
        rearrange(w, f)
        return 0

    lax.fori_loop(DOWN, UP + 1, face, 0)


def half_sum(w, m, tiles, acc, at, add=False):
    for first, end, tile in ((0, 4, 0), (4, 7, 0), (7, 8, 1), (8, 12, 2), (12, 15, 2)):
        total = None
        for k in range(PAIRS):
            block = w[m, pl.ds(k * PAIR + 16 * first, 16 * (end - first)), :].reshape(end - first, 16, LANES)
            prod = block.astype(F32) * tiles[k, tile][None].astype(F32)
            total = prod if total is None else total + prod
        rows = pl.ds(16 * first, 16 * (end - first))
        total = total.reshape(16 * (end - first), LANES)
        acc[at, rows, :] = acc[at, rows, :] + total if add else total


def both_rows(acc, at):
    return acc[at, 0:ROWS, :] + acc[at, ROWS:, :]


def spread(half):
    return half + shift(half, -TILE)


def below_and_above(q, down, up, moves):
    at = lane((ROWS, LANES))
    down_to = (((at + 1) >> 3) & 1 == q) & (at < LANES - 1)
    up_to = (((at - 1) >> 3) & 1 == q) & (at > 0)
    down, up = sum(shift(down, -1 - by) for by in moves), sum(shift(up, 1 - by) for by in moves)
    return jnp.where(down_to, down, 0.0) + jnp.where(up_to, up, 0.0)


def local_terms(q, w, e, terms, acc):
    for kind in (DOWN, UP, STAYS):
        half_sum(w, 2 * kind + q, e.at[q], acc, kind)
    y = below_and_above(q, both_rows(acc, DOWN), both_rows(acc, UP), (0, TILE))
    stays = jnp.where(own_lanes(q), spread(both_rows(acc, STAYS)), 0.0)
    terms[q] = y + swapped_rows(stays)


def leave_terms(q, w, e, leaves, acc):
    half_sum(w, 2 * LEAVES + q, e.at[q], acc, LEAVES)
    leaves[...] = jnp.where(own_lanes(q), spread(both_rows(acc, LEAVES)), leaves[...])


def all_leave_terms(w, e, leaves, acc):
    for q in (0, 1):
        half_sum(w, 2 * LEAVES + q, e.at[q], acc, q)
    leaves[...] = jnp.where(own_lanes(0), spread(both_rows(acc, 0)), spread(both_rows(acc, 1)))


def plain_sums(faces, colors, w, plain, acc, get):
    acc[...] = jnp.zeros(acc.shape, F32)

    def half(t, _):
        get(2 * faces + t).wait()
        half_sum(w, 2 * faces + t, plain.at[0, t & 1], acc, t >> 1, add=True)

        @pl.when(colors == 2)
        def _():
            half_sum(w, 2 * faces + t, plain.at[1, t & 1], acc, 2 + (t >> 1), add=True)

        return 0

    lax.fori_loop(0, 4, half, 0)


def plain_x_terms(c, q, acc, terms, leaves):
    left, right = both_rows(acc, 2 * c), both_rows(acc, 2 * c + 1)
    own, even = own_lanes(q), even_row((ROWS, LANES))
    leaves[...] = jnp.where(own, jnp.where(even, left, right), leaves[...])
    terms[q] = terms[q] + swapped_rows(jnp.where(own, jnp.where(even, right, left), 0.0))


def row_sums(winv, m, rhs, sums, at):
    for k in range(PAIRS):
        prod = winv[m, pl.ds(k * PAIR, PAIR), :].astype(F32) * rhs[...].astype(F32)
        sums[at + 2 * k] = jnp.sum(prod[:ROWS].reshape(ROWS // 8, 8, LANES), axis=0)
        sums[at + 2 * k + 1] = jnp.sum(prod[ROWS:].reshape(ROWS // 8, 8, LANES), axis=0)


def totals(sums):
    total = sums + pltpu.roll(sums, 4, 1)
    return total + pltpu.roll(total, 2, 1)


def write_tiles(total, e):
    for k in range(PAIRS):
        first, second = total[2 * k], total[2 * k + 1]
        e[k, 0] = jnp.concatenate([first, first], axis=0).astype(BF16)
        e[k, 1] = jnp.concatenate([first, second], axis=0).astype(BF16)
        e[k, 2] = jnp.concatenate([second, second], axis=0).astype(BF16)


def write_rhs(value, rhs):
    rhs[...] = jnp.concatenate([value, value], axis=0).astype(BF16)


def update(q, incoming, source, winv, u, e, rhs, sums):
    value = (source[...] - incoming).astype(BF16).astype(F32)
    write_rhs(jnp.where(own_lanes(q), value, shift(value, TILE)), rhs)
    row_sums(winv, q, rhs, sums, 0)
    total = totals(sums[0:HALF])
    write_tiles(total, e.at[q])
    u[q] = total


def plain_update(q, incoming, source, winv, u, e, plain, rhs, sums):
    write_rhs(source[...] - incoming, rhs)

    def half(h, _):
        row_sums(winv, h, rhs, sums, HALF * h)
        return 0

    lax.fori_loop(0, 2, half, 0)
    both = [totals(sums[0:HALF]), totals(sums[HALF:])]
    for h in (0, 1):
        write_tiles(both[h], plain.at[h])
    zero = q == 0
    own = ((lane((HALF, 8, LANES)) >> 3) & 1) == q
    mine, other = jnp.where(zero, both[0], both[1]), jnp.where(zero, both[1], both[0])
    total = jnp.where(own, mine, shift(other, TILE))
    write_tiles(total, e.at[q])
    u[q] = total


def write_messages(leaves, to_a, to_b):
    odd = (lax.axis_index("gx") & 1) == 1
    to_left = leaves[pl.ds(0, BLK, stride=2), :]
    to_right = leaves[pl.ds(1, BLK, stride=2), :]
    to_a[0:BLK, :] = jnp.where(odd, to_left, to_right)
    to_b[0:BLK, :] = jnp.where(odd, to_right, to_left)
    to_a[BLK:, :] = jnp.zeros((MROWS - BLK, LANES), F32)
    to_b[BLK:, :] = jnp.zeros((MROWS - BLK, LANES), F32)


def write_outer(n, k, from_b, from_a, outer):
    me = lax.axis_index("gx")
    odd = me & 1
    outer[pl.ds(1 - odd, BLK, stride=2), :] = from_a[0:BLK, :]
    new = (me > 0) & (me < n - 1)

    @pl.when(new if k is None else new & (odd == 1 - k))
    def _():
        outer[pl.ds(odd, BLK, stride=2), :] = from_b[0:BLK, :]


def write_schedule(order, sched, lead):
    parity = lax.axis_index("gx") & 1
    place = []
    for side in (parity, 1 - parity):
        for q in (0, 1):
            c = 2 * side + q
            at = jnp.int32(0)
            for i in range(1, 4):
                at = jnp.where(order[i] == c, i, at)
            place.append(at)
    mine, theirs = place[:2], place[2:]
    first = jnp.where(mine[0] < mine[1], 0, 1)
    longer = ((order[0] ^ 2) == order[1]) & ((order[0] ^ 3) == order[2])
    s1, s2 = [], []
    for q in (0, 1):
        leads = mine[q] < theirs[q]
        long1 = jnp.where(mine[q] == 0, 0, jnp.where(mine[q] == 3, 2, 1))
        long2 = jnp.where(mine[q] == 0, 4, jnp.where(mine[q] == 3, 2, 3))
        s1.append(jnp.where(longer, long1, jnp.where(leads, 0, 1)))
        s2.append(jnp.where(longer, long2, jnp.where(leads, 2, 1)))
    zero = first == 0
    sched[0] = first
    sched[1] = 1 - first
    sched[2] = jnp.where(zero, s1[0], s1[1])
    sched[3] = jnp.where(zero, s1[1], s1[0])
    sched[4] = jnp.where(zero, s2[1], s2[0])
    sched[5] = jnp.where(zero, s2[0], s2[1])
    sched[6] = jnp.where(longer, 1, 0)
    sched[7] = jnp.where(longer | ((order[0] ^ 3) == order[1]), 0, 1)
    lead[0] = order[0] >> 1


def slot(sched, t):
    q = sched[0] if t in (0, 3) else sched[1]
    return q, sched[2 + t]


def last_color(sched, phase):
    last = jnp.int32(-1)
    for t in range(4):
        q, at = slot(sched, t)
        last = jnp.where(at == phase, q, last)
    return last


def first_kernel(
    order_hbm, coupling, inverse, source_hbm,
    w, winv, source, sched, side, u, e, terms, leaves, outer, to_a, to_b,
    order, plain, rhs, sums, acc, sems,
):
    get_order = pltpu.make_async_copy(order_hbm, order, sems.at[0])
    get_source = pltpu.make_async_copy(source_hbm, source, sems.at[1])
    get_inverse = pltpu.make_async_copy(inverse, winv, sems.at[2])

    def get(m):
        return pltpu.make_async_copy(coupling.at[m], w.at[m], sems.at[3 + m])

    def wait_for(first, end):
        def wait(m, _):
            get(m).wait()
            return 0

        lax.fori_loop(first, end, wait, 0)

    for copy in (get_order, get_inverse, get_source):
        copy.start()
    for ref in (terms, leaves, u, outer):
        ref[...] = jnp.zeros(ref.shape, F32)
    e[...] = jnp.zeros(e.shape, BF16)
    get_order.wait()
    write_schedule(order, sched, side)
    first, last = sched[0], last_color(sched, 0)
    any_step, one_sided = last >= 0, sched[7] == 1
    both = any_step & (last != first)

    def start(m, _):
        get(jnp.where(one_sided, m ^ 4, m)).start()
        return 0

    lax.fori_loop(0, jnp.where(one_sided, 8, 4), start, 0)
    get_source.wait()
    get_inverse.wait()

    @pl.when(any_step)
    def _():
        plain_update(first, jnp.zeros((ROWS, LANES), F32), source, winv, u, e, plain.at[0], rhs, sums)

    @pl.when(both)
    def _():
        plain_sums(2, 1, w, plain, acc, get)
        terms[first] = below_and_above(first, both_rows(acc, 0), both_rows(acc, 1), (0,))
        plain_update(last, terms[first], source, winv, u, e, plain.at[1], rhs, sums)

    @pl.when(any_step)
    def _():
        plain_sums(0, jnp.where(both, 2, 1), w, plain, acc, get)
        plain_x_terms(0, first, acc, terms, leaves)

    @pl.when(both)
    def _():
        plain_x_terms(1, last, acc, terms, leaves)

    write_messages(leaves, to_a, to_b)

    @pl.when(jnp.logical_not(any_step))
    def _():
        rearrange(winv, 0)

        @pl.when(one_sided)
        def _():
            wait_for(4, 8)
            rearrange_y(w)

        wait_for(0, 4)


def first_beside_kernel(sched, coupling, e, w_in, winv_in, terms_in, w, winv, terms, acc, sems):
    del w_in, winv_in, terms_in
    last, one_sided = last_color(sched, 0), sched[7] == 1

    def get(m):
        return pltpu.make_async_copy(coupling.at[m], w.at[m], sems.at[m - 4])

    @pl.when(jnp.logical_not(one_sided))
    def _():
        for m in range(4, 8):
            get(m).start()

    @pl.when(last >= 0)
    def _():
        rearrange(winv, 0)

    rearrange_x(w)

    def face(f, _):
        @pl.when(jnp.logical_not(one_sided))
        def _():
            get(2 * f).wait()
            get(2 * f + 1).wait()

        rearrange(w, f)
        return 0

    @pl.when(jnp.logical_not(one_sided) | (last >= 0))
    def _():
        lax.fori_loop(DOWN, UP + 1, face, 0)

    @pl.when(last >= 0)
    def _():
        local_terms(last, w, e, terms, acc)


def phase_kernel(
    phase, n, k, sched, from_b, from_a, source, w, winv, u_in, e_in, terms_in, leaves_in, outer_in,
    u, e, terms, leaves, outer, to_a, to_b, known, todo, rhs, sums, acc,
):
    del u_in, e_in, terms_in, leaves_in, outer_in
    write_outer(n, k, from_b, from_a, outer)
    count, colors = jnp.int32(0), jnp.int32(0)
    for t in range(4):
        q, at = slot(sched, t)
        todo[count] = q
        active = at == phase
        count += jnp.where(active, 1, 0)
        colors |= jnp.where(active, 1 + q, 0)

    @pl.when(count > 0)
    def _():
        known[...] = source[...] - outer[...]

        def step(i, _):
            q = todo[i]
            update(q, terms[0] + terms[1], known, winv, u, e, rhs, sums)

            @pl.when(i < count - 1)
            def _():
                local_terms(q, w, e, terms, acc)

            return 0

        lax.fori_loop(0, count, step, 0)

        @pl.when(colors < 3)
        def _():
            leave_terms(todo[0], w, e, leaves, acc)

        @pl.when(colors == 3)
        def _():
            all_leave_terms(w, e, leaves, acc)

    write_messages(leaves, to_a, to_b)


def beside_kernel(phase, sched, w, e, terms_in, terms, acc):
    del terms_in
    last = last_color(sched, phase)

    @pl.when(last >= 0)
    def _():
        local_terms(last, w, e, terms, acc)


def last_beside_kernel(phase, sched, w, e, u, terms_in, terms, adjoint, local, longer, acc):
    beside_kernel(phase, sched, w, e, terms_in, terms, acc)
    local[...] = terms[0] + terms[1]
    longer[0] = sched[6]
    even = ((lane((2, LANES)) >> 3) & 1) == 0
    for i in range(HALF):
        u0, u1 = u[0, i, 0:2, :], u[1, i, 0:2, :]
        adjoint[2 * i : 2 * i + 2, :] = jnp.where(even, u0, shift(u1, -TILE))
        adjoint[ROWS // 2 + 2 * i : ROWS // 2 + 2 * i + 2, :] = jnp.where(even, shift(u0, -TILE), u1)


def final_kernel(n, k, from_b, from_a, local, outer_in, off, outer):
    outer[...] = outer_in[...]
    write_outer(n, k, from_b, from_a, outer)
    off[...] = local[...] + outer[...]


def cost(products):
    return pl.CostEstimate(flops=products, bytes_accessed=products // 2, transcendentals=0)


def spec(space):
    return pl.BlockSpec(memory_space=space)


def specs(text):
    return [spec({"v": VMEM, "s": SMEM, "h": pl.ANY}[c]) for c in text]


def pinned(x, space=VMEM):
    return pltpu.with_memory_space_constraint(x, space)


def params(mib):
    return pltpu.CompilerParams(vmem_limit_bytes=mib * 2**20)


def body(n, groups, coupling, inverse, source, order):
    coupling = pinned(coupling.reshape(8, HALF * ROWS, LANES), pltpu.HBM)
    inverse = pinned(inverse.reshape(2, HALF * ROWS, LANES), pltpu.HBM)
    source = pinned(source.reshape(ROWS, LANES), pltpu.HBM)
    w_shape, winv_shape = VMEM(coupling.shape, BF16), VMEM(inverse.shape, BF16)
    message, field, two = VMEM((MROWS, LANES), F32), VMEM((ROWS, LANES), F32), VMEM((2, ROWS, LANES), F32)
    u_shape, e_shape = VMEM((2, HALF, 8, LANES), F32), VMEM((2, PAIRS, 3, 16, LANES), BF16)
    rhs, sums, acc = VMEM((PAIR, LANES), BF16), VMEM((BLK, 8, LANES), F32), VMEM((4, PAIR, LANES), F32)
    flags, flag = SMEM((8,), jnp.int32), SMEM((1,), jnp.int32)

    w, winv, source, sched, side, u, e, terms, leaves, outer, to_a, to_b = pl.pallas_call(
        first_kernel,
        out_shape=(
            w_shape, winv_shape, field, flags, flag, u_shape, e_shape, two, field, field, message, message,
        ),
        in_specs=specs("hhhh"),
        out_specs=specs("vvvssvvvvvvv"),
        scratch_shapes=[
            SMEM((4,), jnp.int32), VMEM((2, *e_shape.shape), BF16), rhs, sums, acc, pltpu.SemaphoreType.DMA((11,)),
        ],
        compiler_params=params(8),
        cost_estimate=cost(40_000_000),
        name="first",
    )(pinned(order, pltpu.HBM), coupling, inverse, source)

    source, sched = pinned(source), pinned(sched, SMEM)

    axes = ("groups", "gx")

    def in_groups(to):
        return [(g * n + i, g * n + j) for g in range(groups) for i, j in to.items()]

    swap = in_groups({i: i ^ 1 for i in range(n)})
    inside = {i: i + 1 if i & 1 else i - 1 for i in range(1, n - 1)}
    far_swap = in_groups(inside)
    far_swap += [(g * n + i, (g ^ 1) * n + i) for g in range(groups) for i in (0, n - 1) if (g ^ 1) < groups]

    def side_pairs(k):
        to = inside | ({0: 1, 1: 2, 2: 0} if k else {0: 2, 2: 1, 1: 0})
        to |= {n - 3: n - 2, n - 2: n - 1, n - 1: n - 3} if k else {n - 2: n - 3, n - 3: n - 1, n - 1: n - 2}
        return in_groups(to)

    def exchange(k, to_a, to_b):
        from_b = lax.ppermute(to_b, axes, far_swap if k is None else side_pairs(k))
        return from_b, lax.ppermute(to_a, axes, swap)

    def run_phase(phase, k, received, u, e, terms, leaves, outer):
        inputs = [*received, source, w, winv, u, e, terms, leaves, outer]
        return pl.pallas_call(
            functools.partial(phase_kernel, phase, n, k),
            out_shape=(u_shape, e_shape, two, field, field, message, message),
            in_specs=specs("s" + "v" * len(inputs)),
            out_specs=specs("vvvvvvv"),
            scratch_shapes=[field, flags, rhs, sums, acc],
            input_output_aliases={6 + i: i for i in range(5)},
            compiler_params=params(4),
            cost_estimate=cost(20_000_000),
            name="phase",
        )(sched, *[pinned(x) for x in inputs])

    def beside(phase, e, terms):
        return pl.pallas_call(
            functools.partial(beside_kernel, phase),
            out_shape=two,
            in_specs=specs("svvv"),
            out_specs=spec(VMEM),
            scratch_shapes=[acc],
            input_output_aliases={3: 0},
            compiler_params=params(4),
            cost_estimate=cost(4_000_000),
            name="beside",
        )(sched, w, pinned(e), pinned(terms))

    def last_beside(phase, u, e, terms):
        return pl.pallas_call(
            functools.partial(last_beside_kernel, phase),
            out_shape=(two, jax.ShapeDtypeStruct((ROWS, LANES), F32), field, flag),
            in_specs=specs("svvvv"),
            out_specs=specs("vvvs"),
            scratch_shapes=[acc],
            input_output_aliases={4: 0},
            compiler_params=params(4),
            cost_estimate=cost(4_000_000),
            name="last_beside",
        )(sched, w, pinned(e), pinned(u), pinned(terms))

    def final(k, received, local, outer):
        return pl.pallas_call(
            functools.partial(final_kernel, n, k),
            out_shape=jax.ShapeDtypeStruct((ROWS, LANES), F32),
            in_specs=specs("vvvv"),
            out_specs=spec(VMEM),
            scratch_shapes=[field],
            compiler_params=params(4),
            cost_estimate=cost(100_000),
            name="final",
        )(*[pinned(x) for x in (*received, local, outer)])

    received = exchange(None, to_a, to_b)
    w, winv, terms = pl.pallas_call(
        first_beside_kernel,
        out_shape=(w_shape, winv_shape, two),
        in_specs=specs("shvvvv"),
        out_specs=specs("vvv"),
        scratch_shapes=[acc, pltpu.SemaphoreType.DMA((4,))],
        input_output_aliases={3: 0, 4: 1, 5: 2},
        compiler_params=params(4),
        cost_estimate=cost(8_000_000),
        name="first_beside",
    )(sched, coupling, pinned(e), pinned(w), pinned(winv), pinned(terms))
    w, winv = pinned(w), pinned(winv)

    def two_phases(phase, turns, received, u, e, terms, leaves, outer):
        for i in (0, 1):
            u, e, terms, leaves, outer, to_a, to_b = run_phase(
                phase + i, turns[i], received, u, e, terms, leaves, outer
            )
            received = exchange(turns[i + 1], to_a, to_b)
            if i == 0:
                terms = beside(phase, e, terms)
        terms, adjoint, local, longer = last_beside(phase + 1, u, e, terms)
        return longer, adjoint, received, local, (u, e, terms, leaves, outer)

    longer, adjoint, received, local, state = two_phases(1, (None,) * 3, received, u, e, terms, leaves, outer)

    def more(side, adjoint, received, local, *state):
        def from_side(k):
            def run(received, *state):
                _, adjoint, received, local, state = two_phases(3, (None, 1 - k, k), received, *state)
                return adjoint, final(k, received, local, state[-1])

            return run

        return lax.cond(side[0] > 0, from_side(1), from_side(0), received, *state)

    def no_more(side, adjoint, received, local, *state):
        return adjoint, final(None, received, local, state[-1])

    adjoint, off = lax.cond(longer[0] > 0, more, no_more, side, adjoint, received, local, *state)
    return adjoint.reshape(BLK, 2, LANES), off.reshape(BLK, 2, LANES)


def solution(mesh):
    call = functools.partial(body, mesh.shape["gx"], mesh.shape["groups"])
    return jax.shard_map(
        call,
        mesh=mesh,
        in_specs=(
            P("groups", None, None, "gx", None),
            P("groups", None, "gx", None),
            P("groups", "gx", None),
            P("groups"),
        ),
        out_specs=(P("groups", "gx", None), P("groups", "gx", None)),
        check_vma=False,
    )
```

```python
import functools

import jax
import jax.numpy as jnp
from jax import lax
from jax.experimental import pallas as pl
from jax.experimental.pallas import tpu as pltpu
from jax.sharding import PartitionSpec as P

BLK = 60
HALF = BLK // 2
ROWS = 2 * BLK
PAIR = 2 * ROWS
PAIRS = HALF // 2
TILE = 8
LANES = 128
MROWS = 64
CHUNK = 720
F32, BF16 = jnp.float32, jnp.bfloat16
VMEM, SMEM = pltpu.VMEM, pltpu.SMEM
LEAVES, STAYS, DOWN, UP = range(4)


def lane(shape):
    return lax.broadcasted_iota(jnp.int32, shape, len(shape) - 1)


def even_row(shape):
    return (lax.broadcasted_iota(jnp.int32, shape, len(shape) - 2) & 1) == 0


def own_lanes(q):
    return ((lane((ROWS, LANES)) >> 3) & 1) == q


def shift(x, by):
    return pltpu.roll(x, by % LANES, len(x.shape) - 1)


def swapped_rows(x):
    x = x.reshape(ROWS // 8, 8, LANES)
    return jnp.where(even_row(x.shape), pltpu.roll(x, 7, 1), pltpu.roll(x, 1, 1)).reshape(ROWS, LANES)


def by_color(first, second):
    even = (lax.broadcasted_iota(jnp.int16, first.shape, 1) & TILE) == 0
    moved = shift(jnp.where(even, second, first), TILE)
    return jnp.where(even, first, moved), jnp.where(even, moved, second)


def rearrange(ref, m):
    for start in range(0, HALF * ROWS, CHUNK):
        rows = pl.ds(start, CHUNK)
        ref[2 * m, rows, :], ref[2 * m + 1, rows, :] = by_color(ref[2 * m, rows, :], ref[2 * m + 1, rows, :])


def rearrange_x(w):
    for start in range(0, HALF * ROWS, CHUNK):
        rows = pl.ds(start, CHUNK)
        even = (lax.broadcasted_iota(jnp.int16, (CHUNK, LANES), 0) & 1) == 0
        left, right = [w[h, rows, :] for h in (0, 1)], [w[2 + h, rows, :] for h in (0, 1)]
        leaves = [jnp.where(even, left[h], right[h]) for h in (0, 1)]
        stays = [jnp.where(even, right[h], left[h]) for h in (0, 1)]
        w[2 * LEAVES, rows, :], w[2 * LEAVES + 1, rows, :] = by_color(*leaves)
        w[2 * STAYS, rows, :], w[2 * STAYS + 1, rows, :] = by_color(*stays)


def rearrange_y(w):
    def face(f, _):
        rearrange(w, f)
        return 0

    lax.fori_loop(DOWN, UP + 1, face, 0)


def half_sum(w, m, tiles, acc, at, add=False):
    for first, end, tile in ((0, 4, 0), (4, 7, 0), (7, 8, 1), (8, 12, 2), (12, 15, 2)):
        total = None
        for k in range(PAIRS):
            block = w[m, pl.ds(k * PAIR + 16 * first, 16 * (end - first)), :].reshape(end - first, 16, LANES)
            prod = block.astype(F32) * tiles[k, tile][None].astype(F32)
            total = prod if total is None else total + prod
        rows = pl.ds(16 * first, 16 * (end - first))
        total = total.reshape(16 * (end - first), LANES)
        acc[at, rows, :] = acc[at, rows, :] + total if add else total


def both_rows(acc, at):
    return acc[at, 0:ROWS, :] + acc[at, ROWS:, :]


def spread(half):
    return half + shift(half, -TILE)


def below_and_above(q, down, up, moves):
    at = lane((ROWS, LANES))
    down_to = (((at + 1) >> 3) & 1 == q) & (at < LANES - 1)
    up_to = (((at - 1) >> 3) & 1 == q) & (at > 0)
    down, up = sum(shift(down, -1 - by) for by in moves), sum(shift(up, 1 - by) for by in moves)
    return jnp.where(down_to, down, 0.0) + jnp.where(up_to, up, 0.0)


def local_terms(q, w, e, terms, acc):
    for kind in (DOWN, UP, STAYS):
        half_sum(w, 2 * kind + q, e.at[q], acc, kind)
    y = below_and_above(q, both_rows(acc, DOWN), both_rows(acc, UP), (0, TILE))
    stays = jnp.where(own_lanes(q), spread(both_rows(acc, STAYS)), 0.0)
    terms[q] = y + swapped_rows(stays)


def leave_terms(q, w, e, leaves, acc):
    half_sum(w, 2 * LEAVES + q, e.at[q], acc, LEAVES)
    leaves[...] = jnp.where(own_lanes(q), spread(both_rows(acc, LEAVES)), leaves[...])


def all_leave_terms(w, e, leaves, acc):
    for q in (0, 1):
        half_sum(w, 2 * LEAVES + q, e.at[q], acc, q)
    leaves[...] = jnp.where(own_lanes(0), spread(both_rows(acc, 0)), spread(both_rows(acc, 1)))


def plain_sums(faces, colors, w, plain, acc, get):
    acc[...] = jnp.zeros(acc.shape, F32)

    def half(t, _):
        get(2 * faces + t).wait()
        half_sum(w, 2 * faces + t, plain.at[0, t & 1], acc, t >> 1, add=True)

        @pl.when(colors == 2)
        def _():
            half_sum(w, 2 * faces + t, plain.at[1, t & 1], acc, 2 + (t >> 1), add=True)

        return 0

    lax.fori_loop(0, 4, half, 0)


def plain_x_terms(c, q, acc, terms, leaves):
    left, right = both_rows(acc, 2 * c), both_rows(acc, 2 * c + 1)
    own, even = own_lanes(q), even_row((ROWS, LANES))
    leaves[...] = jnp.where(own, jnp.where(even, left, right), leaves[...])
    terms[q] = terms[q] + swapped_rows(jnp.where(own, jnp.where(even, right, left), 0.0))


def row_sums(winv, m, rhs, sums, at):
    for k in range(PAIRS):
        prod = winv[m, pl.ds(k * PAIR, PAIR), :].astype(F32) * rhs[...].astype(F32)
        sums[at + 2 * k] = jnp.sum(prod[:ROWS].reshape(ROWS // 8, 8, LANES), axis=0)
        sums[at + 2 * k + 1] = jnp.sum(prod[ROWS:].reshape(ROWS // 8, 8, LANES), axis=0)


def totals(sums):
    total = sums + pltpu.roll(sums, 4, 1)
    return total + pltpu.roll(total, 2, 1)


def write_tiles(total, e):
    for k in range(PAIRS):
        first, second = total[2 * k], total[2 * k + 1]
        e[k, 0] = jnp.concatenate([first, first], axis=0).astype(BF16)
        e[k, 1] = jnp.concatenate([first, second], axis=0).astype(BF16)
        e[k, 2] = jnp.concatenate([second, second], axis=0).astype(BF16)


def write_rhs(value, rhs):
    rhs[...] = jnp.concatenate([value, value], axis=0).astype(BF16)


def update(q, incoming, source, winv, u, e, rhs, sums):
    value = (source[...] - incoming).astype(BF16).astype(F32)
    write_rhs(jnp.where(own_lanes(q), value, shift(value, TILE)), rhs)
    row_sums(winv, q, rhs, sums, 0)
    total = totals(sums[0:HALF])
    write_tiles(total, e.at[q])
    u[q] = total


def plain_update(q, incoming, source, winv, u, e, plain, rhs, sums):
    write_rhs(source[...] - incoming, rhs)

    def half(h, _):
        row_sums(winv, h, rhs, sums, HALF * h)
        return 0

    lax.fori_loop(0, 2, half, 0)
    both = [totals(sums[0:HALF]), totals(sums[HALF:])]
    for h in (0, 1):
        write_tiles(both[h], plain.at[h])
    zero = q == 0
    own = ((lane((HALF, 8, LANES)) >> 3) & 1) == q
    mine, other = jnp.where(zero, both[0], both[1]), jnp.where(zero, both[1], both[0])
    total = jnp.where(own, mine, shift(other, TILE))
    write_tiles(total, e.at[q])
    u[q] = total


def write_messages(leaves, to_a, to_b):
    odd = (lax.axis_index("gx") & 1) == 1
    to_left = leaves[pl.ds(0, BLK, stride=2), :]
    to_right = leaves[pl.ds(1, BLK, stride=2), :]
    to_a[0:BLK, :] = jnp.where(odd, to_left, to_right)
    to_b[0:BLK, :] = jnp.where(odd, to_right, to_left)
    to_a[BLK:, :] = jnp.zeros((MROWS - BLK, LANES), F32)
    to_b[BLK:, :] = jnp.zeros((MROWS - BLK, LANES), F32)


def write_outer(n, k, from_b, from_a, outer):
    me = lax.axis_index("gx")
    odd = (me & 1) == 1
    new = (me > 0) & (me < n - 1)
    if k is not None:
        new = new & ((me & 1) == 1 - k)
    a, b = from_a[0:BLK, :], from_b[0:BLK, :]
    left, right = outer[pl.ds(0, BLK, stride=2), :], outer[pl.ds(1, BLK, stride=2), :]
    outer[pl.ds(0, BLK, stride=2), :] = jnp.where(odd, a, jnp.where(new, b, left))
    outer[pl.ds(1, BLK, stride=2), :] = jnp.where(odd, jnp.where(new, b, right), a)


def write_schedule(order, sched, lead):
    parity = lax.axis_index("gx") & 1
    place = []
    for side in (parity, 1 - parity):
        for q in (0, 1):
            c = 2 * side + q
            at = jnp.int32(0)
            for i in range(1, 4):
                at = jnp.where(order[i] == c, i, at)
            place.append(at)
    mine, theirs = place[:2], place[2:]
    first = jnp.where(mine[0] < mine[1], 0, 1)
    longer = ((order[0] ^ 2) == order[1]) & ((order[0] ^ 3) == order[2])
    s1, s2 = [], []
    for q in (0, 1):
        leads = mine[q] < theirs[q]
        long1 = jnp.where(mine[q] == 0, 0, jnp.where(mine[q] == 3, 2, 1))
        long2 = jnp.where(mine[q] == 0, 4, jnp.where(mine[q] == 3, 2, 3))
        s1.append(jnp.where(longer, long1, jnp.where(leads, 0, 1)))
        s2.append(jnp.where(longer, long2, jnp.where(leads, 2, 1)))
    zero = first == 0
    sched[0] = first
    sched[1] = 1 - first
    sched[2] = jnp.where(zero, s1[0], s1[1])
    sched[3] = jnp.where(zero, s1[1], s1[0])
    sched[4] = jnp.where(zero, s2[1], s2[0])
    sched[5] = jnp.where(zero, s2[0], s2[1])
    sched[6] = jnp.where(longer, 1, 0)
    sched[7] = jnp.where(longer | ((order[0] ^ 3) == order[1]), 0, 1)
    lead[0] = order[0] >> 1


def slot(sched, t):
    q = sched[0] if t in (0, 3) else sched[1]
    return q, sched[2 + t]


def last_color(sched, phase):
    last = jnp.int32(-1)
    for t in range(4):
        q, at = slot(sched, t)
        last = jnp.where(at == phase, q, last)
    return last


def first_kernel(
    order_hbm, coupling, inverse, source_hbm,
    w, winv, source, sched, side, u, e, terms, leaves, outer, to_a, to_b,
    order, plain, rhs, sums, acc, sems,
):
    get_order = pltpu.make_async_copy(order_hbm, order, sems.at[0])
    get_source = pltpu.make_async_copy(source_hbm, source, sems.at[1])
    get_inverse = pltpu.make_async_copy(inverse, winv, sems.at[2])

    def get(m):
        return pltpu.make_async_copy(coupling.at[m], w.at[m], sems.at[3 + m])

    def wait_for(first, end):
        def wait(m, _):
            get(m).wait()
            return 0

        lax.fori_loop(first, end, wait, 0)

    for copy in (get_order, get_inverse, get_source):
        copy.start()
    for ref in (terms, leaves, u, outer):
        ref[...] = jnp.zeros(ref.shape, F32)
    e[...] = jnp.zeros(e.shape, BF16)
    get_order.wait()
    write_schedule(order, sched, side)
    first, last = sched[0], last_color(sched, 0)
    any_step, one_sided = last >= 0, sched[7] == 1
    both = any_step & (last != first)

    def start(m, _):
        get(jnp.where(one_sided, m ^ 4, m)).start()
        return 0

    lax.fori_loop(0, jnp.where(one_sided, 8, 4), start, 0)
    get_source.wait()
    get_inverse.wait()

    @pl.when(any_step)
    def _():
        plain_update(first, jnp.zeros((ROWS, LANES), F32), source, winv, u, e, plain.at[0], rhs, sums)

    @pl.when(both)
    def _():
        plain_sums(2, 1, w, plain, acc, get)
        terms[first] = below_and_above(first, both_rows(acc, 0), both_rows(acc, 1), (0,))
        plain_update(last, terms[first], source, winv, u, e, plain.at[1], rhs, sums)

    @pl.when(any_step)
    def _():
        plain_sums(0, jnp.where(both, 2, 1), w, plain, acc, get)
        plain_x_terms(0, first, acc, terms, leaves)

    @pl.when(both)
    def _():
        plain_x_terms(1, last, acc, terms, leaves)

    write_messages(leaves, to_a, to_b)

    @pl.when(jnp.logical_not(any_step))
    def _():
        rearrange(winv, 0)

        @pl.when(one_sided)
        def _():
            wait_for(4, 8)
            rearrange_y(w)

        wait_for(0, 4)


def first_beside_kernel(sched, coupling, e, w_in, winv_in, terms_in, w, winv, terms, acc, sems):
    del w_in, winv_in, terms_in
    last, one_sided = last_color(sched, 0), sched[7] == 1

    def get(m):
        return pltpu.make_async_copy(coupling.at[m], w.at[m], sems.at[m - 4])

    @pl.when(jnp.logical_not(one_sided))
    def _():
        for m in range(4, 8):
            get(m).start()

    @pl.when(last >= 0)
    def _():
        rearrange(winv, 0)

    rearrange_x(w)

    def face(f, _):
        @pl.when(jnp.logical_not(one_sided))
        def _():
            get(2 * f).wait()
            get(2 * f + 1).wait()

        rearrange(w, f)
        return 0

    @pl.when(jnp.logical_not(one_sided) | (last >= 0))
    def _():
        lax.fori_loop(DOWN, UP + 1, face, 0)

    @pl.when(last >= 0)
    def _():
        local_terms(last, w, e, terms, acc)


def phase_kernel(
    phase, n, k, sched, from_b, from_a, source, w, winv, u_in, e_in, terms_in, leaves_in, outer_in,
    u, e, terms, leaves, outer, to_a, to_b, known, todo, rhs, sums, acc,
):
    del u_in, e_in, terms_in, leaves_in, outer_in
    write_outer(n, k, from_b, from_a, outer)
    count, colors = jnp.int32(0), jnp.int32(0)
    for t in range(4):
        q, at = slot(sched, t)
        todo[count] = q
        active = at == phase
        count += jnp.where(active, 1, 0)
        colors |= jnp.where(active, 1 + q, 0)

    @pl.when(count > 0)
    def _():
        known[...] = source[...] - outer[...]

        def step(i, _):
            q = todo[i]
            update(q, terms[0] + terms[1], known, winv, u, e, rhs, sums)

            @pl.when(i < count - 1)
            def _():
                local_terms(q, w, e, terms, acc)

            return 0

        lax.fori_loop(0, count, step, 0)

        @pl.when(colors < 3)
        def _():
            leave_terms(todo[0], w, e, leaves, acc)

        @pl.when(colors == 3)
        def _():
            all_leave_terms(w, e, leaves, acc)

    write_messages(leaves, to_a, to_b)


def beside_kernel(phase, sched, w, e, terms_in, terms, acc):
    del terms_in
    last = last_color(sched, phase)

    @pl.when(last >= 0)
    def _():
        local_terms(last, w, e, terms, acc)


def last_beside_kernel(phase, sched, w, e, u, terms_in, terms, adjoint, local, longer, acc):
    beside_kernel(phase, sched, w, e, terms_in, terms, acc)
    local[...] = terms[0] + terms[1]
    longer[0] = sched[6]
    even = ((lane((2, LANES)) >> 3) & 1) == 0
    for i in range(HALF):
        u0, u1 = u[0, i, 0:2, :], u[1, i, 0:2, :]
        adjoint[2 * i : 2 * i + 2, :] = jnp.where(even, u0, shift(u1, -TILE))
        adjoint[ROWS // 2 + 2 * i : ROWS // 2 + 2 * i + 2, :] = jnp.where(even, shift(u0, -TILE), u1)


def final_kernel(n, k, from_b, from_a, local, outer_in, off, outer):
    outer[...] = outer_in[...]
    write_outer(n, k, from_b, from_a, outer)
    off[...] = local[...] + outer[...]


def cost(products):
    return pl.CostEstimate(flops=products, bytes_accessed=products // 2, transcendentals=0)


def spec(space):
    return pl.BlockSpec(memory_space=space)


def specs(text):
    return [spec({"v": VMEM, "s": SMEM, "h": pl.ANY}[c]) for c in text]


def pinned(x, space=VMEM):
    return pltpu.with_memory_space_constraint(x, space)


def params(mib):
    return pltpu.CompilerParams(vmem_limit_bytes=mib * 2**20)


def body(n, groups, coupling, inverse, source, order):
    coupling = pinned(coupling.reshape(8, HALF * ROWS, LANES), pltpu.HBM)
    inverse = pinned(inverse.reshape(2, HALF * ROWS, LANES), pltpu.HBM)
    source = pinned(source.reshape(ROWS, LANES), pltpu.HBM)
    w_shape, winv_shape = VMEM(coupling.shape, BF16), VMEM(inverse.shape, BF16)
    message, field, two = VMEM((MROWS, LANES), F32), VMEM((ROWS, LANES), F32), VMEM((2, ROWS, LANES), F32)
    u_shape, e_shape = VMEM((2, HALF, 8, LANES), F32), VMEM((2, PAIRS, 3, 16, LANES), BF16)
    rhs, sums, acc = VMEM((PAIR, LANES), BF16), VMEM((BLK, 8, LANES), F32), VMEM((4, PAIR, LANES), F32)
    flags, flag = SMEM((8,), jnp.int32), SMEM((1,), jnp.int32)

    w, winv, source, sched, side, u, e, terms, leaves, outer, to_a, to_b = pl.pallas_call(
        first_kernel,
        out_shape=(
            w_shape, winv_shape, field, flags, flag, u_shape, e_shape, two, field, field, message, message,
        ),
        in_specs=specs("hhhh"),
        out_specs=specs("vvvssvvvvvvv"),
        scratch_shapes=[
            SMEM((4,), jnp.int32), VMEM((2, *e_shape.shape), BF16), rhs, sums, acc, pltpu.SemaphoreType.DMA((11,)),
        ],
        compiler_params=params(8),
        cost_estimate=cost(40_000_000),
        name="first",
    )(pinned(order, pltpu.HBM), coupling, inverse, source)

    source, sched = pinned(source), pinned(sched, SMEM)

    axes = ("groups", "gx")

    def in_groups(to):
        return [(g * n + i, g * n + j) for g in range(groups) for i, j in to.items()]

    swap = in_groups({i: i ^ 1 for i in range(n)})
    inside = {i: i + 1 if i & 1 else i - 1 for i in range(1, n - 1)}
    far_swap = in_groups(inside)
    far_swap += [(g * n + i, (g ^ 1) * n + i) for g in range(groups) for i in (0, n - 1) if (g ^ 1) < groups]

    def side_pairs(k):
        to = inside | ({0: 1, 1: 2, 2: 0} if k else {0: 2, 2: 1, 1: 0})
        to |= {n - 3: n - 2, n - 2: n - 1, n - 1: n - 3} if k else {n - 2: n - 3, n - 3: n - 1, n - 1: n - 2}
        return in_groups(to)

    def exchange(k, to_a, to_b):
        from_b = lax.ppermute(to_b, axes, far_swap if k is None else side_pairs(k))
        return from_b, lax.ppermute(to_a, axes, swap)

    def run_phase(phase, k, received, u, e, terms, leaves, outer):
        inputs = [*received, source, w, winv, u, e, terms, leaves, outer]
        return pl.pallas_call(
            functools.partial(phase_kernel, phase, n, k),
            out_shape=(u_shape, e_shape, two, field, field, message, message),
            in_specs=specs("s" + "v" * len(inputs)),
            out_specs=specs("vvvvvvv"),
            scratch_shapes=[field, flags, rhs, sums, acc],
            input_output_aliases={6 + i: i for i in range(5)},
            compiler_params=params(4),
            cost_estimate=cost(20_000_000),
            name="phase",
        )(sched, *[pinned(x) for x in inputs])

    def beside(phase, e, terms):
        return pl.pallas_call(
            functools.partial(beside_kernel, phase),
            out_shape=two,
            in_specs=specs("svvv"),
            out_specs=spec(VMEM),
            scratch_shapes=[acc],
            input_output_aliases={3: 0},
            compiler_params=params(4),
            cost_estimate=cost(4_000_000),
            name="beside",
        )(sched, w, pinned(e), pinned(terms))

    def last_beside(phase, u, e, terms):
        return pl.pallas_call(
            functools.partial(last_beside_kernel, phase),
            out_shape=(two, jax.ShapeDtypeStruct((ROWS, LANES), F32), field, flag),
            in_specs=specs("svvvv"),
            out_specs=specs("vvvs"),
            scratch_shapes=[acc],
            input_output_aliases={4: 0},
            compiler_params=params(4),
            cost_estimate=cost(4_000_000),
            name="last_beside",
        )(sched, w, pinned(e), pinned(u), pinned(terms))

    def final(k, received, local, outer):
        return pl.pallas_call(
            functools.partial(final_kernel, n, k),
            out_shape=jax.ShapeDtypeStruct((ROWS, LANES), F32),
            in_specs=specs("vvvv"),
            out_specs=spec(VMEM),
            scratch_shapes=[field],
            compiler_params=params(4),
            cost_estimate=cost(100_000),
            name="final",
        )(*[pinned(x) for x in (*received, local, outer)])

    received = exchange(None, to_a, to_b)
    w, winv, terms = pl.pallas_call(
        first_beside_kernel,
        out_shape=(w_shape, winv_shape, two),
        in_specs=specs("shvvvv"),
        out_specs=specs("vvv"),
        scratch_shapes=[acc, pltpu.SemaphoreType.DMA((4,))],
        input_output_aliases={3: 0, 4: 1, 5: 2},
        compiler_params=params(4),
        cost_estimate=cost(8_000_000),
        name="first_beside",
    )(sched, coupling, pinned(e), pinned(w), pinned(winv), pinned(terms))
    w, winv = pinned(w), pinned(winv)

    def two_phases(phase, turns, received, u, e, terms, leaves, outer):
        for i in (0, 1):
            u, e, terms, leaves, outer, to_a, to_b = run_phase(
                phase + i, turns[i], received, u, e, terms, leaves, outer
            )
            received = exchange(turns[i + 1], to_a, to_b)
            if i == 0:
                terms = beside(phase, e, terms)
        terms, adjoint, local, longer = last_beside(phase + 1, u, e, terms)
        return longer, adjoint, received, local, (u, e, terms, leaves, outer)

    longer, adjoint, received, local, state = two_phases(1, (None,) * 3, received, u, e, terms, leaves, outer)

    def more(side, adjoint, received, local, *state):
        def from_side(k):
            def run(received, *state):
                _, adjoint, received, local, state = two_phases(3, (None, 1 - k, k), received, *state)
                return adjoint, final(k, received, local, state[-1])

            return run

        return lax.cond(side[0] > 0, from_side(1), from_side(0), received, *state)

    def no_more(side, adjoint, received, local, *state):
        return adjoint, final(None, received, local, state[-1])

    adjoint, off = lax.cond(longer[0] > 0, more, no_more, side, adjoint, received, local, *state)
    return adjoint.reshape(BLK, 2, LANES), off.reshape(BLK, 2, LANES)


def solution(mesh):
    call = functools.partial(body, mesh.shape["gx"], mesh.shape["groups"])
    return jax.shard_map(
        call,
        mesh=mesh,
        in_specs=(
            P("groups", None, None, "gx", None),
            P("groups", None, "gx", None),
            P("groups", "gx", None),
            P("groups"),
        ),
        out_specs=(P("groups", "gx", None), P("groups", "gx", None)),
        check_vma=False,
    )
```
